32 devices in a mesh: groups: 2 (over y), seq: 4 (over z), chan: 2 (over x), sub: 2 (over core).
Axes of the slice: x: 2, y: 2, z: 4, core: 2. Of those that a mesh axis runs over, the one named last changes fastest.
Arguments:
- x_in: bfloat16 [1024, 8192], P(('groups', 'seq'), ('chan', 'sub')), parts along dimension 0, may hold values from -36 to 36
- b_in: bfloat16 [1024, 4, 256], P(('groups', 'seq'), 'chan'), parts along dimension 0, may hold values from -6 to 6
- c_in: bfloat16 [1024, 4, 256], P(('groups', 'seq'), 'chan'), parts along dimension 0, may hold values from -0.375 to 0.375
- step_size: float32 [1024, 128], P(('groups', 'seq'), ('chan', 'sub')), parts along dimension 0, may hold values from 0.02 to 0.2
- log_decay: float32 [1024, 128], P(('groups', 'seq'), ('chan', 'sub')), parts along dimension 0, may hold values from -1 to 0, as said below
- skip: float32 [128], P(('chan', 'sub')), may hold values from 0.5 to 1.5
- gate_in: bfloat16 [1024, 8192], P(('groups', 'seq'), ('chan', 'sub')), parts along dimension 0, may hold values from -6 to 6
- norm_gain: float32 [8192], P(('chan', 'sub')), may hold values from 0.1 to 1.9
- walsh_sign: int32 [8192], P(('chan', 'sub')), may hold values from 0 to 1
- channel_shift_power: int32 [8192], P(('chan', 'sub')), may hold values from -1 to 3
- out_weight: bfloat16 [8192, 4096], P(('chan', 'sub'), 'seq'), may hold values from -0.0625 to 0.0625
Outputs:
- projected: bfloat16 [1024, 4096], P(('groups', 'seq', 'chan', 'sub')), parts along dimension 0
The draws below stay inside these ranges and needn't reach their ends.
There are 2 independent parts, one for each index of `groups`. The reference program is written for one: setup_inputs(seed, part) draws one part's arguments, and reference() takes and returns one part's arrays. A program takes and returns all parts, laid end to end along the dimension named above; an argument that names none is the same for every part. Nothing has to cross between parts.
Inputs may be any that keep to these rules, and one draw needn't show every extreme that they name: `log_decay`: every entry is negative.
All inputs are finite; a program needn't handle non-finite values.
Results may differ from the reference program's by a relative error of at most 0.024.
Values may be sent and summed in bfloat16 or wider, within the bound.
No kernel may reach another device: no remote copies, remote signals or barrier semaphores. Data moves between devices by JAX's collectives and lax.ppermute only.
A program may use at most 128 MiB of HBM per device.

```python
import math
import jax
import jax.numpy as jnp
from jax import lax

LOCAL_HEADS = 128
P_SIZE = 64
N = 256
G = 4
NORM_HEADS = 16
OUT = 4096
TOK_DEV = 128
CONTEXT_TOKENS = 512
N_CHAN = 2
N_SUB = 2


def draw_x_in(key, part):
    key_head, key_body = jax.random.split(key, 2)
    head_ids = jnp.arange(LOCAL_HEADS)
    rising = 3.0 ** ((head_ids % (LOCAL_HEADS // G)).astype(jnp.float32) / max(LOCAL_HEADS // G - 1, 1))
    spread = jnp.exp(jax.random.uniform(key_head, (LOCAL_HEADS,), jnp.float32, 0.0, math.log(3.0)))
    head_scale = jnp.repeat(rising * spread, P_SIZE)
    values = jnp.clip(jax.random.normal(key_body, (CONTEXT_TOKENS, LOCAL_HEADS * P_SIZE), jnp.float32), -4.0, 4.0)
    return (values * head_scale[None, :]).astype(jnp.bfloat16)


def draw_log_decay(key, part):
    random_subkey_list = jax.random.split(key, 7)
    slow_share = 0.5
    is_slow = jax.random.bernoulli(random_subkey_list[0], slow_share, (LOCAL_HEADS,))
    slow_rate = jnp.exp(jax.random.uniform(random_subkey_list[1], (LOCAL_HEADS,), jnp.float32, math.log(0.1), math.log(0.5))) / CONTEXT_TOKENS
    fast_rate = jnp.exp(jax.random.uniform(random_subkey_list[2], (LOCAL_HEADS,), jnp.float32, math.log(1.0 / 50.0), math.log(1.0 / 30.0)))
    head_decay_speed = jnp.where(is_slow, slow_rate, fast_rate)
    block_multiplier = jnp.repeat(jnp.exp(jax.random.uniform(random_subkey_list[3], (CONTEXT_TOKENS // TOK_DEV,), jnp.float32, math.log(0.5), math.log(2.0))), TOK_DEV)
    element_multiplier = jnp.exp(jax.random.uniform(random_subkey_list[4], (CONTEXT_TOKENS, LOCAL_HEADS), jnp.float32, math.log(0.5), math.log(2.0)))
    outlier_token_index = jax.random.randint(random_subkey_list[5], (2,), 0, CONTEXT_TOKENS)
    outlier_cost_factor = jax.random.uniform(random_subkey_list[6], (2, LOCAL_HEADS), jnp.float32, 0.2, 0.4)
    outlier_found = (jnp.arange(CONTEXT_TOKENS)[:, None] == outlier_token_index[None, :]).astype(jnp.float32)
    outlier_feature = jnp.sum(outlier_found[:, :, None] * jnp.log(1.0 - outlier_cost_factor)[None, :, :], axis=1)
    return (-head_decay_speed[None, :] * block_multiplier[:, None] * element_multiplier + outlier_feature).astype(jnp.float32)


def with_ends(values, stream_key, least, high):
    dims = values.shape
    place = [jax.random.randint(jax.random.fold_in(stream_key, axis), (), 0, dims[axis]) for axis in range(len(dims))]
    values = values.at[tuple(place)].set(least)
    longest = dims.index(max(dims))
    place[longest] = (place[longest] + 1) % dims[longest]
    return values.at[tuple(place)].set(high)


def level_of(stream_key, shape, shards, smallest, top_value):
    level, own = 1.0, jax.random.fold_in(stream_key, 6)
    for axis_at, parts in shards:
        heights = jnp.exp(jax.random.uniform(jax.random.fold_in(own, axis_at), (parts,), jnp.float32, smallest / len(shards), top_value / len(shards)))
        level = level * jnp.repeat(heights, shape[axis_at] // parts).reshape([-1 if axis == axis_at else 1 for axis in range(len(shape))])
    return level


def noise(own_key, extent, deviation, limit, cuts=(), kind=jnp.bfloat16):
    values = deviation * jax.random.normal(own_key, extent, jnp.float32)
    if cuts:
        values = values * level_of(own_key, extent, cuts, -0.22, 0.18)
    return jnp.clip(values, -limit, limit).astype(kind)


def setup_inputs(seed: int = 0, part: int = 0) -> dict:
    splits = jax.random.split(jax.random.key(seed), 12)
    own_keys = jax.random.split(jax.random.fold_in(splits[11], part), 12)
    return {
        "x_in": draw_x_in(jax.random.fold_in(jax.random.fold_in(splits[11], part), 71), part),
        "b_in": noise(own_keys[1], (CONTEXT_TOKENS, G, N), 1.0, 6.0, ((0, 4), (1, 2))),
        "c_in": noise(own_keys[2], (CONTEXT_TOKENS, G, N), N ** -0.5, 0.375, ((0, 4), (1, 2))),
        "step_size": jnp.clip(jnp.exp(math.log(0.2) - 2.3025851 * jax.random.uniform(own_keys[3], (CONTEXT_TOKENS, LOCAL_HEADS), jnp.float32) ** level_of(own_keys[3], (CONTEXT_TOKENS, LOCAL_HEADS), ((0, 4), (1, 4)), -0.2, 0.2)), 0.02, 0.2),
        "log_decay": draw_log_decay(jax.random.fold_in(jax.random.fold_in(splits[11], part), 71), part),
        "skip": jnp.clip(0.5 + 1.0 * jax.random.uniform(splits[5], (LOCAL_HEADS,), jnp.float32) ** level_of(splits[5], (LOCAL_HEADS,), ((0, 4),), -0.2, 0.2), 0.5, 1.5),
        "gate_in": noise(own_keys[6], (CONTEXT_TOKENS, LOCAL_HEADS * P_SIZE), 1.0, 6.0, ((0, 4), (1, 4))),
        "norm_gain": jnp.clip(1.0 + 0.18 * jax.random.normal(splits[7], (LOCAL_HEADS * P_SIZE,), jnp.float32), 0.1, 1.9),
        "walsh_sign": with_ends(jax.random.randint(splits[8], (LOCAL_HEADS * P_SIZE,), 0, 2), jax.random.fold_in(splits[8], 1), 0, 1).astype(jnp.int32),
        "channel_shift_power": with_ends(jax.random.randint(splits[9], (LOCAL_HEADS * P_SIZE,), -1, 4), jax.random.fold_in(splits[9], 1), -1, 3).astype(jnp.int32),
        "out_weight": noise(splits[10], (LOCAL_HEADS * P_SIZE, OUT), (LOCAL_HEADS * P_SIZE) ** -0.5, 0.0625, ((0, 4), (1, 4))),
    }


norm_eps = 1e-05
clip_level = 4.0
expo_levels = (-1, 0, 1, 2, 3)

def power_two(expo, sign_flip):
    result = jnp.zeros(expo.shape, jnp.float32)
    for level in expo_levels:
        result = result + jnp.where(expo == level, jnp.float32(2.0 ** (sign_flip * level)), jnp.float32(0.0))
    return result

def walsh_rows(values):
    row_count, width = values.shape
    half_span = 1
    while half_span < width:
        shaped = values.reshape(row_count, width // (2 * half_span), 2, half_span)
        upper = shaped[:, :, 0, :]
        lower = shaped[:, :, 1, :]
        values = jnp.stack([upper + lower, upper - lower], axis=2).reshape(row_count, width)
        half_span = half_span * 2
    return values

def reference(x_in, b_in, c_in, step_size, log_decay, skip, gate_in, norm_gain, walsh_sign, channel_shift_power, out_weight):
    highest = lax.Precision.HIGHEST
    head_group = LOCAL_HEADS // G
    block_len = math.gcd(CONTEXT_TOKENS, 256)
    block_count = CONTEXT_TOKENS // block_len
    x_heads = x_in.astype(jnp.float32).reshape(CONTEXT_TOKENS, LOCAL_HEADS, P_SIZE)
    weighted = x_heads * step_size[:, :, None]

    def one_block(state, block_index):
        start = (block_index * block_len).astype(jnp.int32)
        x_block = lax.dynamic_slice_in_dim(weighted, start, block_len, 0).reshape(block_len, G, head_group, P_SIZE)
        b_block = lax.dynamic_slice_in_dim(b_in, start, block_len, 0).astype(jnp.float32)
        c_block = lax.dynamic_slice_in_dim(c_in, start, block_len, 0).astype(jnp.float32)
        decay_block = lax.dynamic_slice_in_dim(log_decay, start, block_len, 0)
        cumul = jnp.cumsum(decay_block, axis=0)
        inner = jnp.einsum('tgn,ugn->tug', c_block, b_block, precision=highest)
        differ = cumul[:, None, :] - cumul[None, :, :]
        causal = (jnp.arange(block_len)[:, None] >= jnp.arange(block_len)[None, :])[:, :, None]
        ratio = jnp.where(causal, jnp.exp(jnp.where(causal, differ, 0.0)), 0.0).reshape(block_len, block_len, G, head_group)
        mixing = ratio * inner[:, :, :, None]
        y_diag = jnp.einsum('tugk,ugkp->tgkp', mixing, x_block, precision=highest)
        y_off = jnp.einsum('tgn,gnkp->tgkp', c_block, state, precision=highest) * jnp.exp(cumul).reshape(block_len, G, head_group)[:, :, :, None]
        total = cumul[-1]
        to_end = jnp.exp(total[None, :] - cumul).reshape(block_len, G, head_group)[:, :, :, None]
        new_state = state * jnp.exp(total).reshape(G, 1, head_group, 1) + jnp.einsum('ugn,ugkp->gnkp', b_block, x_block * to_end, precision=highest)
        return (new_state, (y_diag + y_off).reshape(block_len, LOCAL_HEADS * P_SIZE))
    initial = jnp.zeros((G, N, head_group, P_SIZE), jnp.float32)
    final_state, y_blocks = lax.scan(one_block, initial, jnp.arange(block_count, dtype=jnp.int32))
    y_ssm = y_blocks.reshape(CONTEXT_TOKENS, LOCAL_HEADS * P_SIZE) + (x_heads * skip[None, :, None]).reshape(CONTEXT_TOKENS, LOCAL_HEADS * P_SIZE)
    gated_pre = y_ssm * jax.nn.silu(gate_in.astype(jnp.float32))
    grouped = gated_pre.reshape(CONTEXT_TOKENS, LOCAL_HEADS // NORM_HEADS, NORM_HEADS * P_SIZE)
    mean_sq = lax.optimization_barrier(jnp.mean(grouped * grouped, axis=2, keepdims=True))
    gated = (grouped * lax.rsqrt(mean_sq + norm_eps)).reshape(CONTEXT_TOKENS, LOCAL_HEADS * P_SIZE) * norm_gain[None, :]
    gated = gated.astype(jnp.bfloat16)
    sign_value = jnp.where(walsh_sign == 1, 1.0, -1.0).astype(jnp.float32)
    signed = gated.astype(jnp.float32) * sign_value[None, :]
    rotated = walsh_rows(signed) * (1.0 / math.sqrt(LOCAL_HEADS * P_SIZE))
    quant = jnp.clip(rotated * power_two(channel_shift_power, 1)[None, :], -clip_level, clip_level).astype(jnp.bfloat16)
    scaled = (lax.optimization_barrier(quant).astype(jnp.float32) * power_two(channel_shift_power, -1)[None, :]).astype(jnp.bfloat16)
    slab_count = N_CHAN * N_SUB
    slab_width = LOCAL_HEADS * P_SIZE // slab_count

    def add_slab(slab_index, accum):
        offset = (slab_index * slab_width).astype(jnp.int32)
        columns = lax.dynamic_slice_in_dim(scaled, offset, slab_width, 1)
        weight_rows = lax.dynamic_slice_in_dim(out_weight, offset, slab_width, 0)
        slab_partial = jnp.dot(columns, weight_rows, preferred_element_type=jnp.float32).astype(jnp.bfloat16)
        return accum + lax.optimization_barrier(slab_partial).astype(jnp.float32)
    summed = lax.fori_loop(jnp.int32(0), jnp.int32(slab_count), add_slab, jnp.zeros((CONTEXT_TOKENS, OUT), jnp.float32))
    return summed.astype(jnp.bfloat16)
```

```python
import functools
import math

import jax
import jax.numpy as jnp
import numpy as np
from jax import lax
from jax.experimental import pallas as pl
from jax.experimental.pallas import tpu as pltpu
from jax.sharding import PartitionSpec as P

LOCAL_HEADS = 128
P_SIZE = 64
G = 4
NORM_HEADS = 16


norm_eps = 1e-05
clip_level = 4.0
expo_levels = (-1, 0, 1, 2, 3)
LANES = 128
H_BLOCK = 256
f32 = jnp.float32
bf16 = jnp.bfloat16
PARAMS = pltpu.CompilerParams(vmem_limit_bytes=40 * 2**20)


def power_two(expo, sign_flip):
    result = jnp.zeros(expo.shape, jnp.float32)
    for level in expo_levels:
        result = result + jnp.where(
            expo == level, jnp.float32(2.0 ** (sign_flip * level)), jnp.float32(0.0)
        )
    return result


def dot(a, b):
    return jnp.dot(a, b, preferred_element_type=f32)


def dot_nt(a, b):
    return lax.dot_general(a, b, (((1,), (1,)), ((), ())), preferred_element_type=f32)


def parts_of(value, count):
    terms = []
    for _ in range(count):
        term = value.astype(bf16)
        terms.append(term)
        value = value - term.astype(f32)
    return terms


def exact_dot(exact, value, count=3):
    return sum(dot(exact, term) for term in parts_of(value, count))


def spread(value, expand, count=2):
    return sum(dot(term, expand) for term in parts_of(value, count))


def causal_mask(size):
    row = lax.broadcasted_iota(jnp.int32, (size, size), 0)
    col = lax.broadcasted_iota(jnp.int32, (size, size), 1)
    return row >= col


def message_kernel(x_ref, b_ref, step_ref, decay_ref, expand_ref, msg_ref, cumul_ref):
    tokens, width = x_ref.shape
    heads = step_ref.shape[1]
    states = b_ref.shape[1]
    expand = expand_ref[...]
    triangle = causal_mask(tokens).astype(f32).astype(bf16)
    cumul = exact_dot(triangle, decay_ref[...])
    cumul_ref[...] = cumul
    total = cumul[tokens - 1 : tokens, :]
    scale = spread(jnp.exp(total - cumul) * step_ref[...], expand)
    msg_ref[:, :width] = (x_ref[...].astype(f32) * scale).astype(bf16)
    msg_ref[:, width : width + states] = b_ref[...]
    high, low = parts_of(jnp.exp(total), 2)
    base = width + states
    msg_ref[:, base:] = jnp.zeros((tokens, msg_ref.shape[1] - base), bf16)
    msg_ref[:, base : base + heads] = jnp.broadcast_to(high, (tokens, heads))
    msg_ref[:, base + heads : base + 2 * heads] = jnp.broadcast_to(low, (tokens, heads))


def local_kernel(
    x_ref, b_ref, c_ref, step_ref, cumul_ref, gate_ref, skip_ref, expand_ref, own_ref, far_ref
):
    tokens, width = x_ref.shape
    heads = step_ref.shape[1]
    causal = causal_mask(tokens)
    inner = dot_nt(c_ref[...], b_ref[...])
    cumul = cumul_ref[...]
    cumul_t = cumul.T
    step_t = step_ref[...].T
    first = lax.broadcasted_iota(jnp.int32, (tokens, 2 * P_SIZE), 1) < P_SIZE
    for pair in range(heads // 2):
        mixings = []
        for head in (2 * pair, 2 * pair + 1):
            differ = cumul[:, head : head + 1] - cumul_t[head : head + 1, :]
            ratio = jnp.exp(jnp.where(causal, differ, -jnp.inf))
            mixings.append((ratio * (inner * step_t[head : head + 1, :])).astype(bf16))
        at = slice(pair * 2 * P_SIZE, (pair + 1) * 2 * P_SIZE)
        x_pair = x_ref[:, at]
        zero = jnp.zeros_like(x_pair)
        blocks = jnp.concatenate(
            [jnp.where(first, x_pair, zero), jnp.where(first, zero, x_pair)], axis=0
        )
        own = dot(jnp.concatenate(mixings, axis=1), blocks)
        own = own + x_pair.astype(f32) * skip_ref[:, at]
        gate = gate_ref[:, at].astype(f32)
        own_ref[:, at] = own * (gate / (1.0 + jnp.exp(-gate)))
    reach = jnp.exp(cumul)
    tile = min(width, 512)
    for start in range(0, width, tile):
        at = slice(start, start + tile)
        gate = gate_ref[:, at].astype(f32)
        far_ref[:, at] = spread(reach, expand_ref[:, at]) * (gate / (1.0 + jnp.exp(-gate)))


def mix_kernel(count, *refs):
    messages = refs[:count]
    c_ref, own_ref, far_ref, gain_ref, table_ref, expand_ref, out_ref = refs[count:]
    tokens, width = own_ref.shape
    states = c_ref.shape[1]
    heads = expand_ref.shape[0]
    base = width + states
    c_group = c_ref[...]
    inners = []
    decays = []
    for msg_ref in messages:
        inners.append(dot_nt(c_group, msg_ref[:, width:base]).astype(bf16))
        decay = dot(msg_ref[:16, base : base + heads], expand_ref[...]) + dot(
            msg_ref[:16, base + heads : base + 2 * heads], expand_ref[...]
        )
        decays.append(decay[:1, :])
    norm_width = NORM_HEADS * P_SIZE
    table = table_ref[...]
    parts = []
    for start in range(0, width, norm_width):
        pres = []
        square = jnp.zeros((tokens, 1), f32)
        for begin in range(start, start + norm_width, H_BLOCK):
            at = slice(begin, begin + H_BLOCK)
            carried = None
            for k in reversed(range(count)):
                term = dot(inners[k], messages[k][:, at])
                carried = term if carried is None else term + decays[k][:, at] * carried
            pre = own_ref[:, at]
            if carried is not None:
                pre = pre + far_ref[:, at] * carried
            square = square + jnp.sum(pre * pre, axis=1, keepdims=True)
            pres.append(pre)
        inverse = lax.rsqrt(square * (1.0 / norm_width) + norm_eps)
        for index, pre in enumerate(pres):
            at = slice(start + index * H_BLOCK, start + (index + 1) * H_BLOCK)
            signed = (pre * inverse * gain_ref[:, at]).astype(bf16)
            parts.append(dot(signed, table))
    span = 1
    while span < len(parts):
        for low in range(len(parts)):
            if low & span == 0:
                a, b = parts[low], parts[low + span]
                parts[low], parts[low + span] = a + b, a - b
        span *= 2
    for index, part in enumerate(parts):
        out_ref[:, index * H_BLOCK : (index + 1) * H_BLOCK] = part.astype(bf16)


def sylvester(order):
    table = np.ones((1, 1), np.float32)
    while table.shape[0] < order:
        table = np.block([[table, table], [table, -table]])
    return table


def shift_up(value, axis, distance):
    count = lax.axis_size(axis)
    return lax.ppermute(value, axis, [(k, k + distance) for k in range(count - distance)])


def turn(value, axis, distance):
    count = lax.axis_size(axis)
    return lax.ppermute(value, axis, [(k, (k + distance) % count) for k in range(count)])


def swap(value, axis, bit):
    count = lax.axis_size(axis)
    return lax.ppermute(value, axis, [(k, k ^ (1 << bit)) for k in range(count)])


def bits_of(axis):
    return range(lax.axis_size(axis).bit_length() - 1)


def halve(value, axis):
    here = lax.axis_index(axis)
    for bit in reversed(bits_of(axis)):
        pair = value.reshape((2, value.shape[0] // 2) + value.shape[1:])
        mine = here // 2**bit % 2
        keep = lax.dynamic_index_in_dim(pair, mine, 0, keepdims=False)
        give = lax.dynamic_index_in_dim(pair, 1 - mine, 0, keepdims=False)
        value = (keep.astype(f32) + swap(give, axis, bit).astype(f32)).astype(bf16)
    return value[0]


def body(
    x_in,
    b_in,
    c_in,
    step_size,
    log_decay,
    skip,
    gate_in,
    norm_gain,
    walsh_sign,
    channel_shift_power,
    out_weight,
):
    tokens, width = x_in.shape
    heads = step_size.shape[1]
    states = b_in.shape[2]
    seq_count = lax.axis_size("seq")
    sub_index = lax.axis_index("sub")
    group_local = sub_index * heads // (LOCAL_HEADS // G)
    b_group = lax.dynamic_slice_in_dim(b_in, group_local, 1, 1)[:, 0, :]
    c_group = lax.dynamic_slice_in_dim(c_in, group_local, 1, 1)[:, 0, :]
    expand = jnp.asarray(np.kron(np.eye(heads), np.ones((1, P_SIZE))), bf16)
    table = jnp.asarray(sylvester(H_BLOCK), bf16)

    tail = pl.cdiv(2 * heads, LANES) * LANES
    message, cumul = pl.pallas_call(
        message_kernel,
        out_shape=(
            jax.ShapeDtypeStruct((tokens, width + states + tail), bf16),
            jax.ShapeDtypeStruct((tokens, heads), f32),
        ),
        compiler_params=PARAMS,
        name="message",
    )(x_in, b_group, step_size, log_decay, expand)
    arrived = [shift_up(message, "seq", k) for k in range(1, seq_count)]

    wide_skip = jnp.repeat(skip, P_SIZE)[None, :]
    own, far = pl.pallas_call(
        local_kernel,
        out_shape=(
            jax.ShapeDtypeStruct((tokens, width), f32),
            jax.ShapeDtypeStruct((tokens, width), f32),
        ),
        compiler_params=PARAMS,
        name="local",
    )(x_in, b_group, c_group, step_size, cumul, gate_in, wide_skip, expand)

    signed_gain = (jnp.where(walsh_sign == 1, 1.0, -1.0) * norm_gain)[None, :]
    mixed = pl.pallas_call(
        functools.partial(mix_kernel, len(arrived)),
        out_shape=jax.ShapeDtypeStruct((tokens, width), bf16),
        compiler_params=PARAMS,
        name="mix",
    )(*arrived, c_group, own, far, signed_gain, table, expand)

    for axis in ("sub", "chan"):
        here = lax.axis_index(axis)
        for bit in bits_of(axis):
            other = swap(mixed.astype(bf16), axis, bit).astype(f32)
            sign = 1.0 - 2.0 * (here // 2**bit % 2).astype(f32)
            mixed = mixed.astype(f32) * sign + other
    rotated = mixed * (1.0 / math.sqrt(LOCAL_HEADS * P_SIZE))
    quant = jnp.clip(
        rotated * power_two(channel_shift_power, 1)[None, :], -clip_level, clip_level
    ).astype(bf16)
    scaled = (quant.astype(f32) * power_two(channel_shift_power, -1)[None, :]).astype(bf16)

    chan_count, sub_count = lax.axis_size("chan"), lax.axis_size("sub")
    rows = tokens // (chan_count * sub_count)
    order = sorted(range(1, seq_count), key=lambda k: -min(k, seq_count - k))
    blocks = {0: scaled}
    for k in order:
        blocks[k] = turn(scaled, "seq", k)
    sums = []
    for k in [0] + order:
        partial = dot(blocks[k], out_weight).astype(bf16)
        partial = partial.reshape(chan_count, sub_count, rows, -1)
        partial = halve(jnp.swapaxes(partial, 0, 1), "sub")
        done = halve(partial, "chan")
        sums.append((k, turn(done, "seq", -k % seq_count) if k else done))
    pieces = [value for _, value in sorted(sums, key=lambda item: item[0])]
    stacked = jnp.stack(pieces + pieces, axis=0)
    here = lax.axis_index("seq")
    placed = lax.dynamic_slice_in_dim(
        stacked, (seq_count - here) % seq_count, seq_count, 0
    )
    return jnp.swapaxes(placed, 0, 1).reshape(rows, -1)


def solution(mesh):
    return jax.shard_map(
        body,
        mesh=mesh,
        in_specs=(
            P(("groups", "seq"), ("chan", "sub")),
            P(("groups", "seq"), "chan", None),
            P(("groups", "seq"), "chan", None),
            P(("groups", "seq"), ("chan", "sub")),
            P(("groups", "seq"), ("chan", "sub")),
            P(("chan", "sub")),
            P(("groups", "seq"), ("chan", "sub")),
            P(("chan", "sub")),
            P(("chan", "sub")),
            P(("chan", "sub")),
            P(("chan", "sub"), "seq"),
        ),
        out_specs=P(("groups", "seq", "chan", "sub"), None),
        check_vma=False,
    )
```

```python
import functools
import math

import jax
import jax.numpy as jnp
import numpy as np
from jax import lax
from jax.experimental import pallas as pl
from jax.experimental.pallas import tpu as pltpu
from jax.sharding import PartitionSpec as P

LOCAL_HEADS = 128
P_SIZE = 64
G = 4
NORM_HEADS = 16


norm_eps = 1e-05
clip_level = 4.0
expo_levels = (-1, 0, 1, 2, 3)
LANES = 128
H_BLOCK = 256
f32 = jnp.float32
bf16 = jnp.bfloat16
PARAMS = pltpu.CompilerParams(vmem_limit_bytes=40 * 2**20)


def power_two(expo, sign_flip):
    result = jnp.zeros(expo.shape, jnp.float32)
    for level in expo_levels:
        result = result + jnp.where(
            expo == level, jnp.float32(2.0 ** (sign_flip * level)), jnp.float32(0.0)
        )
    return result


def dot(a, b):
    return jnp.dot(a, b, preferred_element_type=f32)


def dot_nt(a, b):
    return lax.dot_general(a, b, (((1,), (1,)), ((), ())), preferred_element_type=f32)


def parts_of(value, count):
    terms = []
    for _ in range(count):
        term = value.astype(bf16)
        terms.append(term)
        value = value - term.astype(f32)
    return terms


def exact_dot(exact, value, count=3):
    return sum(dot(exact, term) for term in parts_of(value, count))


def spread(value, expand, count=2):
    return sum(dot(term, expand) for term in parts_of(value, count))


def causal_mask(size):
    row = lax.broadcasted_iota(jnp.int32, (size, size), 0)
    col = lax.broadcasted_iota(jnp.int32, (size, size), 1)
    return row >= col


def message_kernel(x_ref, b_ref, step_ref, decay_ref, expand_ref, msg_ref, cumul_ref):
    tokens, width = x_ref.shape
    heads = step_ref.shape[1]
    states = b_ref.shape[1]
    expand = expand_ref[...]
    triangle = causal_mask(tokens).astype(f32).astype(bf16)
    cumul = exact_dot(triangle, decay_ref[...])
    cumul_ref[...] = cumul
    total = cumul[tokens - 1 : tokens, :]
    scale = spread(jnp.exp(total - cumul) * step_ref[...], expand)
    msg_ref[:, :width] = (x_ref[...].astype(f32) * scale).astype(bf16)
    msg_ref[:, width : width + states] = b_ref[...]
    high, low = parts_of(jnp.exp(total), 2)
    base = width + states
    msg_ref[:, base:] = jnp.zeros((tokens, msg_ref.shape[1] - base), bf16)
    msg_ref[:, base : base + heads] = jnp.broadcast_to(high, (tokens, heads))
    msg_ref[:, base + heads : base + 2 * heads] = jnp.broadcast_to(low, (tokens, heads))


def local_kernel(
    x_ref, b_ref, c_ref, step_ref, cumul_ref, gate_ref, skip_ref, expand_ref, own_ref, far_ref
):
    tokens, width = x_ref.shape
    heads = step_ref.shape[1]
    causal = causal_mask(tokens)
    inner = dot_nt(c_ref[...], b_ref[...])
    cumul = cumul_ref[...]
    cumul_t = cumul.T
    step_t = step_ref[...].T
    first = lax.broadcasted_iota(jnp.int32, (tokens, 2 * P_SIZE), 1) < P_SIZE
    for pair in range(heads // 2):
        mixings = []
        for head in (2 * pair, 2 * pair + 1):
            differ = cumul[:, head : head + 1] - cumul_t[head : head + 1, :]
            ratio = jnp.exp(jnp.where(causal, differ, -jnp.inf))
            mixings.append((ratio * (inner * step_t[head : head + 1, :])).astype(bf16))
        at = slice(pair * 2 * P_SIZE, (pair + 1) * 2 * P_SIZE)
        x_pair = x_ref[:, at]
        zero = jnp.zeros_like(x_pair)
        blocks = jnp.concatenate(
            [jnp.where(first, x_pair, zero), jnp.where(first, zero, x_pair)], axis=0
        )
        own = dot(jnp.concatenate(mixings, axis=1), blocks)
        own = own + x_pair.astype(f32) * skip_ref[:, at]
        gate = gate_ref[:, at].astype(f32)
        own_ref[:, at] = own * (gate / (1.0 + jnp.exp(-gate)))
    reach = jnp.exp(cumul)
    tile = min(width, 512)
    for start in range(0, width, tile):
        at = slice(start, start + tile)
        gate = gate_ref[:, at].astype(f32)
        far_ref[:, at] = spread(reach, expand_ref[:, at]) * (gate / (1.0 + jnp.exp(-gate)))


def mix_kernel(count, *refs):
    messages = refs[:count]
    c_ref, own_ref, far_ref, gain_ref, table_ref, expand_ref, out_ref = refs[count:]
    tokens, width = own_ref.shape
    states = c_ref.shape[1]
    heads = expand_ref.shape[0]
    base = width + states
    c_group = c_ref[...]
    inners = []
    decays = []
    for msg_ref in messages:
        inners.append(dot_nt(c_group, msg_ref[:, width:base]).astype(bf16))
        decay = dot(msg_ref[:16, base : base + heads], expand_ref[...]) + dot(
            msg_ref[:16, base + heads : base + 2 * heads], expand_ref[...]
        )
        decays.append(decay[:1, :])
    norm_width = NORM_HEADS * P_SIZE
    table = table_ref[...]
    parts = []
    for start in range(0, width, norm_width):
        pres = []
        square = jnp.zeros((tokens, 1), f32)
        for begin in range(start, start + norm_width, H_BLOCK):
            at = slice(begin, begin + H_BLOCK)
            carried = None
            for k in reversed(range(count)):
                term = dot(inners[k], messages[k][:, at])
                carried = term if carried is None else term + decays[k][:, at] * carried
            pre = own_ref[:, at]
            if carried is not None:
                pre = pre + far_ref[:, at] * carried
            square = square + jnp.sum(pre * pre, axis=1, keepdims=True)
            pres.append(pre)
        inverse = lax.rsqrt(square * (1.0 / norm_width) + norm_eps)
        for index, pre in enumerate(pres):
            at = slice(start + index * H_BLOCK, start + (index + 1) * H_BLOCK)
            signed = (pre * inverse * gain_ref[:, at]).astype(bf16)
            parts.append(dot(signed, table))
    butterflies(parts)
    for index, part in enumerate(parts):
        out_ref[:, index * H_BLOCK : (index + 1) * H_BLOCK] = part.astype(bf16)


def half_at(which, size):
    return pl.ds(pl.multiple_of(which * size, size), size)


def pack_kernel(
    where_ref,
    x_ref,
    gate_ref,
    b_ref,
    c_ref,
    step_ref,
    decay_ref,
    expand_ref,
    pair_ref,
    straight_ref,
    cross_ref,
):
    tokens, width = x_ref.shape
    half, heads, states = width // 2, step_ref.shape[1] // 2, b_ref.shape[1]
    member = where_ref[0]
    step = step_ref[...]
    decay = decay_ref[...]
    triangle = causal_mask(tokens).astype(f32).astype(bf16)
    cumul = exact_dot(triangle, decay)
    total = cumul[tokens - 1 : tokens, :]
    scale = jnp.exp(total - cumul) * step
    kept = jnp.exp(total)

    def pick(value, which):
        return jnp.where(which == 0, value[:, :heads], value[:, heads:])

    other = 1 - member
    pair_ref[:, :half] = x_ref[:, half_at(other, half)]
    pair_ref[:, half : 2 * half] = gate_ref[:, half_at(other, half)]
    pair_ref[:, 2 * half : 2 * half + states] = b_ref[...]
    base = 2 * half + 2 * states
    pair_ref[:, 2 * half + states : base] = c_ref[...]
    pair_ref[:, base:] = jnp.zeros((tokens, pair_ref.shape[1] - base), bf16)
    terms = parts_of(pick(step, other), 3) + parts_of(pick(decay, other), 3)
    for index, term in enumerate(terms):
        pair_ref[:, base + index * heads : base + (index + 1) * heads] = term

    base = half + states
    for out_ref, which in ((straight_ref, member), (cross_ref, other)):
        wide = spread(pick(scale, which), expand_ref[...])
        out_ref[:, :half] = (x_ref[:, half_at(which, half)].astype(f32) * wide).astype(bf16)
        out_ref[:, half:base] = b_ref[...]
        out_ref[:, base:] = jnp.zeros((tokens, out_ref.shape[1] - base), bf16)
        for index, term in enumerate(parts_of(pick(kept, which), 2)):
            out_ref[:, base + index * heads : base + (index + 1) * heads] = jnp.broadcast_to(
                term, (tokens, heads)
            )


def pair_kernel(
    where_ref,
    x_ref,
    gate_ref,
    b_ref,
    c_ref,
    step_ref,
    decay_ref,
    msg_ref,
    skip_ref,
    expand_ref,
    own_ref,
    far_ref,
    c_pair_ref,
    x_both,
    gate_both,
    b_both,
    step_both,
    decay_both,
):
    tokens, width = x_ref.shape
    half, heads, states = width // 2, step_ref.shape[1] // 2, b_ref.shape[1]
    member = where_ref[0]
    mine, theirs = half_at(member, tokens), half_at(1 - member, tokens)

    def pick(value):
        return jnp.where(member == 0, value[:, :heads], value[:, heads:])

    x_both[mine, :] = x_ref[:, half_at(member, half)]
    x_both[theirs, :] = msg_ref[:, :half]
    gate_both[mine, :] = gate_ref[:, half_at(member, half)]
    gate_both[theirs, :] = msg_ref[:, half : 2 * half]
    b_both[mine, :] = b_ref[...]
    b_both[theirs, :] = msg_ref[:, 2 * half : 2 * half + states]
    base = 2 * half + 2 * states
    c_pair_ref[mine, :] = c_ref[...]
    c_pair_ref[theirs, :] = msg_ref[:, 2 * half + states : base]

    def received(first):
        terms = [
            msg_ref[:, base + index * heads : base + (index + 1) * heads].astype(f32)
            for index in range(first, first + 3)
        ]
        return (terms[2] + terms[1]) + terms[0]

    step_both[mine, :] = pick(step_ref[...])
    step_both[theirs, :] = received(0)
    decay_both[mine, :] = pick(decay_ref[...])
    decay_both[theirs, :] = received(3)

    span = 2 * tokens
    causal = causal_mask(span)
    inner = jnp.where(causal, dot_nt(c_pair_ref[...], b_both[...]), 0.0)
    cumul = exact_dot(causal.astype(f32).astype(bf16), decay_both[...])
    cumul_t = cumul.T
    step_t = step_both[...].T
    skip = skip_ref[:, half_at(member, half)]
    reach = parts_of(jnp.exp(cumul), 2)
    first = lax.broadcasted_iota(jnp.int32, (tokens, 2 * P_SIZE), 1) < P_SIZE
    for pair in range(heads // 2):
        at = slice(pair * 2 * P_SIZE, (pair + 1) * 2 * P_SIZE)
        spans = []
        for block in range(2):
            x_block = x_both[block * tokens : (block + 1) * tokens, at]
            zero = jnp.zeros_like(x_block)
            spans.append((jnp.where(first, x_block, zero), jnp.where(first, zero, x_block)))
        for block in range(2):
            rows = slice(block * tokens, (block + 1) * tokens)
            mixings, values = [], []
            for place, head in enumerate((2 * pair, 2 * pair + 1)):
                for earlier in range(block + 1):
                    cols = slice(earlier * tokens, (earlier + 1) * tokens)
                    differ = cumul[rows, head : head + 1] - cumul_t[head : head + 1, cols]
                    if earlier == block:
                        differ = jnp.where(causal[:tokens, :tokens], differ, 0.0)
                    ratio = jnp.exp(differ)
                    mixings.append(
                        (ratio * (inner[rows, cols] * step_t[head : head + 1, cols])).astype(bf16)
                    )
                    values.append(spans[earlier][place])
            own = dot(jnp.concatenate(mixings, axis=1), jnp.concatenate(values, axis=0))
            own = own + x_both[rows, at].astype(f32) * skip[:, at]
            gate = gate_both[rows, at].astype(f32)
            gate = gate / (1.0 + jnp.exp(-gate))
            own_ref[rows, at] = own * gate
            wide = sum(dot(term[rows, :], expand_ref[:, at]) for term in reach)
            far_ref[rows, at] = wide * gate


def gate_mix_kernel(count, pieces, *refs):
    straight, cross = refs[:count], refs[count : 2 * count]
    where_ref, c_ref, own_ref, far_ref, gain_ref, table_ref, expand_ref = refs[2 * count : -2]
    out_refs = refs[-2:]
    span, half = own_ref.shape
    states = c_ref.shape[1]
    heads = expand_ref.shape[0]
    base = half + states
    member = where_ref[0]
    c_pair = c_ref[...]

    def kept(msg_ref):
        return (
            dot(msg_ref[:16, base : base + heads], expand_ref[...])
            + dot(msg_ref[:16, base + heads : base + 2 * heads], expand_ref[...])
        )[:1, :]

    inners, factors, pair_kept = [], [], []
    for straight_ref, cross_ref in zip(straight, cross):
        inners.append(
            [dot_nt(c_pair, ref[:, half:base]).astype(bf16) for ref in (straight_ref, cross_ref)]
        )
        one, two = kept(straight_ref), kept(cross_ref)
        pair_kept.append(one * two)
        factors.append((jnp.where(member == 0, two, 1.0), jnp.where(member == 0, 1.0, one)))
    gain = gain_ref[:, half_at(member, half)]
    table = table_ref[...]
    parts = []
    norm_width = NORM_HEADS * P_SIZE
    for start in range(0, half, norm_width):
        pres = []
        square = jnp.zeros((span, 1), f32)
        for begin in range(start, start + norm_width, H_BLOCK):
            at = slice(begin, begin + H_BLOCK)
            pre = own_ref[:, at]
            carried = None
            for k in reversed(range(count)):
                term = factors[k][0][:, at] * dot(inners[k][0], straight[k][:, at])
                term = term + factors[k][1][:, at] * dot(inners[k][1], cross[k][:, at])
                carried = term if carried is None else term + pair_kept[k][:, at] * carried
            if carried is not None:
                pre = pre + far_ref[:, at] * carried
            square = square + jnp.sum(pre * pre, axis=1, keepdims=True)
            pres.append(pre)
        inverse = lax.rsqrt(square * (1.0 / norm_width) + norm_eps)
        for index, pre in enumerate(pres):
            at = slice(start + index * H_BLOCK, start + (index + 1) * H_BLOCK)
            parts.append(dot((pre * inverse * gain[:, at]).astype(bf16), table))
    butterflies(parts)
    size = span // pieces
    for index, part in enumerate(parts):
        at = slice(index * H_BLOCK, (index + 1) * H_BLOCK)
        part = part.astype(bf16)
        for piece in range(pieces):
            to = slice(piece // 2 * size, (piece // 2 + 1) * size)
            out_refs[piece % 2][to, at] = part[piece * size : (piece + 1) * size, :]


def butterflies(parts):
    span = 1
    while span < len(parts):
        for low in range(len(parts)):
            if low & span == 0:
                a, b = parts[low], parts[low + span]
                parts[low], parts[low + span] = a + b, a - b
        span *= 2


def project_kernel(pairs, where_ref, *refs):
    pieces = refs[: 2 * pairs]
    up_ref, down_ref, weight_ref, out_ref = refs[2 * pairs :]
    half = pieces[0].shape[1]
    sign = (1 - 2 * where_ref[0]).astype(f32)
    sub_count, chan_count, _, blocks, size, features = out_ref.shape
    for pair in range(pairs):
        one = pieces[2 * pair][...].astype(f32)
        two = pieces[2 * pair + 1][...].astype(f32)
        total = None
        for side, mixed in enumerate((one + two, (one - two) * sign)):
            at = slice(side * half, (side + 1) * half)
            quant = jnp.clip(mixed * up_ref[:, at], -clip_level, clip_level).astype(bf16)
            scaled = (quant.astype(f32) * down_ref[:, at]).astype(bf16)
            term = dot(scaled, weight_ref[at, :])
            total = term if total is None else total + term
        total = total.astype(bf16)
        row = 0
        for block in range(blocks):
            for chan in range(chan_count):
                for sub in range(sub_count):
                    out_ref[sub, chan, pair, block] = total[row : row + size, :]
                    row += size


def place_kernel(count, where_ref, *refs):
    out_ref = refs[-1]
    size, features = refs[0].shape
    for index, ref in enumerate(refs[:-1]):
        group, distance = index // count, index % count
        at = half_at(where_ref[0] ^ distance, features)
        out_ref[group * size : (group + 1) * size, at] = ref[...]


def sylvester(order):
    table = np.ones((1, 1), np.float32)
    while table.shape[0] < order:
        table = np.block([[table, table], [table, -table]])
    return table


def shift_up(value, axis, distance):
    count = lax.axis_size(axis)
    return lax.ppermute(value, axis, [(k, k + distance) for k in range(count - distance)])


def turn(value, axis, distance):
    count = lax.axis_size(axis)
    return lax.ppermute(value, axis, [(k, (k + distance) % count) for k in range(count)])


def swap(value, axis, bit):
    count = lax.axis_size(axis)
    return lax.ppermute(value, axis, [(k, k ^ (1 << bit)) for k in range(count)])


def bits_of(axis):
    return range(lax.axis_size(axis).bit_length() - 1)


def halve(value, axis):
    here = lax.axis_index(axis)
    for bit in reversed(bits_of(axis)):
        pair = value.reshape((2, value.shape[0] // 2) + value.shape[1:])
        mine = here // 2**bit % 2
        keep = lax.dynamic_index_in_dim(pair, mine, 0, keepdims=False)
        give = lax.dynamic_index_in_dim(pair, 1 - mine, 0, keepdims=False)
        value = (keep.astype(f32) + swap(give, axis, bit).astype(f32)).astype(bf16)
    return value[0]


def call(kernel, out_shape, name, args, scalars=0, scratch=()):
    specs = [pl.BlockSpec(memory_space=pltpu.SMEM)] * scalars
    specs += [pl.BlockSpec(memory_space=pltpu.VMEM)] * (len(args) - scalars)
    return pl.pallas_call(
        kernel,
        out_shape=out_shape,
        in_specs=specs,
        scratch_shapes=scratch,
        compiler_params=PARAMS,
        name=name,
    )(*args)


def swap_seq(value, distance):
    count = lax.axis_size("seq")
    return lax.ppermute(value, "seq", [(k, k ^ distance) for k in range(count)])


def paired_body(
    x_in,
    b_in,
    c_in,
    step_size,
    log_decay,
    skip,
    gate_in,
    norm_gain,
    walsh_sign,
    channel_shift_power,
    out_weight,
):
    tokens, width = x_in.shape
    heads = step_size.shape[1]
    states = b_in.shape[2]
    half, half_heads = width // 2, heads // 2
    seq_count, chan_count, sub_count = (lax.axis_size(a) for a in ("seq", "chan", "sub"))
    pairs = seq_count // 2
    here = lax.axis_index("seq")
    member = here % 2
    where = jnp.full((1,), member, jnp.int32)
    group_local = lax.axis_index("sub") * heads // (LOCAL_HEADS // G)
    b_group = lax.dynamic_slice_in_dim(b_in, group_local, 1, 1)[:, 0, :]
    c_group = lax.dynamic_slice_in_dim(c_in, group_local, 1, 1)[:, 0, :]
    expand = jnp.asarray(np.kron(np.eye(half_heads), np.ones((1, P_SIZE))), bf16)
    table = jnp.asarray(sylvester(H_BLOCK), bf16)

    def shape(rows, columns, kind):
        return jax.ShapeDtypeStruct((rows, columns), kind)

    def padded(columns):
        return pl.cdiv(columns, LANES) * LANES

    local = (x_in, gate_in, b_group, c_group, step_size, log_decay)
    later = shape(tokens, half + states + padded(2 * half_heads), bf16)
    to_pair, straight, cross = call(
        pack_kernel,
        (shape(tokens, 2 * half + 2 * states + padded(6 * half_heads), bf16), later, later),
        "pack",
        (where, *local, expand),
        1,
    )
    to_pair = swap_seq(to_pair, 1)
    straights, crosses = [], []
    for ahead in range(1, pairs):
        firsts = range(seq_count - 2 * ahead)
        straights.append(lax.ppermute(straight, "seq", [(k, k + 2 * ahead) for k in firsts]))
        crosses.append(lax.ppermute(cross, "seq", [(k, (k ^ 1) + 2 * ahead) for k in firsts]))

    span = 2 * tokens
    own, far, c_pair = call(
        pair_kernel,
        (shape(span, half, f32), shape(span, half, f32), shape(span, states, bf16)),
        "pair",
        (where, *local, to_pair, jnp.repeat(skip, P_SIZE)[None, :], expand),
        1,
        (
            pltpu.VMEM((span, half), bf16),
            pltpu.VMEM((span, half), bf16),
            pltpu.VMEM((span, states), bf16),
            pltpu.VMEM((span, half_heads), f32),
            pltpu.VMEM((span, half_heads), f32),
        ),
    )
    signed_gain = (jnp.where(walsh_sign == 1, 1.0, -1.0) * norm_gain)[None, :]
    owners = chan_count * sub_count
    size = tokens // (2 * owners)
    count = len(straights)
    chunks = pl.pallas_call(
        functools.partial(gate_mix_kernel, count, span // size),
        out_shape=(shape(tokens, half, bf16),) * 2,
        in_specs=[pl.BlockSpec(memory_space=pltpu.VMEM)] * (2 * count)
        + [pl.BlockSpec(memory_space=pltpu.SMEM)]
        + [pl.BlockSpec(memory_space=pltpu.VMEM)] * 6,
        compiler_params=PARAMS,
        name="mix",
    )(*straights, *crosses, where, c_pair, own, far, signed_gain, table, expand)

    def across(mixed):
        for axis in ("sub", "chan"):
            place = lax.axis_index(axis)
            for bit in bits_of(axis):
                sign = 1.0 - 2.0 * (place // 2**bit % 2).astype(f32)
                mixed = (mixed.astype(f32) * sign + swap(mixed, axis, bit).astype(f32)).astype(bf16)
        return mixed

    first, second = across(chunks[0]), across(chunks[1])
    gathered = [first, swap_seq(first, 1)]
    for ahead in range(1, pairs):
        gathered.append(swap_seq(first, 2 * ahead))
        gathered.append(swap_seq(gathered[-1], 1))
    gathered = [gathered, [second] + [swap_seq(second, k) for k in range(1, seq_count)]]

    up = (power_two(channel_shift_power, 1) * (1.0 / math.sqrt(LOCAL_HEADS * P_SIZE)))[None, :]
    down = power_two(channel_shift_power, -1)[None, :]
    features = out_weight.shape[1]
    placed = []
    for pieces in gathered:
        partial = call(
            functools.partial(project_kernel, pairs),
            jax.ShapeDtypeStruct((sub_count, chan_count, pairs, 2, size, features), bf16),
            "project",
            (where, *pieces, up, down, out_weight),
            1,
        )
        summed = halve(halve(partial, "sub"), "chan")
        for distance in range(seq_count):
            block = (member + distance) % 2
            value = lax.dynamic_index_in_dim(summed[distance // 2], block, 0, keepdims=False)
            placed.append(swap_seq(value, distance) if distance else value)
    return call(
        functools.partial(place_kernel, seq_count),
        shape(2 * size, seq_count * features, bf16),
        "place",
        (jnp.full((1,), here, jnp.int32), *placed),
        1,
    )


def body(x_in, b_in, c_in, step_size, *rest):
    tokens, heads = step_size.shape
    seq_count = lax.axis_size("seq")
    pieces = 2 * lax.axis_size("chan") * lax.axis_size("sub")
    if (
        heads % (2 * NORM_HEADS) == 0
        and seq_count % 2 == 0
        and seq_count & (seq_count - 1) == 0
        and tokens % (16 * pieces) == 0
    ):
        return paired_body(x_in, b_in, c_in, step_size, *rest)
    return plain_body(x_in, b_in, c_in, step_size, *rest)


def plain_body(
    x_in,
    b_in,
    c_in,
    step_size,
    log_decay,
    skip,
    gate_in,
    norm_gain,
    walsh_sign,
    channel_shift_power,
    out_weight,
):
    tokens, width = x_in.shape
    heads = step_size.shape[1]
    states = b_in.shape[2]
    seq_count = lax.axis_size("seq")
    sub_index = lax.axis_index("sub")
    group_local = sub_index * heads // (LOCAL_HEADS // G)
    b_group = lax.dynamic_slice_in_dim(b_in, group_local, 1, 1)[:, 0, :]
    c_group = lax.dynamic_slice_in_dim(c_in, group_local, 1, 1)[:, 0, :]
    expand = jnp.asarray(np.kron(np.eye(heads), np.ones((1, P_SIZE))), bf16)
    table = jnp.asarray(sylvester(H_BLOCK), bf16)

    tail = pl.cdiv(2 * heads, LANES) * LANES
    message, cumul = pl.pallas_call(
        message_kernel,
        out_shape=(
            jax.ShapeDtypeStruct((tokens, width + states + tail), bf16),
            jax.ShapeDtypeStruct((tokens, heads), f32),
        ),
        compiler_params=PARAMS,
        name="message",
    )(x_in, b_group, step_size, log_decay, expand)
    arrived = [shift_up(message, "seq", k) for k in range(1, seq_count)]

    wide_skip = jnp.repeat(skip, P_SIZE)[None, :]
    own, far = pl.pallas_call(
        local_kernel,
        out_shape=(
            jax.ShapeDtypeStruct((tokens, width), f32),
            jax.ShapeDtypeStruct((tokens, width), f32),
        ),
        compiler_params=PARAMS,
        name="local",
    )(x_in, b_group, c_group, step_size, cumul, gate_in, wide_skip, expand)

    signed_gain = (jnp.where(walsh_sign == 1, 1.0, -1.0) * norm_gain)[None, :]
    mixed = pl.pallas_call(
        functools.partial(mix_kernel, len(arrived)),
        out_shape=jax.ShapeDtypeStruct((tokens, width), bf16),
        compiler_params=PARAMS,
        name="mix",
    )(*arrived, c_group, own, far, signed_gain, table, expand)

    for axis in ("sub", "chan"):
        here = lax.axis_index(axis)
        for bit in bits_of(axis):
            other = swap(mixed.astype(bf16), axis, bit).astype(f32)
            sign = 1.0 - 2.0 * (here // 2**bit % 2).astype(f32)
            mixed = mixed.astype(f32) * sign + other
    rotated = mixed * (1.0 / math.sqrt(LOCAL_HEADS * P_SIZE))
    quant = jnp.clip(
        rotated * power_two(channel_shift_power, 1)[None, :], -clip_level, clip_level
    ).astype(bf16)
    scaled = (quant.astype(f32) * power_two(channel_shift_power, -1)[None, :]).astype(bf16)

    chan_count, sub_count = lax.axis_size("chan"), lax.axis_size("sub")
    rows = tokens // (chan_count * sub_count)
    order = sorted(range(1, seq_count), key=lambda k: -min(k, seq_count - k))
    blocks = {0: scaled}
    for k in order:
        blocks[k] = turn(scaled, "seq", k)
    sums = []
    for k in [0] + order:
        partial = dot(blocks[k], out_weight).astype(bf16)
        partial = partial.reshape(chan_count, sub_count, rows, -1)
        partial = halve(jnp.swapaxes(partial, 0, 1), "sub")
        done = halve(partial, "chan")
        sums.append((k, turn(done, "seq", -k % seq_count) if k else done))
    pieces = [value for _, value in sorted(sums, key=lambda item: item[0])]
    stacked = jnp.stack(pieces + pieces, axis=0)
    here = lax.axis_index("seq")
    placed = lax.dynamic_slice_in_dim(
        stacked, (seq_count - here) % seq_count, seq_count, 0
    )
    return jnp.swapaxes(placed, 0, 1).reshape(rows, -1)


def solution(mesh):
    return jax.shard_map(
        body,
        mesh=mesh,
        in_specs=(
            P(("groups", "seq"), ("chan", "sub")),
            P(("groups", "seq"), "chan", None),
            P(("groups", "seq"), "chan", None),
            P(("groups", "seq"), ("chan", "sub")),
            P(("groups", "seq"), ("chan", "sub")),
            P(("chan", "sub")),
            P(("groups", "seq"), ("chan", "sub")),
            P(("chan", "sub")),
            P(("chan", "sub")),
            P(("chan", "sub")),
            P(("chan", "sub"), "seq"),
        ),
        out_specs=P(("groups", "seq", "chan", "sub"), None),
        check_vma=False,
    )
```

```python
import functools
import math

import jax
import jax.numpy as jnp
import numpy as np
from jax import lax
from jax.experimental import pallas as pl
from jax.experimental.pallas import tpu as pltpu
from jax.sharding import PartitionSpec as P

LOCAL_HEADS = 128
P_SIZE = 64
G = 4
NORM_HEADS = 16


norm_eps = 1e-05
clip_level = 4.0
expo_levels = (-1, 0, 1, 2, 3)
LANES = 128
H_BLOCK = 256
COST = pl.CostEstimate(flops=1, transcendentals=0, bytes_accessed=30_000_000)
f32 = jnp.float32
bf16 = jnp.bfloat16
PARAMS = pltpu.CompilerParams(vmem_limit_bytes=16 * 2**20)
WIDE_PARAMS = pltpu.CompilerParams(vmem_limit_bytes=16 * 2**20)


def power_two(expo, sign_flip):
    result = jnp.zeros(expo.shape, jnp.float32)
    for level in expo_levels:
        result = result + jnp.where(
            expo == level, jnp.float32(2.0 ** (sign_flip * level)), jnp.float32(0.0)
        )
    return result


def dot(a, b):
    return jnp.dot(a, b, preferred_element_type=f32)


def dot_nt(a, b):
    return lax.dot_general(a, b, (((1,), (1,)), ((), ())), preferred_element_type=f32)


def parts_of(value, count):
    terms = []
    for _ in range(count):
        term = value.astype(bf16)
        terms.append(term)
        value = value - term.astype(f32)
    return terms


def exact_dot(exact, value, count=3):
    return sum(dot(exact, term) for term in parts_of(value, count))


def spread(value, expand, count=2):
    return sum(dot(term, expand) for term in parts_of(value, count))


def causal_mask(size):
    row = lax.broadcasted_iota(jnp.int32, (size, size), 0)
    col = lax.broadcasted_iota(jnp.int32, (size, size), 1)
    return row >= col


def message_kernel(x_ref, b_ref, step_ref, decay_ref, expand_ref, msg_ref, cumul_ref):
    tokens, width = x_ref.shape
    heads = step_ref.shape[1]
    states = b_ref.shape[1]
    expand = expand_ref[...]
    triangle = causal_mask(tokens).astype(f32).astype(bf16)
    cumul = exact_dot(triangle, decay_ref[...])
    cumul_ref[...] = cumul
    total = cumul[tokens - 1 : tokens, :]
    scale = spread(jnp.exp(total - cumul) * step_ref[...], expand)
    msg_ref[:, :width] = (x_ref[...].astype(f32) * scale).astype(bf16)
    msg_ref[:, width : width + states] = b_ref[...]
    high, low = parts_of(jnp.exp(total), 2)
    base = width + states
    msg_ref[:, base:] = jnp.zeros((tokens, msg_ref.shape[1] - base), bf16)
    msg_ref[:, base : base + heads] = jnp.broadcast_to(high, (tokens, heads))
    msg_ref[:, base + heads : base + 2 * heads] = jnp.broadcast_to(low, (tokens, heads))


def local_kernel(
    x_ref, b_ref, c_ref, step_ref, cumul_ref, gate_ref, skip_ref, expand_ref, own_ref, far_ref
):
    tokens, width = x_ref.shape
    heads = step_ref.shape[1]
    causal = causal_mask(tokens)
    inner = dot_nt(c_ref[...], b_ref[...])
    cumul = cumul_ref[...]
    cumul_t = cumul.T
    step_t = step_ref[...].T
    first = lax.broadcasted_iota(jnp.int32, (tokens, 2 * P_SIZE), 1) < P_SIZE
    for pair in range(heads // 2):
        mixings = []
        for head in (2 * pair, 2 * pair + 1):
            differ = cumul[:, head : head + 1] - cumul_t[head : head + 1, :]
            ratio = jnp.exp(jnp.where(causal, differ, -jnp.inf))
            mixings.append((ratio * (inner * step_t[head : head + 1, :])).astype(bf16))
        at = slice(pair * 2 * P_SIZE, (pair + 1) * 2 * P_SIZE)
        x_pair = x_ref[:, at]
        zero = jnp.zeros_like(x_pair)
        blocks = jnp.concatenate(
            [jnp.where(first, x_pair, zero), jnp.where(first, zero, x_pair)], axis=0
        )
        own = dot(jnp.concatenate(mixings, axis=1), blocks)
        own = own + x_pair.astype(f32) * skip_ref[:, at]
        gate = gate_ref[:, at].astype(f32)
        own_ref[:, at] = own * (gate / (1.0 + jnp.exp(-gate)))
    reach = jnp.exp(cumul)
    tile = min(width, 512)
    for start in range(0, width, tile):
        at = slice(start, start + tile)
        gate = gate_ref[:, at].astype(f32)
        far_ref[:, at] = spread(reach, expand_ref[:, at]) * (gate / (1.0 + jnp.exp(-gate)))


def mix_kernel(count, *refs):
    messages = refs[:count]
    c_ref, own_ref, far_ref, gain_ref, table_ref, expand_ref, out_ref = refs[count:]
    tokens, width = own_ref.shape
    states = c_ref.shape[1]
    heads = expand_ref.shape[0]
    base = width + states
    c_group = c_ref[...]
    inners = []
    decays = []
    for msg_ref in messages:
        inners.append(dot_nt(c_group, msg_ref[:, width:base]).astype(bf16))
        decay = dot(msg_ref[:16, base : base + heads], expand_ref[...]) + dot(
            msg_ref[:16, base + heads : base + 2 * heads], expand_ref[...]
        )
        decays.append(decay[:1, :])
    norm_width = NORM_HEADS * P_SIZE
    table = table_ref[...]
    parts = []
    for start in range(0, width, norm_width):
        pres = []
        square = jnp.zeros((tokens, 1), f32)
        for begin in range(start, start + norm_width, H_BLOCK):
            at = slice(begin, begin + H_BLOCK)
            carried = None
            for k in reversed(range(count)):
                term = dot(inners[k], messages[k][:, at])
                carried = term if carried is None else term + decays[k][:, at] * carried
            pre = own_ref[:, at]
            if carried is not None:
                pre = pre + far_ref[:, at] * carried
            square = square + jnp.sum(pre * pre, axis=1, keepdims=True)
            pres.append(pre)
        inverse = lax.rsqrt(square * (1.0 / norm_width) + norm_eps)
        for index, pre in enumerate(pres):
            at = slice(start + index * H_BLOCK, start + (index + 1) * H_BLOCK)
            signed = (pre * inverse * gain_ref[:, at]).astype(bf16)
            parts.append(dot(signed, table))
    butterflies(parts)
    for index, part in enumerate(parts):
        out_ref[:, index * H_BLOCK : (index + 1) * H_BLOCK] = part.astype(bf16)


def half_at(which, size):
    return pl.ds(pl.multiple_of(which * size, size), size)


def start_all(copies):
    for copy in copies:
        copy.start()
    return copies


def wait_all(copies):
    for copy in copies:
        copy.wait()


def later_kernel(
    where_ref,
    x_ref,
    b_ref,
    step_ref,
    decay_ref,
    straight_ref,
    cross_ref,
    x_own,
    b_own,
    step_own,
    decay_own,
    sems,
):
    copies = start_all(
        [
            pltpu.make_async_copy(ref, own, sems.at[index])
            for index, (ref, own) in enumerate(
                (
                    (decay_ref, decay_own),
                    (step_ref, step_own),
                    (b_ref, b_own),
                    (x_ref, x_own),
                )
            )
        ]
    )
    tokens, width = x_ref.shape
    half, heads, states = width // 2, step_ref.shape[0] // 2, b_ref.shape[1]
    member = where_ref[0]
    expand = expansion(heads)
    triangle = causal_mask(tokens).astype(f32).astype(bf16)
    wait_all(copies[:2])
    cumul = exact_dot(triangle, decay_own[...].T)
    total = cumul[tokens - 1 : tokens, :]
    scale = jnp.exp(total - cumul) * step_own[...].T
    kept = jnp.exp(total)

    def pick(value, which):
        return jnp.where(which == 0, value[:, :heads], value[:, heads:])

    base = half + states
    copies[2].wait()
    copies[3].wait()
    for out_ref, which in ((straight_ref, member), (cross_ref, 1 - member)):
        wide = spread(pick(scale, which), expand)
        out_ref[:, :half] = (x_own[:, half_at(which, half)].astype(f32) * wide).astype(bf16)
        out_ref[:, half:base] = b_own[...]
        out_ref[:, base:] = jnp.zeros((tokens, out_ref.shape[1] - base), bf16)
        for index, term in enumerate(parts_of(pick(kept, which), 2)):
            out_ref[:, base + index * heads : base + (index + 1) * heads] = jnp.broadcast_to(
                term, (tokens, heads)
            )


def pack_kernel(
    where_ref,
    x_ref,
    gate_ref,
    b_ref,
    c_ref,
    step_ref,
    decay_ref,
    after_ref,
    pair_ref,
    step_own,
    decay_own,
    sems,
):
    tokens, width = x_ref.shape
    half, heads, states = width // 2, step_ref.shape[0] // 2, b_ref.shape[1]
    other = 1 - where_ref[0]
    base = 2 * half + 2 * states
    copies = start_all(
        [
            pltpu.make_async_copy(ref, own, sems.at[index])
            for index, (ref, own) in enumerate(
                (
                    (decay_ref, decay_own),
                    (step_ref, step_own),
                    (x_ref.at[:, half_at(other, half)], pair_ref.at[:, :half]),
                    (gate_ref.at[:, half_at(other, half)], pair_ref.at[:, half : 2 * half]),
                    (b_ref, pair_ref.at[:, 2 * half : 2 * half + states]),
                    (c_ref, pair_ref.at[:, 2 * half + states : base]),
                )
            )
        ]
    )

    def pick(value):
        return jnp.where(other == 0, value[:heads, :], value[heads:, :]).T

    wait_all(copies[:2])
    pair_ref[:, base:] = jnp.zeros((tokens, pair_ref.shape[1] - base), bf16)
    terms = parts_of(pick(step_own[...]), 3) + parts_of(pick(decay_own[...]), 3)
    for index, term in enumerate(terms):
        pair_ref[:, base + index * heads : base + (index + 1) * heads] = term
    wait_all(copies[2:])


def expansion(heads):
    shape = (heads, heads * P_SIZE)
    row = lax.broadcasted_iota(jnp.int32, shape, 0)
    col = lax.broadcasted_iota(jnp.int32, shape, 1)
    return ((col >= row * P_SIZE) & (col < (row + 1) * P_SIZE)).astype(f32).astype(bf16)


def pair_kernel(
    where_ref,
    x_ref,
    gate_ref,
    b_ref,
    c_ref,
    step_ref,
    decay_ref,
    msg_ref,
    skip_ref,
    own_ref,
    far_ref,
    c_pair_ref,
    x_both,
    gate_both,
    b_both,
    step_both,
    decay_both,
    step_own,
    decay_own,
    sems,
):
    tokens, width = x_ref.shape
    half, heads, states = width // 2, step_ref.shape[0] // 2, b_ref.shape[1]
    member = where_ref[0]
    mine, theirs = half_at(member, tokens), half_at(1 - member, tokens)
    copies = start_all(
        [
            pltpu.make_async_copy(ref, own, sems.at[index])
            for index, (ref, own) in enumerate(
                (
                    (decay_ref, decay_own),
                    (step_ref, step_own),
                    (b_ref, b_both.at[mine, :]),
                    (c_ref, c_pair_ref.at[mine, :]),
                    (x_ref.at[:, half_at(member, half)], x_both.at[mine, :]),
                    (gate_ref.at[:, half_at(member, half)], gate_both.at[mine, :]),
                )
            )
        ]
    )

    def pick(value):
        return jnp.where(member == 0, value[:heads, :], value[heads:, :]).T

    x_both[theirs, :] = msg_ref[:, :half]
    gate_both[theirs, :] = msg_ref[:, half : 2 * half]
    b_both[theirs, :] = msg_ref[:, 2 * half : 2 * half + states]
    base = 2 * half + 2 * states
    c_pair_ref[theirs, :] = msg_ref[:, 2 * half + states : base]

    def received(first):
        terms = [
            msg_ref[:, base + index * heads : base + (index + 1) * heads].astype(f32)
            for index in range(first, first + 3)
        ]
        return (terms[2] + terms[1]) + terms[0]

    step_both[theirs, :] = received(0)
    decay_both[theirs, :] = received(3)
    wait_all(copies)
    step_both[mine, :] = pick(step_own[...])
    decay_both[mine, :] = pick(decay_own[...])

    span = 2 * tokens
    causal = causal_mask(span)
    inner = jnp.where(causal, dot_nt(c_pair_ref[...], b_both[...]), 0.0)
    cumul = exact_dot(causal.astype(f32).astype(bf16), decay_both[...])
    cumul_t = cumul.T
    step_t = step_both[...].T
    skip = skip_ref[:, half_at(member, half)]
    expand = expansion(heads)
    reach = parts_of(jnp.exp(cumul), 2)
    first = lax.broadcasted_iota(jnp.int32, (tokens, 2 * P_SIZE), 1) < P_SIZE
    for pair in range(heads // 2):
        at = slice(pair * 2 * P_SIZE, (pair + 1) * 2 * P_SIZE)
        spans = []
        for block in range(2):
            x_block = x_both[block * tokens : (block + 1) * tokens, at]
            zero = jnp.zeros_like(x_block)
            spans.append((jnp.where(first, x_block, zero), jnp.where(first, zero, x_block)))
        for block in range(2):
            rows = slice(block * tokens, (block + 1) * tokens)
            mixings, values = [], []
            for place, head in enumerate((2 * pair, 2 * pair + 1)):
                for earlier in range(block + 1):
                    cols = slice(earlier * tokens, (earlier + 1) * tokens)
                    differ = cumul[rows, head : head + 1] - cumul_t[head : head + 1, cols]
                    if earlier == block:
                        differ = jnp.where(causal[:tokens, :tokens], differ, 0.0)
                    ratio = jnp.exp(differ)
                    mixings.append(
                        (ratio * (inner[rows, cols] * step_t[head : head + 1, cols])).astype(bf16)
                    )
                    values.append(spans[earlier][place])
            own = dot(jnp.concatenate(mixings, axis=1), jnp.concatenate(values, axis=0))
            own = own + x_both[rows, at].astype(f32) * skip[:, at]
            gate = gate_both[rows, at].astype(f32)
            gate = gate / (1.0 + jnp.exp(-gate))
            own_ref[rows, at] = own * gate
            wide = sum(dot(term[rows, :], expand[:, at]) for term in reach)
            far_ref[rows, at] = wide * gate


def gate_mix_kernel(count, pieces, *refs):
    straight, cross = refs[:count], refs[count : 2 * count]
    where_ref, c_ref, own_ref, far_ref, gain_ref, table_ref = refs[2 * count : -2]
    out_refs = refs[-2:]
    span, half = own_ref.shape
    states = c_ref.shape[1]
    heads = half // P_SIZE
    base = half + states
    member = where_ref[0]
    c_pair = c_ref[...]
    expand = expansion(heads)

    def kept(msg_ref):
        return (
            dot(msg_ref[:16, base : base + heads], expand)
            + dot(msg_ref[:16, base + heads : base + 2 * heads], expand)
        )[:1, :]

    inners, factors, pair_kept = [], [], []
    for straight_ref, cross_ref in zip(straight, cross):
        inners.append(
            [dot_nt(c_pair, ref[:, half:base]).astype(bf16) for ref in (straight_ref, cross_ref)]
        )
        one, two = kept(straight_ref), kept(cross_ref)
        pair_kept.append(one * two)
        factors.append((jnp.where(member == 0, two, 1.0), jnp.where(member == 0, 1.0, one)))
    gain = gain_ref[:, half_at(member, half)]
    table = table_ref[...]
    parts = []
    norm_width = NORM_HEADS * P_SIZE
    for start in range(0, half, norm_width):
        pres = []
        square = jnp.zeros((span, 1), f32)
        for begin in range(start, start + norm_width, H_BLOCK):
            at = slice(begin, begin + H_BLOCK)
            pre = own_ref[:, at]
            carried = None
            for k in reversed(range(count)):
                term = factors[k][0][:, at] * dot(inners[k][0], straight[k][:, at])
                term = term + factors[k][1][:, at] * dot(inners[k][1], cross[k][:, at])
                carried = term if carried is None else term + pair_kept[k][:, at] * carried
            if carried is not None:
                pre = pre + far_ref[:, at] * carried
            square = square + jnp.sum(pre * pre, axis=1, keepdims=True)
            pres.append(pre)
        inverse = lax.rsqrt(square * (1.0 / norm_width) + norm_eps)
        for index, pre in enumerate(pres):
            at = slice(start + index * H_BLOCK, start + (index + 1) * H_BLOCK)
            parts.append(dot((pre * inverse * gain[:, at]).astype(bf16), table))
    butterflies(parts)
    size = span // pieces
    for index, part in enumerate(parts):
        at = slice(index * H_BLOCK, (index + 1) * H_BLOCK)
        part = part.astype(bf16)
        for piece in range(pieces):
            to = slice(piece // 2 * size, (piece // 2 + 1) * size)
            out_refs[piece % 2][to, at] = part[piece * size : (piece + 1) * size, :]


def butterflies(parts):
    span = 1
    while span < len(parts):
        for low in range(len(parts)):
            if low & span == 0:
                a, b = parts[low], parts[low + span]
                parts[low], parts[low + span] = a + b, a - b
        span *= 2


def add_kernel(sign_ref, mixed_ref, received_ref, out_ref):
    sign = sign_ref[0].astype(f32)
    out_ref[...] = (mixed_ref[...].astype(f32) * sign + received_ref[...].astype(f32)).astype(bf16)


def project_kernel(pairs, where_ref, weight_ref, *refs):
    pieces = refs[: 2 * pairs]
    up_ref, down_ref, out_ref, weight_own, sums, sems = refs[2 * pairs :]
    rows, half = pieces[0].shape
    sign = (1 - 2 * where_ref[0]).astype(f32)
    sub_count, chan_count, _, blocks, size, features = out_ref.shape
    tile = half // 2
    copies = start_all(
        [
            pltpu.make_async_copy(
                weight_ref.at[start : start + tile, :],
                weight_own.at[start : start + tile, :],
                sems.at[start // tile],
            )
            for start in range(0, 2 * half, tile)
        ]
    )
    for step, copy in enumerate(copies):
        at = slice(step * tile, (step + 1) * tile)
        inner = slice(step * tile % half, step * tile % half + tile)
        scaled = []
        for pair in range(pairs):
            one = pieces[2 * pair][:, inner].astype(f32)
            two = pieces[2 * pair + 1][:, inner].astype(f32)
            mixed = (one - two) * sign if step * tile >= half else one + two
            quant = jnp.clip(mixed * up_ref[:, at], -clip_level, clip_level).astype(bf16)
            scaled.append((quant.astype(f32) * down_ref[:, at]).astype(bf16))
        copy.wait()
        term = dot(jnp.concatenate(scaled, axis=0), weight_own[at, :])
        if step == 0:
            sums[...] = term
        elif step < len(copies) - 1:
            sums[...] += term
        else:
            total = (sums[...] + term).astype(bf16)
    row = 0
    for pair in range(pairs):
        for block in range(blocks):
            for chan in range(chan_count):
                for sub in range(sub_count):
                    out_ref[sub, chan, pair, block] = total[row : row + size, :]
                    row += size


def place_kernel(where_ref, *refs):
    out_ref = refs[-1]
    features = refs[0].shape[1]
    for distance, ref in enumerate(refs[:-1]):
        out_ref[:, half_at(where_ref[0] ^ distance, features)] = ref[...]


def sylvester(order):
    table = np.ones((1, 1), np.float32)
    while table.shape[0] < order:
        table = np.block([[table, table], [table, -table]])
    return table


def shift_up(value, axis, distance):
    count = lax.axis_size(axis)
    return lax.ppermute(value, axis, [(k, k + distance) for k in range(count - distance)])


def turn(value, axis, distance):
    count = lax.axis_size(axis)
    return lax.ppermute(value, axis, [(k, (k + distance) % count) for k in range(count)])


def swap(value, axis, bit):
    count = lax.axis_size(axis)
    return lax.ppermute(value, axis, [(k, k ^ (1 << bit)) for k in range(count)])


def bits_of(axis):
    return range(lax.axis_size(axis).bit_length() - 1)


def halve(value, axis):
    here = lax.axis_index(axis)
    for bit in reversed(bits_of(axis)):
        pair = value.reshape((2, value.shape[0] // 2) + value.shape[1:])
        mine = here // 2**bit % 2
        keep = lax.dynamic_index_in_dim(pair, mine, 0, keepdims=False)
        give = lax.dynamic_index_in_dim(pair, 1 - mine, 0, keepdims=False)
        value = (keep.astype(f32) + swap(give, axis, bit).astype(f32)).astype(bf16)
    return value[0]


def call(kernel, out_shape, name, args, scalars=0, anywhere=0, scratch=(), params=PARAMS):
    specs = [pl.BlockSpec(memory_space=pltpu.SMEM)] * scalars
    specs += [pl.BlockSpec(memory_space=pltpu.HBM)] * anywhere
    specs += [pl.BlockSpec(memory_space=pltpu.VMEM)] * (len(args) - scalars - anywhere)
    return pl.pallas_call(
        kernel,
        out_shape=out_shape,
        in_specs=specs,
        scratch_shapes=scratch,
        compiler_params=params,
        cost_estimate=COST,
        name=name,
    )(*args)


def swap_seq(value, distance):
    count = lax.axis_size("seq")
    return lax.ppermute(value, "seq", [(k, k ^ distance) for k in range(count)])


def paired_body(
    x_in,
    b_in,
    c_in,
    step_size,
    log_decay,
    skip,
    gate_in,
    norm_gain,
    walsh_sign,
    channel_shift_power,
    out_weight,
):
    tokens, width = x_in.shape
    heads = step_size.shape[1]
    states = b_in.shape[2]
    half, half_heads = width // 2, heads // 2
    seq_count, chan_count, sub_count = (lax.axis_size(a) for a in ("seq", "chan", "sub"))
    pairs = seq_count // 2
    here = lax.axis_index("seq")
    member = here % 2
    group_local = lax.axis_index("sub") * heads // (LOCAL_HEADS // G)
    where = jnp.full((1,), member, jnp.int32)
    b_group = lax.dynamic_index_in_dim(b_in, group_local, 1, keepdims=False)
    c_group = lax.dynamic_index_in_dim(c_in, group_local, 1, keepdims=False)
    table = jnp.asarray(sylvester(H_BLOCK), bf16)

    def shape(rows, columns, kind):
        return jax.ShapeDtypeStruct((rows, columns), kind)

    def padded(columns):
        return pl.cdiv(columns, LANES) * LANES

    step, decay = step_size.T, log_decay.T
    later = shape(tokens, half + states + padded(2 * half_heads), bf16)
    head_buffer = pltpu.VMEM(step.shape, f32)
    straight, cross = call(
        later_kernel,
        (later, later),
        "later",
        (where, x_in, b_group, step, decay),
        1,
        4,
        (
            pltpu.VMEM((tokens, width), bf16),
            pltpu.VMEM((tokens, states), bf16),
            head_buffer,
            head_buffer,
            pltpu.SemaphoreType.DMA((4,)),
        ),
    )
    local = (x_in, gate_in, b_group, c_group, step, decay)
    to_pair = call(
        pack_kernel,
        shape(tokens, 2 * half + 2 * states + padded(6 * half_heads), bf16),
        "pack",
        (where, *local, straight),
        1,
        7,
        (
            head_buffer,
            head_buffer,
            pltpu.SemaphoreType.DMA((6,)),
        ),
    )
    to_pair = swap_seq(to_pair, 1)
    straights, crosses = [], []
    for ahead in range(1, pairs):
        firsts = range(seq_count - 2 * ahead)
        straights.append(lax.ppermute(straight, "seq", [(k, k + 2 * ahead) for k in firsts]))
        crosses.append(lax.ppermute(cross, "seq", [(k, (k ^ 1) + 2 * ahead) for k in firsts]))

    span = 2 * tokens
    own, far, c_pair = call(
        pair_kernel,
        (
            shape(span, half, f32),
            shape(span, half, f32),
            shape(span, states, bf16),
        ),
        "pair",
        (where, *local, to_pair, jnp.repeat(skip, P_SIZE)[None, :]),
        1,
        6,
        (
            pltpu.VMEM((span, half), bf16),
            pltpu.VMEM((span, half), bf16),
            pltpu.VMEM((span, states), bf16),
            pltpu.VMEM((span, half_heads), f32),
            pltpu.VMEM((span, half_heads), f32),
            head_buffer,
            head_buffer,
            pltpu.SemaphoreType.DMA((6,)),
        ),
    )
    signed_gain = (jnp.where(walsh_sign == 1, 1.0, -1.0) * norm_gain)[None, :]
    owners = chan_count * sub_count
    size = tokens // (2 * owners)
    count = len(straights)
    chunks = pl.pallas_call(
        functools.partial(gate_mix_kernel, count, span // size),
        out_shape=(shape(tokens, half, bf16),) * 2,
        in_specs=[pl.BlockSpec(memory_space=pltpu.VMEM)] * (2 * count)
        + [pl.BlockSpec(memory_space=pltpu.SMEM)]
        + [pl.BlockSpec(memory_space=pltpu.VMEM)] * 5,
        compiler_params=PARAMS,
        cost_estimate=COST,
        name="mix",
    )(*straights, *crosses, where, c_pair, own, far, signed_gain, table)

    def add_across(mixed, axis, bit, received):
        place = lax.axis_index(axis)
        sign = 1.0 - 2.0 * (place // 2**bit % 2).astype(f32)
        return (mixed.astype(f32) * sign + received.astype(f32)).astype(bf16)

    def across(mixed, axis):
        for bit in bits_of(axis):
            mixed = add_across(mixed, axis, bit, swap(mixed, axis, bit))
        return mixed

    first, second = (across(chunk, "sub") for chunk in chunks)
    first = across(first, "chan")
    first, second = lax.optimization_barrier((first, second))
    bits = bits_of("chan")
    for bit in bits[:-1]:
        second = add_across(second, "chan", bit, swap(second, "chan", bit))
    received = swap(second, "chan", bits[-1]) if bits else None
    ahead = range(1, pairs)
    far_first = [swap_seq(first, 2 * k) for k in ahead]
    near_first = swap_seq(first, 1)
    first, second, received, far_first, near_first = lax.optimization_barrier(
        (first, second, received, far_first, near_first)
    )
    if bits:
        sign = 1 - 2 * (lax.axis_index("chan") // 2 ** bits[-1] % 2)
        second = call(
            add_kernel,
            shape(tokens, half, bf16),
            "add",
            (jnp.full((1,), sign, jnp.int32), second, received),
            1,
        )
    passed_first = [swap_seq(value, 1) for value in far_first]
    all_first = [first, near_first]
    for far, passed in zip(far_first, passed_first):
        all_first += [far, passed]
    second_late = lax.optimization_barrier((second, passed_first))[0] if pairs > 1 else second
    all_second = [second, swap_seq(second_late, 1)]
    all_second += [swap_seq(second, k) for k in range(2, seq_count)]

    up = (power_two(channel_shift_power, 1) * (1.0 / math.sqrt(LOCAL_HEADS * P_SIZE)))[None, :]
    down = power_two(channel_shift_power, -1)[None, :]
    features = out_weight.shape[1]

    def project(pieces):
        return call(
            functools.partial(project_kernel, pairs),
            jax.ShapeDtypeStruct((sub_count, chan_count, pairs, 2, size, features), bf16),
            "project",
            (where, out_weight, *pieces, up, down),
            1,
            1,
            (
                pltpu.VMEM(out_weight.shape, bf16),
                pltpu.VMEM((pairs * tokens, features), f32),
                pltpu.SemaphoreType.DMA((4,)),
            ),
            WIDE_PARAMS,
        )

    def reduce(partial):
        return halve(halve(partial, "sub"), "chan")

    done = lax.optimization_barrier(jnp.bool_(True))
    done_first = lax.cond(
        done,
        lambda *pieces: reduce(project(pieces)),
        lambda *pieces: jnp.zeros((pairs, 2, size, features), bf16),
        *all_first,
    )
    done_first, all_second = lax.optimization_barrier((done_first, all_second))
    done_second = reduce(project(all_second))
    summed = jnp.stack([done_first, done_second], axis=2)
    returned = []
    for distance in range(seq_count):
        block = (member + distance) % 2
        value = lax.dynamic_index_in_dim(summed[distance // 2], block, 0, keepdims=False)
        value = value.reshape(2 * size, features)
        returned.append(swap_seq(value, distance) if distance else value)
    return call(
        place_kernel,
        shape(2 * size, seq_count * features, bf16),
        "place",
        (jnp.full((1,), here, jnp.int32), *returned),
        1,
    )


def body(x_in, b_in, c_in, step_size, *rest):
    tokens, heads = step_size.shape
    seq_count = lax.axis_size("seq")
    pieces = 2 * lax.axis_size("chan") * lax.axis_size("sub")
    if (
        heads % (2 * NORM_HEADS) == 0
        and seq_count % 2 == 0
        and seq_count & (seq_count - 1) == 0
        and tokens % (16 * pieces) == 0
    ):
        return paired_body(x_in, b_in, c_in, step_size, *rest)
    return plain_body(x_in, b_in, c_in, step_size, *rest)


def plain_body(
    x_in,
    b_in,
    c_in,
    step_size,
    log_decay,
    skip,
    gate_in,
    norm_gain,
    walsh_sign,
    channel_shift_power,
    out_weight,
):
    tokens, width = x_in.shape
    heads = step_size.shape[1]
    states = b_in.shape[2]
    seq_count = lax.axis_size("seq")
    sub_index = lax.axis_index("sub")
    group_local = sub_index * heads // (LOCAL_HEADS // G)
    b_group = lax.dynamic_slice_in_dim(b_in, group_local, 1, 1)[:, 0, :]
    c_group = lax.dynamic_slice_in_dim(c_in, group_local, 1, 1)[:, 0, :]
    expand = jnp.asarray(np.kron(np.eye(heads), np.ones((1, P_SIZE))), bf16)
    table = jnp.asarray(sylvester(H_BLOCK), bf16)

    tail = pl.cdiv(2 * heads, LANES) * LANES
    message, cumul = pl.pallas_call(
        message_kernel,
        out_shape=(
            jax.ShapeDtypeStruct((tokens, width + states + tail), bf16),
            jax.ShapeDtypeStruct((tokens, heads), f32),
        ),
        compiler_params=PARAMS,
        name="message",
    )(x_in, b_group, step_size, log_decay, expand)
    arrived = [shift_up(message, "seq", k) for k in range(1, seq_count)]

    wide_skip = jnp.repeat(skip, P_SIZE)[None, :]
    own, far = pl.pallas_call(
        local_kernel,
        out_shape=(
            jax.ShapeDtypeStruct((tokens, width), f32),
            jax.ShapeDtypeStruct((tokens, width), f32),
        ),
        compiler_params=PARAMS,
        name="local",
    )(x_in, b_group, c_group, step_size, cumul, gate_in, wide_skip, expand)

    signed_gain = (jnp.where(walsh_sign == 1, 1.0, -1.0) * norm_gain)[None, :]
    mixed = pl.pallas_call(
        functools.partial(mix_kernel, len(arrived)),
        out_shape=jax.ShapeDtypeStruct((tokens, width), bf16),
        compiler_params=PARAMS,
        name="mix",
    )(*arrived, c_group, own, far, signed_gain, table, expand)

    for axis in ("sub", "chan"):
        here = lax.axis_index(axis)
        for bit in bits_of(axis):
            other = swap(mixed.astype(bf16), axis, bit).astype(f32)
            sign = 1.0 - 2.0 * (here // 2**bit % 2).astype(f32)
            mixed = mixed.astype(f32) * sign + other
    rotated = mixed * (1.0 / math.sqrt(LOCAL_HEADS * P_SIZE))
    quant = jnp.clip(
        rotated * power_two(channel_shift_power, 1)[None, :], -clip_level, clip_level
    ).astype(bf16)
    scaled = (quant.astype(f32) * power_two(channel_shift_power, -1)[None, :]).astype(bf16)

    chan_count, sub_count = lax.axis_size("chan"), lax.axis_size("sub")
    rows = tokens // (chan_count * sub_count)
    order = sorted(range(1, seq_count), key=lambda k: -min(k, seq_count - k))
    blocks = {0: scaled}
    for k in order:
        blocks[k] = turn(scaled, "seq", k)
    sums = []
    for k in [0] + order:
        partial = dot(blocks[k], out_weight).astype(bf16)
        partial = partial.reshape(chan_count, sub_count, rows, -1)
        partial = halve(jnp.swapaxes(partial, 0, 1), "sub")
        done = halve(partial, "chan")
        sums.append((k, turn(done, "seq", -k % seq_count) if k else done))
    pieces = [value for _, value in sorted(sums, key=lambda item: item[0])]
    stacked = jnp.stack(pieces + pieces, axis=0)
    here = lax.axis_index("seq")
    placed = lax.dynamic_slice_in_dim(
        stacked, (seq_count - here) % seq_count, seq_count, 0
    )
    return jnp.swapaxes(placed, 0, 1).reshape(rows, -1)


def solution(mesh):
    return jax.shard_map(
        body,
        mesh=mesh,
        in_specs=(
            P(("groups", "seq"), ("chan", "sub")),
            P(("groups", "seq"), "chan", None),
            P(("groups", "seq"), "chan", None),
            P(("groups", "seq"), ("chan", "sub")),
            P(("groups", "seq"), ("chan", "sub")),
            P(("chan", "sub")),
            P(("groups", "seq"), ("chan", "sub")),
            P(("chan", "sub")),
            P(("chan", "sub")),
            P(("chan", "sub")),
            P(("chan", "sub"), "seq"),
        ),
        out_specs=P(("groups", "seq", "chan", "sub"), None),
        check_vma=False,
    )
```

```python
import functools
import math

import jax
import jax.numpy as jnp
import numpy as np
from jax import lax
from jax.experimental import pallas as pl
from jax.experimental.pallas import tpu as pltpu
from jax.sharding import PartitionSpec as P

LOCAL_HEADS = 128
P_SIZE = 64
G = 4
NORM_HEADS = 16


norm_eps = 1e-05
clip_level = 4.0
expo_levels = (-1, 0, 1, 2, 3)
LANES = 128
H_BLOCK = 256
COST = pl.CostEstimate(flops=1, transcendentals=0, bytes_accessed=30_000_000)
SMALL = pl.CostEstimate(flops=1, transcendentals=0, bytes_accessed=1)
f32 = jnp.float32
bf16 = jnp.bfloat16
PARAMS = pltpu.CompilerParams(vmem_limit_bytes=16 * 2**20)
WIDE_PARAMS = pltpu.CompilerParams(vmem_limit_bytes=16 * 2**20)


def power_two(expo, sign_flip):
    result = jnp.zeros(expo.shape, jnp.float32)
    for level in expo_levels:
        result = result + jnp.where(
            expo == level, jnp.float32(2.0 ** (sign_flip * level)), jnp.float32(0.0)
        )
    return result


def dot(a, b):
    return jnp.dot(a, b, preferred_element_type=f32)


def dot_nt(a, b):
    return lax.dot_general(a, b, (((1,), (1,)), ((), ())), preferred_element_type=f32)


def parts_of(value, count):
    terms = []
    for _ in range(count):
        term = value.astype(bf16)
        terms.append(term)
        value = value - term.astype(f32)
    return terms


def exact_dot(exact, value, count=3):
    return sum(dot(exact, term) for term in parts_of(value, count))


def spread(value, expand, count=2):
    return sum(dot(term, expand) for term in parts_of(value, count))


def causal_mask(size):
    row = lax.broadcasted_iota(jnp.int32, (size, size), 0)
    col = lax.broadcasted_iota(jnp.int32, (size, size), 1)
    return row >= col


def message_kernel(x_ref, b_ref, step_ref, decay_ref, expand_ref, msg_ref, cumul_ref):
    tokens, width = x_ref.shape
    heads = step_ref.shape[1]
    states = b_ref.shape[1]
    expand = expand_ref[...]
    triangle = causal_mask(tokens).astype(f32).astype(bf16)
    cumul = exact_dot(triangle, decay_ref[...])
    cumul_ref[...] = cumul
    total = cumul[tokens - 1 : tokens, :]
    scale = spread(jnp.exp(total - cumul) * step_ref[...], expand)
    msg_ref[:, :width] = (x_ref[...].astype(f32) * scale).astype(bf16)
    msg_ref[:, width : width + states] = b_ref[...]
    high, low = parts_of(jnp.exp(total), 2)
    base = width + states
    msg_ref[:, base:] = jnp.zeros((tokens, msg_ref.shape[1] - base), bf16)
    msg_ref[:, base : base + heads] = jnp.broadcast_to(high, (tokens, heads))
    msg_ref[:, base + heads : base + 2 * heads] = jnp.broadcast_to(low, (tokens, heads))


def local_kernel(
    x_ref, b_ref, c_ref, step_ref, cumul_ref, gate_ref, skip_ref, expand_ref, own_ref, far_ref
):
    tokens, width = x_ref.shape
    heads = step_ref.shape[1]
    causal = causal_mask(tokens)
    inner = dot_nt(c_ref[...], b_ref[...])
    cumul = cumul_ref[...]
    cumul_t = cumul.T
    step_t = step_ref[...].T
    first = lax.broadcasted_iota(jnp.int32, (tokens, 2 * P_SIZE), 1) < P_SIZE
    for pair in range(heads // 2):
        mixings = []
        for head in (2 * pair, 2 * pair + 1):
            differ = cumul[:, head : head + 1] - cumul_t[head : head + 1, :]
            ratio = jnp.exp(jnp.where(causal, differ, -jnp.inf))
            mixings.append((ratio * (inner * step_t[head : head + 1, :])).astype(bf16))
        at = slice(pair * 2 * P_SIZE, (pair + 1) * 2 * P_SIZE)
        x_pair = x_ref[:, at]
        zero = jnp.zeros_like(x_pair)
        blocks = jnp.concatenate(
            [jnp.where(first, x_pair, zero), jnp.where(first, zero, x_pair)], axis=0
        )
        own = dot(jnp.concatenate(mixings, axis=1), blocks)
        own = own + x_pair.astype(f32) * skip_ref[:, at]
        gate = gate_ref[:, at].astype(f32)
        own_ref[:, at] = own * (gate / (1.0 + jnp.exp(-gate)))
    reach = jnp.exp(cumul)
    tile = min(width, 512)
    for start in range(0, width, tile):
        at = slice(start, start + tile)
        gate = gate_ref[:, at].astype(f32)
        far_ref[:, at] = spread(reach, expand_ref[:, at]) * (gate / (1.0 + jnp.exp(-gate)))


def mix_kernel(count, *refs):
    messages = refs[:count]
    c_ref, own_ref, far_ref, gain_ref, table_ref, expand_ref, out_ref = refs[count:]
    tokens, width = own_ref.shape
    states = c_ref.shape[1]
    heads = expand_ref.shape[0]
    base = width + states
    c_group = c_ref[...]
    inners = []
    decays = []
    for msg_ref in messages:
        inners.append(dot_nt(c_group, msg_ref[:, width:base]).astype(bf16))
        decay = dot(msg_ref[:16, base : base + heads], expand_ref[...]) + dot(
            msg_ref[:16, base + heads : base + 2 * heads], expand_ref[...]
        )
        decays.append(decay[:1, :])
    norm_width = NORM_HEADS * P_SIZE
    table = table_ref[...]
    parts = []
    for start in range(0, width, norm_width):
        pres = []
        square = jnp.zeros((tokens, 1), f32)
        for begin in range(start, start + norm_width, H_BLOCK):
            at = slice(begin, begin + H_BLOCK)
            carried = None
            for k in reversed(range(count)):
                term = dot(inners[k], messages[k][:, at])
                carried = term if carried is None else term + decays[k][:, at] * carried
            pre = own_ref[:, at]
            if carried is not None:
                pre = pre + far_ref[:, at] * carried
            square = square + jnp.sum(pre * pre, axis=1, keepdims=True)
            pres.append(pre)
        inverse = lax.rsqrt(square * (1.0 / norm_width) + norm_eps)
        for index, pre in enumerate(pres):
            at = slice(start + index * H_BLOCK, start + (index + 1) * H_BLOCK)
            signed = (pre * inverse * gain_ref[:, at]).astype(bf16)
            parts.append(dot(signed, table))
    butterflies(parts)
    for index, part in enumerate(parts):
        out_ref[:, index * H_BLOCK : (index + 1) * H_BLOCK] = part.astype(bf16)


def half_at(which, size):
    return pl.ds(pl.multiple_of(which * size, size), size)


def start_all(copies):
    for copy in copies:
        copy.start()
    return copies


def wait_all(copies):
    for copy in copies:
        copy.wait()


def block_rows(index, size):
    return slice(index * size, (index + 1) * size)


def pack_kernel(
    where_ref,
    x_mine_ref,
    x_other_ref,
    b_ref,
    c_ref,
    step_ref,
    decay_ref,
    mine_ref,
    other_ref,
    straight_ref,
    cross_ref,
):
    tokens, states = b_ref.shape
    half = x_mine_ref.shape[1]
    heads = step_ref.shape[0] // 2
    member = where_ref[0]
    triangle = causal_mask(tokens).astype(f32).astype(bf16)
    step = step_ref[...].T
    decay = decay_ref[...].T
    cumul = exact_dot(triangle, decay)
    total = cumul[tokens - 1 : tokens, :]
    scale = jnp.exp(total - cumul) * step
    kept = jnp.exp(total)

    def pick(value, which):
        return jnp.where(which == 0, value[:, :heads], value[:, heads:])

    other_ref[:, :half] = x_other_ref[...]
    for out_ref, base, which in ((mine_ref, 0, member), (other_ref, half, 1 - member)):
        out_ref[:, base : base + states] = b_ref[...]
        out_ref[:, base + states : base + 2 * states] = c_ref[...]
        base += 2 * states
        out_ref[:, base:] = jnp.zeros((tokens, out_ref.shape[1] - base), bf16)
        terms = parts_of(pick(step, which), 3) + parts_of(pick(decay, which), 3)
        for index, term in enumerate(terms):
            out_ref[:, base + index * heads : base + (index + 1) * heads] = term
    expand = expansion(heads)
    for out_ref, x_ref, which in (
        (straight_ref, x_mine_ref, member),
        (cross_ref, x_other_ref, 1 - member),
    ):
        wide = spread(pick(scale, which), expand)
        weighted = (x_ref[...].astype(f32) * wide).astype(bf16)
        for index in range(half // LANES):
            out_ref[block_rows(index, tokens), :] = weighted[:, block_rows(index, LANES)]
        for index in range(states // LANES):
            out_ref[block_rows(half // LANES + index, tokens), :] = b_ref[
                :, block_rows(index, LANES)
            ]
        base = (half + states) // LANES * tokens
        rows = out_ref.shape[0] - base
        out_ref[base:, :] = jnp.zeros((rows, LANES), bf16)
        for index, term in enumerate(parts_of(pick(kept, which), 2)):
            out_ref[base:, block_rows(index, heads)] = jnp.broadcast_to(term, (rows, heads))


def expansion(heads):
    shape = (heads, heads * P_SIZE)
    row = lax.broadcasted_iota(jnp.int32, shape, 0)
    col = lax.broadcasted_iota(jnp.int32, shape, 1)
    return ((col >= row * P_SIZE) & (col < (row + 1) * P_SIZE)).astype(f32).astype(bf16)


def pair_kernel(
    where_ref,
    x_ref,
    meta_ref,
    msg_ref,
    skip_ref,
    own_ref,
    far_ref,
    c_pair_ref,
    x_both,
    b_both,
    step_both,
    decay_both,
):
    tokens, half = x_ref.shape
    states = c_pair_ref.shape[1]
    heads = half // P_SIZE
    member = where_ref[0]
    for which, x, meta in (
        (member, x_ref, meta_ref),
        (1 - member, msg_ref.at[:, :half], msg_ref.at[:, half:]),
    ):
        rows = half_at(which, tokens)
        x_both[rows, :] = x[...]
        b_both[rows, :] = meta[:, :states]
        c_pair_ref[rows, :] = meta[:, states : 2 * states]
        for index, both in enumerate((step_both, decay_both)):
            base = 2 * states + 3 * index * heads
            terms = [
                meta[:, base + term * heads : base + (term + 1) * heads].astype(f32)
                for term in range(3)
            ]
            both[rows, :] = (terms[2] + terms[1]) + terms[0]

    span = 2 * tokens
    causal = causal_mask(span)
    inner = jnp.where(causal, dot_nt(c_pair_ref[...], b_both[...]), 0.0)
    cumul = exact_dot(causal.astype(f32).astype(bf16), decay_both[...])
    cumul_t = cumul.T
    step_t = step_both[...].T
    skip = skip_ref[:, half_at(member, half)]
    expand = expansion(heads)
    reach = parts_of(jnp.exp(cumul), 2)
    first = lax.broadcasted_iota(jnp.int32, (tokens, 2 * P_SIZE), 1) < P_SIZE
    for pair in range(heads // 2):
        at = slice(pair * 2 * P_SIZE, (pair + 1) * 2 * P_SIZE)
        spans = []
        for block in range(2):
            x_block = x_both[block * tokens : (block + 1) * tokens, at]
            zero = jnp.zeros_like(x_block)
            spans.append((jnp.where(first, x_block, zero), jnp.where(first, zero, x_block)))
        for block in range(2):
            rows = slice(block * tokens, (block + 1) * tokens)
            mixings, values = [], []
            for place, head in enumerate((2 * pair, 2 * pair + 1)):
                for earlier in range(block + 1):
                    cols = slice(earlier * tokens, (earlier + 1) * tokens)
                    differ = cumul[rows, head : head + 1] - cumul_t[head : head + 1, cols]
                    if earlier == block:
                        differ = jnp.where(causal[:tokens, :tokens], differ, 0.0)
                    ratio = jnp.exp(differ)
                    mixings.append(
                        (ratio * (inner[rows, cols] * step_t[head : head + 1, cols])).astype(bf16)
                    )
                    values.append(spans[earlier][place])
            own = dot(jnp.concatenate(mixings, axis=1), jnp.concatenate(values, axis=0))
            own_ref[rows, at] = own + x_both[rows, at].astype(f32) * skip[:, at]
            far_ref[rows, at] = sum(dot(term[rows, :], expand[:, at]) for term in reach)


def gate_mix_kernel(count, pieces, *refs):
    sent = refs[: 2 * count]
    where_ref, gate_ref, gate_pair_ref, c_ref, own_ref, far_ref, gain_ref, table_ref = refs[
        2 * count : -3
    ]
    out_refs, gate_both = refs[-3:-1], refs[-1]
    span, half = own_ref.shape
    tokens = span // 2
    states = c_ref.shape[1]
    heads = half // P_SIZE
    member = where_ref[0]
    c_pair = c_ref[...]
    expand = expansion(heads)

    for which, gate in ((member, gate_ref), (1 - member, gate_pair_ref)):
        gate_both[half_at(which, tokens), :] = gate[...]

    def columns(ref, start, size):
        blocks = range(start // LANES, (start + size) // LANES)
        return jnp.concatenate([ref[block_rows(index, tokens), :] for index in blocks], axis=1)

    def kept(ref):
        base = (half + states) // LANES * tokens
        high, low = (ref[base:, block_rows(index, heads)] for index in range(2))
        return (dot(high, expand) + dot(low, expand))[:1, :]

    inners = [dot_nt(c_pair, columns(ref, half, states)).astype(bf16) for ref in sent]
    factors, pair_kept = [], []
    for k in range(count):
        one, two = kept(sent[2 * k]), kept(sent[2 * k + 1])
        pair_kept.append(one * two)
        factors += [jnp.where(member == 0, two, 1.0), jnp.where(member == 0, 1.0, one)]
    gain = gain_ref[:, half_at(member, half)]
    table = table_ref[...]
    parts = []
    norm_width = NORM_HEADS * P_SIZE
    for start in range(0, half, norm_width):
        pres = []
        square = jnp.zeros((span, 1), f32)
        for begin in range(start, start + norm_width, H_BLOCK):
            at = slice(begin, begin + H_BLOCK)
            pre = own_ref[:, at]
            carried = None
            for k in reversed(range(count)):
                term = 0.0
                for j in (2 * k, 2 * k + 1):
                    term = term + factors[j][:, at] * dot(
                        inners[j], columns(sent[j], begin, H_BLOCK)
                    )
                carried = term if carried is None else term + pair_kept[k][:, at] * carried
            if carried is not None:
                pre = pre + far_ref[:, at] * carried
            gate = gate_both[:, at].astype(f32)
            pre = pre * (gate / (1.0 + jnp.exp(-gate)))
            square = square + jnp.sum(pre * pre, axis=1, keepdims=True)
            pres.append(pre)
        inverse = lax.rsqrt(square * (1.0 / norm_width) + norm_eps)
        for index, pre in enumerate(pres):
            at = slice(start + index * H_BLOCK, start + (index + 1) * H_BLOCK)
            parts.append(dot((pre * inverse * gain[:, at]).astype(bf16), table))
    butterflies(parts)
    size = span // pieces
    for index, part in enumerate(parts):
        at = slice(index * H_BLOCK, (index + 1) * H_BLOCK)
        part = part.astype(bf16)
        for piece in range(pieces):
            to = slice(piece // 2 * size, (piece // 2 + 1) * size)
            out_refs[piece % 2][to, at] = part[piece * size : (piece + 1) * size, :]


def butterflies(parts):
    span = 1
    while span < len(parts):
        for low in range(len(parts)):
            if low & span == 0:
                a, b = parts[low], parts[low + span]
                parts[low], parts[low + span] = a + b, a - b
        span *= 2


def add_kernel(sign_ref, mixed_ref, received_ref, out_ref):
    sign = sign_ref[0].astype(f32)
    out_ref[...] = (mixed_ref[...].astype(f32) * sign + received_ref[...].astype(f32)).astype(bf16)


def project_kernel(pairs, where_ref, weight_ref, *refs):
    pieces = refs[: 2 * pairs]
    up_ref, down_ref, out_ref, weight_own, sums, sems = refs[2 * pairs :]
    rows, half = pieces[0].shape
    sign = (1 - 2 * where_ref[0]).astype(f32)
    sub_count, chan_count, _, blocks, size, features = out_ref.shape
    tile = half // 2
    copies = start_all(
        [
            pltpu.make_async_copy(
                weight_ref.at[start : start + tile, :],
                weight_own.at[start : start + tile, :],
                sems.at[start // tile],
            )
            for start in range(0, 2 * half, tile)
        ]
    )
    for step, copy in enumerate(copies):
        at = slice(step * tile, (step + 1) * tile)
        inner = slice(step * tile % half, step * tile % half + tile)
        scaled = []
        for pair in range(pairs):
            one = pieces[2 * pair][:, inner].astype(f32)
            two = pieces[2 * pair + 1][:, inner].astype(f32)
            mixed = (one - two) * sign if step * tile >= half else one + two
            quant = jnp.clip(mixed * up_ref[:, at], -clip_level, clip_level).astype(bf16)
            scaled.append((quant.astype(f32) * down_ref[:, at]).astype(bf16))
        copy.wait()
        term = dot(jnp.concatenate(scaled, axis=0), weight_own[at, :])
        if step == 0:
            sums[...] = term
        elif step < len(copies) - 1:
            sums[...] += term
        else:
            total = (sums[...] + term).astype(bf16)
    row = 0
    for pair in range(pairs):
        for block in range(blocks):
            for chan in range(chan_count):
                for sub in range(sub_count):
                    out_ref[sub, chan, pair, block] = total[row : row + size, :]
                    row += size


def place_kernel(where_ref, *refs):
    out_ref = refs[-1]
    features = refs[0].shape[1]
    for distance, ref in enumerate(refs[:-1]):
        out_ref[:, half_at(where_ref[0] ^ distance, features)] = ref[...]


def sylvester(order):
    table = np.ones((1, 1), np.float32)
    while table.shape[0] < order:
        table = np.block([[table, table], [table, -table]])
    return table


def shift_up(value, axis, distance):
    count = lax.axis_size(axis)
    return lax.ppermute(value, axis, [(k, k + distance) for k in range(count - distance)])


def turn(value, axis, distance):
    count = lax.axis_size(axis)
    return lax.ppermute(value, axis, [(k, (k + distance) % count) for k in range(count)])


def swap(value, axis, bit):
    count = lax.axis_size(axis)
    return lax.ppermute(value, axis, [(k, k ^ (1 << bit)) for k in range(count)])


def bits_of(axis):
    return range(lax.axis_size(axis).bit_length() - 1)


def halve(value, axis):
    here = lax.axis_index(axis)
    for bit in reversed(bits_of(axis)):
        pair = value.reshape((2, value.shape[0] // 2) + value.shape[1:])
        mine = here // 2**bit % 2
        keep = lax.dynamic_index_in_dim(pair, mine, 0, keepdims=False)
        give = lax.dynamic_index_in_dim(pair, 1 - mine, 0, keepdims=False)
        value = (keep.astype(f32) + swap(give, axis, bit).astype(f32)).astype(bf16)
    return value[0]


def call(kernel, out_shape, name, args, scalars=0, anywhere=0, scratch=(), params=PARAMS, cost=COST):
    specs = [pl.BlockSpec(memory_space=pltpu.SMEM)] * scalars
    specs += [pl.BlockSpec(memory_space=pltpu.HBM)] * anywhere
    specs += [pl.BlockSpec(memory_space=pltpu.VMEM)] * (len(args) - scalars - anywhere)
    return pl.pallas_call(
        kernel,
        out_shape=out_shape,
        in_specs=specs,
        scratch_shapes=scratch,
        compiler_params=params,
        cost_estimate=cost,
        name=name,
    )(*args)


def swap_seq(value, distance):
    count = lax.axis_size("seq")
    return lax.ppermute(value, "seq", [(k, k ^ distance) for k in range(count)])


def paired_body(
    x_in,
    b_in,
    c_in,
    step_size,
    log_decay,
    skip,
    gate_in,
    norm_gain,
    walsh_sign,
    channel_shift_power,
    out_weight,
):
    tokens, width = x_in.shape
    heads = step_size.shape[1]
    states = b_in.shape[2]
    half, half_heads = width // 2, heads // 2
    seq_count, chan_count, sub_count = (lax.axis_size(a) for a in ("seq", "chan", "sub"))
    pairs = seq_count // 2
    here = lax.axis_index("seq")
    member = here % 2
    group_local = lax.axis_index("sub") * heads // (LOCAL_HEADS // G)
    where = jnp.full((1,), member, jnp.int32)
    b_group = lax.dynamic_index_in_dim(b_in, group_local, 1, keepdims=False)
    c_group = lax.dynamic_index_in_dim(c_in, group_local, 1, keepdims=False)
    table = jnp.asarray(sylvester(H_BLOCK), bf16)

    def shape(rows, columns, kind):
        return jax.ShapeDtypeStruct((rows, columns), kind)

    def padded(columns):
        return pl.cdiv(columns, LANES) * LANES

    def half_of(value, which):
        return lax.dynamic_slice_in_dim(value, which * half, half, 1)

    x_mine, x_other = half_of(x_in, member), half_of(x_in, 1 - member)
    gate_mine, gate_other = half_of(gate_in, member), half_of(gate_in, 1 - member)
    with_pair = shape(tokens, 2 * states + padded(6 * half_heads), bf16)
    with_later = shape((half + states) // LANES * tokens + 16, LANES, bf16)
    meta_mine, to_pair, straight, cross = call(
        pack_kernel,
        (with_pair, shape(tokens, half + with_pair.shape[1], bf16), with_later, with_later),
        "pack",
        (where, x_mine, x_other, b_group, c_group, step_size.T, log_decay.T),
        1,
    )
    sent = []
    for ahead in range(1, pairs):
        firsts = range(seq_count - 2 * ahead)
        sent.append(lax.ppermute(straight, "seq", [(k, k + 2 * ahead) for k in firsts]))
        sent.append(lax.ppermute(cross, "seq", [(k, (k ^ 1) + 2 * ahead) for k in firsts]))
    from_pair, gate_pair = swap_seq(to_pair, 1), swap_seq(gate_other, 1)

    span = 2 * tokens
    own, far, c_pair = call(
        pair_kernel,
        (
            shape(span, half, f32),
            shape(span, half, f32),
            shape(span, states, bf16),
        ),
        "pair",
        (
            where,
            x_mine,
            meta_mine,
            from_pair,
            jnp.repeat(skip, P_SIZE)[None, :],
        ),
        1,
        0,
        (
            pltpu.VMEM((span, half), bf16),
            pltpu.VMEM((span, states), bf16),
            pltpu.VMEM((span, half_heads), f32),
            pltpu.VMEM((span, half_heads), f32),
        ),
        cost=SMALL,
    )
    signed_gain = (jnp.where(walsh_sign == 1, 1.0, -1.0) * norm_gain)[None, :]
    owners = chan_count * sub_count
    size = tokens // (2 * owners)
    count = len(sent) // 2
    chunks = pl.pallas_call(
        functools.partial(gate_mix_kernel, count, span // size),
        out_shape=(shape(tokens, half, bf16),) * 2,
        in_specs=[pl.BlockSpec(memory_space=pltpu.VMEM)] * (2 * count)
        + [pl.BlockSpec(memory_space=pltpu.SMEM)]
        + [pl.BlockSpec(memory_space=pltpu.VMEM)] * 7,
        scratch_shapes=[pltpu.VMEM((span, half), bf16)],
        compiler_params=PARAMS,
        cost_estimate=COST,
        name="mix",
    )(*sent, where, gate_mine, gate_pair, c_pair, own, far, signed_gain, table)

    def add_across(mixed, axis, bit, received):
        place = lax.axis_index(axis)
        sign = 1.0 - 2.0 * (place // 2**bit % 2).astype(f32)
        return (mixed.astype(f32) * sign + received.astype(f32)).astype(bf16)

    def across(mixed, axis):
        for bit in bits_of(axis):
            mixed = add_across(mixed, axis, bit, swap(mixed, axis, bit))
        return mixed

    first, second = (across(chunk, "sub") for chunk in chunks)
    first = across(first, "chan")
    first, second = lax.optimization_barrier((first, second))
    bits = bits_of("chan")
    for bit in bits[:-1]:
        second = add_across(second, "chan", bit, swap(second, "chan", bit))
    received = swap(second, "chan", bits[-1]) if bits else None
    ahead = range(1, pairs)
    far_first = [swap_seq(first, 2 * k) for k in ahead]
    near_first = swap_seq(first, 1)
    first, second, received, far_first, near_first = lax.optimization_barrier(
        (first, second, received, far_first, near_first)
    )
    if bits:
        sign = 1 - 2 * (lax.axis_index("chan") // 2 ** bits[-1] % 2)
        second = call(
            add_kernel,
            shape(tokens, half, bf16),
            "add",
            (jnp.full((1,), sign, jnp.int32), second, received),
            1,
        )
    passed_first = [swap_seq(value, 1) for value in far_first]
    all_first = [first, near_first]
    for far, passed in zip(far_first, passed_first):
        all_first += [far, passed]
    second_late = lax.optimization_barrier((second, passed_first))[0] if pairs > 1 else second
    all_second = [second, swap_seq(second_late, 1)]
    all_second += [swap_seq(second, k) for k in range(2, seq_count)]

    up = (power_two(channel_shift_power, 1) * (1.0 / math.sqrt(LOCAL_HEADS * P_SIZE)))[None, :]
    down = power_two(channel_shift_power, -1)[None, :]
    features = out_weight.shape[1]

    def project(pieces):
        return call(
            functools.partial(project_kernel, pairs),
            jax.ShapeDtypeStruct((sub_count, chan_count, pairs, 2, size, features), bf16),
            "project",
            (where, out_weight, *pieces, up, down),
            1,
            1,
            (
                pltpu.VMEM(out_weight.shape, bf16),
                pltpu.VMEM((pairs * tokens, features), f32),
                pltpu.SemaphoreType.DMA((4,)),
            ),
            WIDE_PARAMS,
        )

    def reduce(partial):
        return halve(halve(partial, "sub"), "chan")

    done = lax.optimization_barrier(jnp.bool_(True))
    done_first = lax.cond(
        done,
        lambda *pieces: reduce(project(pieces)),
        lambda *pieces: jnp.zeros((pairs, 2, size, features), bf16),
        *all_first,
    )
    done_first, all_second = lax.optimization_barrier((done_first, all_second))
    done_second = reduce(project(all_second))
    summed = jnp.stack([done_first, done_second], axis=2)
    returned = []
    for distance in range(seq_count):
        block = (member + distance) % 2
        value = lax.dynamic_index_in_dim(summed[distance // 2], block, 0, keepdims=False)
        value = value.reshape(2 * size, features)
        returned.append(swap_seq(value, distance) if distance else value)
    return call(
        place_kernel,
        shape(2 * size, seq_count * features, bf16),
        "place",
        (jnp.full((1,), here, jnp.int32), *returned),
        1,
    )


def body(x_in, b_in, c_in, step_size, *rest):
    tokens, heads = step_size.shape
    seq_count = lax.axis_size("seq")
    pieces = 2 * lax.axis_size("chan") * lax.axis_size("sub")
    if (
        heads % (2 * NORM_HEADS) == 0
        and seq_count % 2 == 0
        and seq_count & (seq_count - 1) == 0
        and tokens % (16 * pieces) == 0
    ):
        return paired_body(x_in, b_in, c_in, step_size, *rest)
    return plain_body(x_in, b_in, c_in, step_size, *rest)


def plain_body(
    x_in,
    b_in,
    c_in,
    step_size,
    log_decay,
    skip,
    gate_in,
    norm_gain,
    walsh_sign,
    channel_shift_power,
    out_weight,
):
    tokens, width = x_in.shape
    heads = step_size.shape[1]
    states = b_in.shape[2]
    seq_count = lax.axis_size("seq")
    sub_index = lax.axis_index("sub")
    group_local = sub_index * heads // (LOCAL_HEADS // G)
    b_group = lax.dynamic_slice_in_dim(b_in, group_local, 1, 1)[:, 0, :]
    c_group = lax.dynamic_slice_in_dim(c_in, group_local, 1, 1)[:, 0, :]
    expand = jnp.asarray(np.kron(np.eye(heads), np.ones((1, P_SIZE))), bf16)
    table = jnp.asarray(sylvester(H_BLOCK), bf16)

    tail = pl.cdiv(2 * heads, LANES) * LANES
    message, cumul = pl.pallas_call(
        message_kernel,
        out_shape=(
            jax.ShapeDtypeStruct((tokens, width + states + tail), bf16),
            jax.ShapeDtypeStruct((tokens, heads), f32),
        ),
        compiler_params=PARAMS,
        name="message",
    )(x_in, b_group, step_size, log_decay, expand)
    arrived = [shift_up(message, "seq", k) for k in range(1, seq_count)]

    wide_skip = jnp.repeat(skip, P_SIZE)[None, :]
    own, far = pl.pallas_call(
        local_kernel,
        out_shape=(
            jax.ShapeDtypeStruct((tokens, width), f32),
            jax.ShapeDtypeStruct((tokens, width), f32),
        ),
        compiler_params=PARAMS,
        name="local",
    )(x_in, b_group, c_group, step_size, cumul, gate_in, wide_skip, expand)

    signed_gain = (jnp.where(walsh_sign == 1, 1.0, -1.0) * norm_gain)[None, :]
    mixed = pl.pallas_call(
        functools.partial(mix_kernel, len(arrived)),
        out_shape=jax.ShapeDtypeStruct((tokens, width), bf16),
        compiler_params=PARAMS,
        name="mix",
    )(*arrived, c_group, own, far, signed_gain, table, expand)

    for axis in ("sub", "chan"):
        here = lax.axis_index(axis)
        for bit in bits_of(axis):
            other = swap(mixed.astype(bf16), axis, bit).astype(f32)
            sign = 1.0 - 2.0 * (here // 2**bit % 2).astype(f32)
            mixed = mixed.astype(f32) * sign + other
    rotated = mixed * (1.0 / math.sqrt(LOCAL_HEADS * P_SIZE))
    quant = jnp.clip(
        rotated * power_two(channel_shift_power, 1)[None, :], -clip_level, clip_level
    ).astype(bf16)
    scaled = (quant.astype(f32) * power_two(channel_shift_power, -1)[None, :]).astype(bf16)

    chan_count, sub_count = lax.axis_size("chan"), lax.axis_size("sub")
    rows = tokens // (chan_count * sub_count)
    order = sorted(range(1, seq_count), key=lambda k: -min(k, seq_count - k))
    blocks = {0: scaled}
    for k in order:
        blocks[k] = turn(scaled, "seq", k)
    sums = []
    for k in [0] + order:
        partial = dot(blocks[k], out_weight).astype(bf16)
        partial = partial.reshape(chan_count, sub_count, rows, -1)
        partial = halve(jnp.swapaxes(partial, 0, 1), "sub")
        done = halve(partial, "chan")
        sums.append((k, turn(done, "seq", -k % seq_count) if k else done))
    pieces = [value for _, value in sorted(sums, key=lambda item: item[0])]
    stacked = jnp.stack(pieces + pieces, axis=0)
    here = lax.axis_index("seq")
    placed = lax.dynamic_slice_in_dim(
        stacked, (seq_count - here) % seq_count, seq_count, 0
    )
    return jnp.swapaxes(placed, 0, 1).reshape(rows, -1)


def solution(mesh):
    return jax.shard_map(
        body,
        mesh=mesh,
        in_specs=(
            P(("groups", "seq"), ("chan", "sub")),
            P(("groups", "seq"), "chan", None),
            P(("groups", "seq"), "chan", None),
            P(("groups", "seq"), ("chan", "sub")),
            P(("groups", "seq"), ("chan", "sub")),
            P(("chan", "sub")),
            P(("groups", "seq"), ("chan", "sub")),
            P(("chan", "sub")),
            P(("chan", "sub")),
            P(("chan", "sub")),
            P(("chan", "sub"), "seq"),
        ),
        out_specs=P(("groups", "seq", "chan", "sub"), None),
        check_vma=False,
    )
```

```python
import functools
import math

import jax
import jax.numpy as jnp
import numpy as np
from jax import lax
from jax.experimental import pallas as pl
from jax.experimental.pallas import tpu as pltpu
from jax.sharding import PartitionSpec as P

LOCAL_HEADS = 128
P_SIZE = 64
G = 4
NORM_HEADS = 16


norm_eps = 1e-05
clip_level = 4.0
expo_levels = (-1, 0, 1, 2, 3)
LANES = 128
H_BLOCK = 256
COST = pl.CostEstimate(flops=1, transcendentals=0, bytes_accessed=30_000_000)
SMALL = pl.CostEstimate(flops=1, transcendentals=0, bytes_accessed=1)
f32 = jnp.float32
bf16 = jnp.bfloat16
PARAMS = pltpu.CompilerParams(vmem_limit_bytes=16 * 2**20)
WIDE_PARAMS = pltpu.CompilerParams(vmem_limit_bytes=16 * 2**20)


def power_two(expo, sign_flip):
    result = jnp.zeros(expo.shape, jnp.float32)
    for level in expo_levels:
        result = result + jnp.where(
            expo == level, jnp.float32(2.0 ** (sign_flip * level)), jnp.float32(0.0)
        )
    return result


def dot(a, b):
    return jnp.dot(a, b, preferred_element_type=f32)


def dot_nt(a, b):
    return lax.dot_general(a, b, (((1,), (1,)), ((), ())), preferred_element_type=f32)


def parts_of(value, count):
    terms = []
    for _ in range(count):
        term = value.astype(bf16)
        terms.append(term)
        value = value - term.astype(f32)
    return terms


def exact_dot(exact, value, count=3):
    return sum(dot(exact, term) for term in parts_of(value, count))


def spread(value, expand, count=2):
    return sum(dot(term, expand) for term in parts_of(value, count))


def causal_mask(size):
    row = lax.broadcasted_iota(jnp.int32, (size, size), 0)
    col = lax.broadcasted_iota(jnp.int32, (size, size), 1)
    return row >= col


def message_kernel(x_ref, b_ref, step_ref, decay_ref, expand_ref, msg_ref, cumul_ref):
    tokens, width = x_ref.shape
    heads = step_ref.shape[1]
    states = b_ref.shape[1]
    expand = expand_ref[...]
    triangle = causal_mask(tokens).astype(f32).astype(bf16)
    cumul = exact_dot(triangle, decay_ref[...])
    cumul_ref[...] = cumul
    total = cumul[tokens - 1 : tokens, :]
    scale = spread(jnp.exp(total - cumul) * step_ref[...], expand)
    msg_ref[:, :width] = (x_ref[...].astype(f32) * scale).astype(bf16)
    msg_ref[:, width : width + states] = b_ref[...]
    high, low = parts_of(jnp.exp(total), 2)
    base = width + states
    msg_ref[:, base:] = jnp.zeros((tokens, msg_ref.shape[1] - base), bf16)
    msg_ref[:, base : base + heads] = jnp.broadcast_to(high, (tokens, heads))
    msg_ref[:, base + heads : base + 2 * heads] = jnp.broadcast_to(low, (tokens, heads))


def local_kernel(
    x_ref, b_ref, c_ref, step_ref, cumul_ref, gate_ref, skip_ref, expand_ref, own_ref, far_ref
):
    tokens, width = x_ref.shape
    heads = step_ref.shape[1]
    causal = causal_mask(tokens)
    inner = dot_nt(c_ref[...], b_ref[...])
    cumul = cumul_ref[...]
    cumul_t = cumul.T
    step_t = step_ref[...].T
    first = lax.broadcasted_iota(jnp.int32, (tokens, 2 * P_SIZE), 1) < P_SIZE
    for pair in range(heads // 2):
        mixings = []
        for head in (2 * pair, 2 * pair + 1):
            differ = cumul[:, head : head + 1] - cumul_t[head : head + 1, :]
            ratio = jnp.exp(jnp.where(causal, differ, -jnp.inf))
            mixings.append((ratio * (inner * step_t[head : head + 1, :])).astype(bf16))
        at = slice(pair * 2 * P_SIZE, (pair + 1) * 2 * P_SIZE)
        x_pair = x_ref[:, at]
        zero = jnp.zeros_like(x_pair)
        blocks = jnp.concatenate(
            [jnp.where(first, x_pair, zero), jnp.where(first, zero, x_pair)], axis=0
        )
        own = dot(jnp.concatenate(mixings, axis=1), blocks)
        own = own + x_pair.astype(f32) * skip_ref[:, at]
        gate = gate_ref[:, at].astype(f32)
        own_ref[:, at] = own * (gate / (1.0 + jnp.exp(-gate)))
    reach = jnp.exp(cumul)
    tile = min(width, 512)
    for start in range(0, width, tile):
        at = slice(start, start + tile)
        gate = gate_ref[:, at].astype(f32)
        far_ref[:, at] = spread(reach, expand_ref[:, at]) * (gate / (1.0 + jnp.exp(-gate)))


def mix_kernel(count, *refs):
    messages = refs[:count]
    c_ref, own_ref, far_ref, gain_ref, table_ref, expand_ref, out_ref = refs[count:]
    tokens, width = own_ref.shape
    states = c_ref.shape[1]
    heads = expand_ref.shape[0]
    base = width + states
    c_group = c_ref[...]
    inners = []
    decays = []
    for msg_ref in messages:
        inners.append(dot_nt(c_group, msg_ref[:, width:base]).astype(bf16))
        decay = dot(msg_ref[:16, base : base + heads], expand_ref[...]) + dot(
            msg_ref[:16, base + heads : base + 2 * heads], expand_ref[...]
        )
        decays.append(decay[:1, :])
    norm_width = NORM_HEADS * P_SIZE
    table = table_ref[...]
    parts = []
    for start in range(0, width, norm_width):
        pres = []
        square = jnp.zeros((tokens, 1), f32)
        for begin in range(start, start + norm_width, H_BLOCK):
            at = slice(begin, begin + H_BLOCK)
            carried = None
            for k in reversed(range(count)):
                term = dot(inners[k], messages[k][:, at])
                carried = term if carried is None else term + decays[k][:, at] * carried
            pre = own_ref[:, at]
            if carried is not None:
                pre = pre + far_ref[:, at] * carried
            square = square + jnp.sum(pre * pre, axis=1, keepdims=True)
            pres.append(pre)
        inverse = lax.rsqrt(square * (1.0 / norm_width) + norm_eps)
        for index, pre in enumerate(pres):
            at = slice(start + index * H_BLOCK, start + (index + 1) * H_BLOCK)
            signed = (pre * inverse * gain_ref[:, at]).astype(bf16)
            parts.append(dot(signed, table))
    butterflies(parts)
    for index, part in enumerate(parts):
        out_ref[:, index * H_BLOCK : (index + 1) * H_BLOCK] = part.astype(bf16)


def half_at(which, size):
    return pl.ds(pl.multiple_of(which * size, size), size)


def start_all(copies):
    for copy in copies:
        copy.start()
    return copies


def wait_all(copies):
    for copy in copies:
        copy.wait()


def block_rows(index, size):
    return slice(index * size, (index + 1) * size)


def pack_kernel(
    where_ref,
    x_mine_ref,
    x_other_ref,
    b_ref,
    c_ref,
    steps_ref,
    mine_ref,
    other_ref,
    straight_ref,
    cross_ref,
):
    tokens, states = b_ref.shape
    half = x_mine_ref.shape[1]
    heads = steps_ref.shape[0] // 4
    member = where_ref[0]
    triangle = causal_mask(tokens).astype(f32).astype(bf16)
    step = steps_ref[: 2 * heads, :].T
    decay = steps_ref[2 * heads :, :].T
    cumul = exact_dot(triangle, decay)
    total = cumul[tokens - 1 : tokens, :]
    scale = jnp.exp(total - cumul) * step
    kept = jnp.exp(total)

    def pick(value, which):
        return jnp.where(which == 0, value[:, :heads], value[:, heads:])

    other_ref[:, :half] = x_other_ref[...]
    for out_ref, base, which in ((mine_ref, 0, member), (other_ref, half, 1 - member)):
        out_ref[:, base : base + states] = b_ref[...]
        out_ref[:, base + states : base + 2 * states] = c_ref[...]
        base += 2 * states
        out_ref[:, base:] = jnp.zeros((tokens, out_ref.shape[1] - base), bf16)
        terms = parts_of(pick(step, which), 3) + parts_of(pick(decay, which), 3)
        for index, term in enumerate(terms):
            out_ref[:, base + index * heads : base + (index + 1) * heads] = term
    expand = expansion(heads)
    for out_ref, x_ref, which in (
        (straight_ref, x_mine_ref, member),
        (cross_ref, x_other_ref, 1 - member),
    ):
        wide = spread(pick(scale, which), expand)
        weighted = (x_ref[...].astype(f32) * wide).astype(bf16)
        for index in range(half // LANES):
            out_ref[block_rows(index, tokens), :] = weighted[:, block_rows(index, LANES)]
        for index in range(states // LANES):
            out_ref[block_rows(half // LANES + index, tokens), :] = b_ref[
                :, block_rows(index, LANES)
            ]
        base = (half + states) // LANES * tokens
        rows = out_ref.shape[0] - base
        out_ref[base:, :] = jnp.zeros((rows, LANES), bf16)
        for index, term in enumerate(parts_of(pick(kept, which), 2)):
            out_ref[base:, block_rows(index, heads)] = jnp.broadcast_to(term, (rows, heads))


def expansion(heads):
    shape = (heads, heads * P_SIZE)
    row = lax.broadcasted_iota(jnp.int32, shape, 0)
    col = lax.broadcasted_iota(jnp.int32, shape, 1)
    return ((col >= row * P_SIZE) & (col < (row + 1) * P_SIZE)).astype(f32).astype(bf16)


def pair_kernel(
    where_ref,
    x_ref,
    meta_ref,
    msg_ref,
    skip_ref,
    own_ref,
    far_ref,
    c_pair_ref,
    x_both,
    b_both,
    step_both,
    decay_both,
):
    tokens, half = x_ref.shape
    states = c_pair_ref.shape[1]
    heads = half // P_SIZE
    member = where_ref[0]
    for which, x, meta in (
        (member, x_ref, meta_ref),
        (1 - member, msg_ref.at[:, :half], msg_ref.at[:, half:]),
    ):
        rows = half_at(which, tokens)
        x_both[rows, :] = x[...]
        b_both[rows, :] = meta[:, :states]
        c_pair_ref[rows, :] = meta[:, states : 2 * states]
        for index, both in enumerate((step_both, decay_both)):
            base = 2 * states + 3 * index * heads
            terms = [
                meta[:, base + term * heads : base + (term + 1) * heads].astype(f32)
                for term in range(3)
            ]
            both[rows, :] = (terms[2] + terms[1]) + terms[0]

    span = 2 * tokens
    causal = causal_mask(span)
    inner = jnp.where(causal, dot_nt(c_pair_ref[...], b_both[...]), 0.0)
    cumul = exact_dot(causal.astype(f32).astype(bf16), decay_both[...])
    cumul_t = cumul.T
    step_t = step_both[...].T
    skip = skip_ref[:, half_at(member, half)]
    expand = expansion(heads)
    reach = parts_of(jnp.exp(cumul), 2)
    first = lax.broadcasted_iota(jnp.int32, (tokens, 2 * P_SIZE), 1) < P_SIZE
    for pair in range(heads // 2):
        at = slice(pair * 2 * P_SIZE, (pair + 1) * 2 * P_SIZE)
        spans = []
        for block in range(2):
            x_block = x_both[block * tokens : (block + 1) * tokens, at]
            zero = jnp.zeros_like(x_block)
            spans.append((jnp.where(first, x_block, zero), jnp.where(first, zero, x_block)))
        for block in range(2):
            rows = slice(block * tokens, (block + 1) * tokens)
            mixings, values = [], []
            for place, head in enumerate((2 * pair, 2 * pair + 1)):
                for earlier in range(block + 1):
                    cols = slice(earlier * tokens, (earlier + 1) * tokens)
                    differ = cumul[rows, head : head + 1] - cumul_t[head : head + 1, cols]
                    if earlier == block:
                        differ = jnp.where(causal[:tokens, :tokens], differ, 0.0)
                    ratio = jnp.exp(differ)
                    mixings.append(
                        (ratio * (inner[rows, cols] * step_t[head : head + 1, cols])).astype(bf16)
                    )
                    values.append(spans[earlier][place])
            own = dot(jnp.concatenate(mixings, axis=1), jnp.concatenate(values, axis=0))
            own_ref[rows, at] = own + x_both[rows, at].astype(f32) * skip[:, at]
            far_ref[rows, at] = sum(dot(term[rows, :], expand[:, at]) for term in reach)


def gate_mix_kernel(count, pieces, *refs):
    sent = refs[: 2 * count]
    where_ref, gate_ref, gate_pair_ref, c_ref, own_ref, far_ref, gain_ref, table_ref = refs[
        2 * count : -3
    ]
    out_refs, gate_both = refs[-3:-1], refs[-1]
    span, half = own_ref.shape
    tokens = span // 2
    states = c_ref.shape[1]
    heads = half // P_SIZE
    member = where_ref[0]
    c_pair = c_ref[...]
    expand = expansion(heads)

    for which, gate in ((member, gate_ref), (1 - member, gate_pair_ref)):
        gate_both[half_at(which, tokens), :] = gate[...]

    def columns(ref, start, size):
        blocks = range(start // LANES, (start + size) // LANES)
        return jnp.concatenate([ref[block_rows(index, tokens), :] for index in blocks], axis=1)

    def kept(ref):
        base = (half + states) // LANES * tokens
        high, low = (ref[base:, block_rows(index, heads)] for index in range(2))
        return (dot(high, expand) + dot(low, expand))[:1, :]

    inners = [dot_nt(c_pair, columns(ref, half, states)).astype(bf16) for ref in sent]
    factors, pair_kept = [], []
    for k in range(count):
        one, two = kept(sent[2 * k]), kept(sent[2 * k + 1])
        pair_kept.append(one * two)
        factors += [jnp.where(member == 0, two, 1.0), jnp.where(member == 0, 1.0, one)]
    gain = gain_ref[:, half_at(member, half)]
    table = table_ref[...]
    parts = []
    norm_width = NORM_HEADS * P_SIZE
    for start in range(0, half, norm_width):
        pres = []
        square = jnp.zeros((span, 1), f32)
        for begin in range(start, start + norm_width, H_BLOCK):
            at = slice(begin, begin + H_BLOCK)
            pre = own_ref[:, at]
            carried = None
            for k in reversed(range(count)):
                term = 0.0
                for j in (2 * k, 2 * k + 1):
                    term = term + factors[j][:, at] * dot(
                        inners[j], columns(sent[j], begin, H_BLOCK)
                    )
                carried = term if carried is None else term + pair_kept[k][:, at] * carried
            if carried is not None:
                pre = pre + far_ref[:, at] * carried
            gate = gate_both[:, at].astype(f32)
            pre = pre * (gate / (1.0 + jnp.exp(-gate)))
            square = square + jnp.sum(pre * pre, axis=1, keepdims=True)
            pres.append(pre)
        inverse = lax.rsqrt(square * (1.0 / norm_width) + norm_eps)
        for index, pre in enumerate(pres):
            at = slice(start + index * H_BLOCK, start + (index + 1) * H_BLOCK)
            parts.append(dot((pre * inverse * gain[:, at]).astype(bf16), table))
    butterflies(parts)
    size = span // pieces
    for index, part in enumerate(parts):
        at = slice(index * H_BLOCK, (index + 1) * H_BLOCK)
        part = part.astype(bf16)
        for piece in range(pieces):
            to = slice(piece // 2 * size, (piece // 2 + 1) * size)
            out_refs[piece % 2][to, at] = part[piece * size : (piece + 1) * size, :]


def butterflies(parts):
    span = 1
    while span < len(parts):
        for low in range(len(parts)):
            if low & span == 0:
                a, b = parts[low], parts[low + span]
                parts[low], parts[low + span] = a + b, a - b
        span *= 2


def add_kernel(sign_ref, mixed_ref, received_ref, out_ref):
    sign = sign_ref[0].astype(f32)
    out_ref[...] = (mixed_ref[...].astype(f32) * sign + received_ref[...].astype(f32)).astype(bf16)


def project_kernel(pairs, where_ref, weight_ref, *refs):
    pieces = refs[: 2 * pairs]
    up_ref, down_ref, out_ref, weight_own, sums, sems = refs[2 * pairs :]
    rows, half = pieces[0].shape
    sign = (1 - 2 * where_ref[0]).astype(f32)
    sub_count, chan_count, _, blocks, size, features = out_ref.shape
    tile = half // 2
    copies = start_all(
        [
            pltpu.make_async_copy(
                weight_ref.at[start : start + tile, :],
                weight_own.at[start : start + tile, :],
                sems.at[start // tile],
            )
            for start in range(0, 2 * half, tile)
        ]
    )
    for step, copy in enumerate(copies):
        at = slice(step * tile, (step + 1) * tile)
        inner = slice(step * tile % half, step * tile % half + tile)
        scaled = []
        for pair in range(pairs):
            one = pieces[2 * pair][:, inner].astype(f32)
            two = pieces[2 * pair + 1][:, inner].astype(f32)
            mixed = (one - two) * sign if step * tile >= half else one + two
            quant = jnp.clip(mixed * up_ref[:, at], -clip_level, clip_level).astype(bf16)
            scaled.append((quant.astype(f32) * down_ref[:, at]).astype(bf16))
        copy.wait()
        term = dot(jnp.concatenate(scaled, axis=0), weight_own[at, :])
        if step == 0:
            sums[...] = term
        elif step < len(copies) - 1:
            sums[...] += term
        else:
            total = (sums[...] + term).astype(bf16)
    row = 0
    for pair in range(pairs):
        for block in range(blocks):
            for chan in range(chan_count):
                for sub in range(sub_count):
                    out_ref[sub, chan, pair, block] = total[row : row + size, :]
                    row += size


def place_kernel(where_ref, *refs):
    out_ref = refs[-1]
    features = refs[0].shape[1]
    for distance, ref in enumerate(refs[:-1]):
        out_ref[:, half_at(where_ref[0] ^ distance, features)] = ref[...]


def sylvester(order):
    table = np.ones((1, 1), np.float32)
    while table.shape[0] < order:
        table = np.block([[table, table], [table, -table]])
    return table


def shift_up(value, axis, distance):
    count = lax.axis_size(axis)
    return lax.ppermute(value, axis, [(k, k + distance) for k in range(count - distance)])


def turn(value, axis, distance):
    count = lax.axis_size(axis)
    return lax.ppermute(value, axis, [(k, (k + distance) % count) for k in range(count)])


def swap(value, axis, bit):
    count = lax.axis_size(axis)
    return lax.ppermute(value, axis, [(k, k ^ (1 << bit)) for k in range(count)])


def bits_of(axis):
    return range(lax.axis_size(axis).bit_length() - 1)


def halve(value, axis):
    here = lax.axis_index(axis)
    for bit in reversed(bits_of(axis)):
        pair = value.reshape((2, value.shape[0] // 2) + value.shape[1:])
        mine = here // 2**bit % 2
        keep = lax.dynamic_index_in_dim(pair, mine, 0, keepdims=False)
        give = lax.dynamic_index_in_dim(pair, 1 - mine, 0, keepdims=False)
        value = (keep.astype(f32) + swap(give, axis, bit).astype(f32)).astype(bf16)
    return value[0]


def call(kernel, out_shape, name, args, scalars=0, anywhere=0, scratch=(), params=PARAMS, cost=COST):
    specs = [pl.BlockSpec(memory_space=pltpu.SMEM)] * scalars
    specs += [pl.BlockSpec(memory_space=pltpu.HBM)] * anywhere
    specs += [pl.BlockSpec(memory_space=pltpu.VMEM)] * (len(args) - scalars - anywhere)
    return pl.pallas_call(
        kernel,
        out_shape=out_shape,
        in_specs=specs,
        scratch_shapes=scratch,
        compiler_params=params,
        cost_estimate=cost,
        name=name,
    )(*args)


def swap_seq(value, distance):
    count = lax.axis_size("seq")
    return lax.ppermute(value, "seq", [(k, k ^ distance) for k in range(count)])


def paired_body(
    x_in,
    b_in,
    c_in,
    step_size,
    log_decay,
    skip,
    gate_in,
    norm_gain,
    walsh_sign,
    channel_shift_power,
    out_weight,
):
    tokens, width = x_in.shape
    heads = step_size.shape[1]
    states = b_in.shape[2]
    half, half_heads = width // 2, heads // 2
    seq_count, chan_count, sub_count = (lax.axis_size(a) for a in ("seq", "chan", "sub"))
    pairs = seq_count // 2
    here = lax.axis_index("seq")
    member = here % 2
    group_local = lax.axis_index("sub") * heads // (LOCAL_HEADS // G)
    where = jnp.full((1,), member, jnp.int32)
    b_group = lax.dynamic_index_in_dim(b_in, group_local, 1, keepdims=False)
    c_group = lax.dynamic_index_in_dim(c_in, group_local, 1, keepdims=False)
    table = jnp.asarray(sylvester(H_BLOCK), bf16)

    def shape(rows, columns, kind):
        return jax.ShapeDtypeStruct((rows, columns), kind)

    def padded(columns):
        return pl.cdiv(columns, LANES) * LANES

    def half_of(value, which):
        return lax.dynamic_slice_in_dim(value, which * half, half, 1)

    x_mine, x_other = half_of(x_in, member), half_of(x_in, 1 - member)
    gate_mine, gate_other = half_of(gate_in, member), half_of(gate_in, 1 - member)
    steps = jnp.concatenate([step_size.T, log_decay.T], axis=0)
    with_pair = shape(tokens, 2 * states + padded(6 * half_heads), bf16)
    with_later = shape((half + states) // LANES * tokens + 16, LANES, bf16)
    meta_mine, to_pair, straight, cross = call(
        pack_kernel,
        (with_pair, shape(tokens, half + with_pair.shape[1], bf16), with_later, with_later),
        "pack",
        (where, x_mine, x_other, b_group, c_group, steps),
        1,
    )
    sent = []
    for ahead in range(1, pairs):
        firsts = range(seq_count - 2 * ahead)
        sent.append(lax.ppermute(straight, "seq", [(k, k + 2 * ahead) for k in firsts]))
        sent.append(lax.ppermute(cross, "seq", [(k, (k ^ 1) + 2 * ahead) for k in firsts]))
    from_pair, gate_pair = swap_seq(to_pair, 1), swap_seq(gate_other, 1)

    span = 2 * tokens
    own, far, c_pair = call(
        pair_kernel,
        (
            shape(span, half, f32),
            shape(span, half, f32),
            shape(span, states, bf16),
        ),
        "pair",
        (
            where,
            x_mine,
            meta_mine,
            from_pair,
            jnp.repeat(skip, P_SIZE)[None, :],
        ),
        1,
        0,
        (
            pltpu.VMEM((span, half), bf16),
            pltpu.VMEM((span, states), bf16),
            pltpu.VMEM((span, half_heads), f32),
            pltpu.VMEM((span, half_heads), f32),
        ),
        cost=SMALL,
    )
    signed_gain = (jnp.where(walsh_sign == 1, 1.0, -1.0) * norm_gain)[None, :]
    owners = chan_count * sub_count
    size = tokens // (2 * owners)
    count = len(sent) // 2
    chunks = pl.pallas_call(
        functools.partial(gate_mix_kernel, count, span // size),
        out_shape=(shape(tokens, half, bf16),) * 2,
        in_specs=[pl.BlockSpec(memory_space=pltpu.VMEM)] * (2 * count)
        + [pl.BlockSpec(memory_space=pltpu.SMEM)]
        + [pl.BlockSpec(memory_space=pltpu.VMEM)] * 7,
        scratch_shapes=[pltpu.VMEM((span, half), bf16)],
        compiler_params=PARAMS,
        cost_estimate=COST,
        name="mix",
    )(*sent, where, gate_mine, gate_pair, c_pair, own, far, signed_gain, table)

    def add_across(mixed, axis, bit, received):
        place = lax.axis_index(axis)
        sign = 1.0 - 2.0 * (place // 2**bit % 2).astype(f32)
        return (mixed.astype(f32) * sign + received.astype(f32)).astype(bf16)

    def across(mixed, axis):
        for bit in bits_of(axis):
            mixed = add_across(mixed, axis, bit, swap(mixed, axis, bit))
        return mixed

    first, second = (across(chunk, "sub") for chunk in chunks)
    first = across(first, "chan")
    first, second = lax.optimization_barrier((first, second))
    bits = bits_of("chan")
    for bit in bits[:-1]:
        second = add_across(second, "chan", bit, swap(second, "chan", bit))
    received = swap(second, "chan", bits[-1]) if bits else None
    ahead = range(1, pairs)
    far_first = [swap_seq(first, 2 * k) for k in ahead]
    near_first = swap_seq(first, 1)
    first, second, received, far_first, near_first = lax.optimization_barrier(
        (first, second, received, far_first, near_first)
    )
    if bits:
        sign = 1 - 2 * (lax.axis_index("chan") // 2 ** bits[-1] % 2)
        second = call(
            add_kernel,
            shape(tokens, half, bf16),
            "add",
            (jnp.full((1,), sign, jnp.int32), second, received),
            1,
        )
    passed_first = [swap_seq(value, 1) for value in far_first]
    all_first = [first, near_first]
    for far, passed in zip(far_first, passed_first):
        all_first += [far, passed]
    second_late = lax.optimization_barrier((second, passed_first))[0] if pairs > 1 else second
    all_second = [second, swap_seq(second_late, 1)]
    all_second += [swap_seq(second, k) for k in range(2, seq_count)]

    up = (power_two(channel_shift_power, 1) * (1.0 / math.sqrt(LOCAL_HEADS * P_SIZE)))[None, :]
    down = power_two(channel_shift_power, -1)[None, :]
    features = out_weight.shape[1]

    def project(pieces):
        return call(
            functools.partial(project_kernel, pairs),
            jax.ShapeDtypeStruct((sub_count, chan_count, pairs, 2, size, features), bf16),
            "project",
            (where, out_weight, *pieces, up, down),
            1,
            1,
            (
                pltpu.VMEM(out_weight.shape, bf16),
                pltpu.VMEM((pairs * tokens, features), f32),
                pltpu.SemaphoreType.DMA((4,)),
            ),
            WIDE_PARAMS,
        )

    def reduce(partial):
        return halve(halve(partial, "sub"), "chan")

    done = lax.optimization_barrier(jnp.bool_(True))
    done_first = lax.cond(
        done,
        lambda *pieces: reduce(project(pieces)),
        lambda *pieces: jnp.zeros((pairs, 2, size, features), bf16),
        *all_first,
    )
    done_first, all_second = lax.optimization_barrier((done_first, all_second))
    done_second = reduce(project(all_second))
    summed = jnp.stack([done_first, done_second], axis=2)
    returned = []
    for distance in range(seq_count):
        block = (member + distance) % 2
        value = lax.dynamic_index_in_dim(summed[distance // 2], block, 0, keepdims=False)
        value = value.reshape(2 * size, features)
        returned.append(swap_seq(value, distance) if distance else value)
    return call(
        place_kernel,
        shape(2 * size, seq_count * features, bf16),
        "place",
        (jnp.full((1,), here, jnp.int32), *returned),
        1,
    )


def body(x_in, b_in, c_in, step_size, *rest):
    tokens, heads = step_size.shape
    seq_count = lax.axis_size("seq")
    pieces = 2 * lax.axis_size("chan") * lax.axis_size("sub")
    if (
        heads % (2 * NORM_HEADS) == 0
        and seq_count % 2 == 0
        and seq_count & (seq_count - 1) == 0
        and tokens % (16 * pieces) == 0
    ):
        return paired_body(x_in, b_in, c_in, step_size, *rest)
    return plain_body(x_in, b_in, c_in, step_size, *rest)


def plain_body(
    x_in,
    b_in,
    c_in,
    step_size,
    log_decay,
    skip,
    gate_in,
    norm_gain,
    walsh_sign,
    channel_shift_power,
    out_weight,
):
    tokens, width = x_in.shape
    heads = step_size.shape[1]
    states = b_in.shape[2]
    seq_count = lax.axis_size("seq")
    sub_index = lax.axis_index("sub")
    group_local = sub_index * heads // (LOCAL_HEADS // G)
    b_group = lax.dynamic_slice_in_dim(b_in, group_local, 1, 1)[:, 0, :]
    c_group = lax.dynamic_slice_in_dim(c_in, group_local, 1, 1)[:, 0, :]
    expand = jnp.asarray(np.kron(np.eye(heads), np.ones((1, P_SIZE))), bf16)
    table = jnp.asarray(sylvester(H_BLOCK), bf16)

    tail = pl.cdiv(2 * heads, LANES) * LANES
    message, cumul = pl.pallas_call(
        message_kernel,
        out_shape=(
            jax.ShapeDtypeStruct((tokens, width + states + tail), bf16),
            jax.ShapeDtypeStruct((tokens, heads), f32),
        ),
        compiler_params=PARAMS,
        name="message",
    )(x_in, b_group, step_size, log_decay, expand)
    arrived = [shift_up(message, "seq", k) for k in range(1, seq_count)]

    wide_skip = jnp.repeat(skip, P_SIZE)[None, :]
    own, far = pl.pallas_call(
        local_kernel,
        out_shape=(
            jax.ShapeDtypeStruct((tokens, width), f32),
            jax.ShapeDtypeStruct((tokens, width), f32),
        ),
        compiler_params=PARAMS,
        name="local",
    )(x_in, b_group, c_group, step_size, cumul, gate_in, wide_skip, expand)

    signed_gain = (jnp.where(walsh_sign == 1, 1.0, -1.0) * norm_gain)[None, :]
    mixed = pl.pallas_call(
        functools.partial(mix_kernel, len(arrived)),
        out_shape=jax.ShapeDtypeStruct((tokens, width), bf16),
        compiler_params=PARAMS,
        name="mix",
    )(*arrived, c_group, own, far, signed_gain, table, expand)

    for axis in ("sub", "chan"):
        here = lax.axis_index(axis)
        for bit in bits_of(axis):
            other = swap(mixed.astype(bf16), axis, bit).astype(f32)
            sign = 1.0 - 2.0 * (here // 2**bit % 2).astype(f32)
            mixed = mixed.astype(f32) * sign + other
    rotated = mixed * (1.0 / math.sqrt(LOCAL_HEADS * P_SIZE))
    quant = jnp.clip(
        rotated * power_two(channel_shift_power, 1)[None, :], -clip_level, clip_level
    ).astype(bf16)
    scaled = (quant.astype(f32) * power_two(channel_shift_power, -1)[None, :]).astype(bf16)

    chan_count, sub_count = lax.axis_size("chan"), lax.axis_size("sub")
    rows = tokens // (chan_count * sub_count)
    order = sorted(range(1, seq_count), key=lambda k: -min(k, seq_count - k))
    blocks = {0: scaled}
    for k in order:
        blocks[k] = turn(scaled, "seq", k)
    sums = []
    for k in [0] + order:
        partial = dot(blocks[k], out_weight).astype(bf16)
        partial = partial.reshape(chan_count, sub_count, rows, -1)
        partial = halve(jnp.swapaxes(partial, 0, 1), "sub")
        done = halve(partial, "chan")
        sums.append((k, turn(done, "seq", -k % seq_count) if k else done))
    pieces = [value for _, value in sorted(sums, key=lambda item: item[0])]
    stacked = jnp.stack(pieces + pieces, axis=0)
    here = lax.axis_index("seq")
    placed = lax.dynamic_slice_in_dim(
        stacked, (seq_count - here) % seq_count, seq_count, 0
    )
    return jnp.swapaxes(placed, 0, 1).reshape(rows, -1)


def solution(mesh):
    return jax.shard_map(
        body,
        mesh=mesh,
        in_specs=(
            P(("groups", "seq"), ("chan", "sub")),
            P(("groups", "seq"), "chan", None),
            P(("groups", "seq"), "chan", None),
            P(("groups", "seq"), ("chan", "sub")),
            P(("groups", "seq"), ("chan", "sub")),
            P(("chan", "sub")),
            P(("groups", "seq"), ("chan", "sub")),
            P(("chan", "sub")),
            P(("chan", "sub")),
            P(("chan", "sub")),
            P(("chan", "sub"), "seq"),
        ),
        out_specs=P(("groups", "seq", "chan", "sub"), None),
        check_vma=False,
    )
```

```python
import functools
import math

import jax
import jax.numpy as jnp
import numpy as np
from jax import lax
from jax.experimental import pallas as pl
from jax.experimental.pallas import tpu as pltpu
from jax.sharding import PartitionSpec as P

LOCAL_HEADS = 128
P_SIZE = 64
G = 4
NORM_HEADS = 16


norm_eps = 1e-05
clip_level = 4.0
expo_levels = (-1, 0, 1, 2, 3)
LANES = 128
H_BLOCK = 256
COST = pl.CostEstimate(flops=1, transcendentals=0, bytes_accessed=30_000_000)
SMALL = pl.CostEstimate(flops=1, transcendentals=0, bytes_accessed=1)
f32 = jnp.float32
bf16 = jnp.bfloat16
PARAMS = pltpu.CompilerParams(vmem_limit_bytes=16 * 2**20)
WIDE_PARAMS = pltpu.CompilerParams(vmem_limit_bytes=16 * 2**20)


def power_two(expo, sign_flip):
    result = jnp.zeros(expo.shape, jnp.float32)
    for level in expo_levels:
        result = result + jnp.where(
            expo == level, jnp.float32(2.0 ** (sign_flip * level)), jnp.float32(0.0)
        )
    return result


def dot(a, b):
    return jnp.dot(a, b, preferred_element_type=f32)


def dot_nt(a, b):
    return lax.dot_general(a, b, (((1,), (1,)), ((), ())), preferred_element_type=f32)


def parts_of(value, count):
    terms = []
    for _ in range(count):
        term = value.astype(bf16)
        terms.append(term)
        value = value - term.astype(f32)
    return terms


def exact_dot(exact, value, count=3):
    return sum(dot(exact, term) for term in parts_of(value, count))


def spread(value, expand, count=2):
    return sum(dot(term, expand) for term in parts_of(value, count))


def causal_mask(size):
    row = lax.broadcasted_iota(jnp.int32, (size, size), 0)
    col = lax.broadcasted_iota(jnp.int32, (size, size), 1)
    return row >= col


def message_kernel(x_ref, b_ref, step_ref, decay_ref, expand_ref, msg_ref, cumul_ref):
    tokens, width = x_ref.shape
    heads = step_ref.shape[1]
    states = b_ref.shape[1]
    expand = expand_ref[...]
    triangle = causal_mask(tokens).astype(f32).astype(bf16)
    cumul = exact_dot(triangle, decay_ref[...])
    cumul_ref[...] = cumul
    total = cumul[tokens - 1 : tokens, :]
    scale = spread(jnp.exp(total - cumul) * step_ref[...], expand)
    msg_ref[:, :width] = (x_ref[...].astype(f32) * scale).astype(bf16)
    msg_ref[:, width : width + states] = b_ref[...]
    high, low = parts_of(jnp.exp(total), 2)
    base = width + states
    msg_ref[:, base:] = jnp.zeros((tokens, msg_ref.shape[1] - base), bf16)
    msg_ref[:, base : base + heads] = jnp.broadcast_to(high, (tokens, heads))
    msg_ref[:, base + heads : base + 2 * heads] = jnp.broadcast_to(low, (tokens, heads))


def local_kernel(
    x_ref, b_ref, c_ref, step_ref, cumul_ref, gate_ref, skip_ref, expand_ref, own_ref, far_ref
):
    tokens, width = x_ref.shape
    heads = step_ref.shape[1]
    causal = causal_mask(tokens)
    inner = dot_nt(c_ref[...], b_ref[...])
    cumul = cumul_ref[...]
    cumul_t = cumul.T
    step_t = step_ref[...].T
    first = lax.broadcasted_iota(jnp.int32, (tokens, 2 * P_SIZE), 1) < P_SIZE
    for pair in range(heads // 2):
        mixings = []
        for head in (2 * pair, 2 * pair + 1):
            differ = cumul[:, head : head + 1] - cumul_t[head : head + 1, :]
            ratio = jnp.exp(jnp.where(causal, differ, -jnp.inf))
            mixings.append((ratio * (inner * step_t[head : head + 1, :])).astype(bf16))
        at = slice(pair * 2 * P_SIZE, (pair + 1) * 2 * P_SIZE)
        x_pair = x_ref[:, at]
        zero = jnp.zeros_like(x_pair)
        blocks = jnp.concatenate(
            [jnp.where(first, x_pair, zero), jnp.where(first, zero, x_pair)], axis=0
        )
        own = dot(jnp.concatenate(mixings, axis=1), blocks)
        own = own + x_pair.astype(f32) * skip_ref[:, at]
        gate = gate_ref[:, at].astype(f32)
        own_ref[:, at] = own * (gate / (1.0 + jnp.exp(-gate)))
    reach = jnp.exp(cumul)
    tile = min(width, 512)
    for start in range(0, width, tile):
        at = slice(start, start + tile)
        gate = gate_ref[:, at].astype(f32)
        far_ref[:, at] = spread(reach, expand_ref[:, at]) * (gate / (1.0 + jnp.exp(-gate)))


def mix_kernel(count, *refs):
    messages = refs[:count]
    c_ref, own_ref, far_ref, gain_ref, table_ref, expand_ref, out_ref = refs[count:]
    tokens, width = own_ref.shape
    states = c_ref.shape[1]
    heads = expand_ref.shape[0]
    base = width + states
    c_group = c_ref[...]
    inners = []
    decays = []
    for msg_ref in messages:
        inners.append(dot_nt(c_group, msg_ref[:, width:base]).astype(bf16))
        decay = dot(msg_ref[:16, base : base + heads], expand_ref[...]) + dot(
            msg_ref[:16, base + heads : base + 2 * heads], expand_ref[...]
        )
        decays.append(decay[:1, :])
    norm_width = NORM_HEADS * P_SIZE
    table = table_ref[...]
    parts = []
    for start in range(0, width, norm_width):
        pres = []
        square = jnp.zeros((tokens, 1), f32)
        for begin in range(start, start + norm_width, H_BLOCK):
            at = slice(begin, begin + H_BLOCK)
            carried = None
            for k in reversed(range(count)):
                term = dot(inners[k], messages[k][:, at])
                carried = term if carried is None else term + decays[k][:, at] * carried
            pre = own_ref[:, at]
            if carried is not None:
                pre = pre + far_ref[:, at] * carried
            square = square + jnp.sum(pre * pre, axis=1, keepdims=True)
            pres.append(pre)
        inverse = lax.rsqrt(square * (1.0 / norm_width) + norm_eps)
        for index, pre in enumerate(pres):
            at = slice(start + index * H_BLOCK, start + (index + 1) * H_BLOCK)
            signed = (pre * inverse * gain_ref[:, at]).astype(bf16)
            parts.append(dot(signed, table))
    butterflies(parts)
    for index, part in enumerate(parts):
        out_ref[:, index * H_BLOCK : (index + 1) * H_BLOCK] = part.astype(bf16)


def half_at(which, size):
    return pl.ds(pl.multiple_of(which * size, size), size)


def start_all(copies):
    for copy in copies:
        copy.start()
    return copies


def wait_all(copies):
    for copy in copies:
        copy.wait()


def block_rows(index, size):
    return slice(index * size, (index + 1) * size)


def pack_kernel(
    where_ref,
    x_mine_ref,
    x_other_ref,
    b_ref,
    c_ref,
    steps_ref,
    mine_ref,
    other_ref,
    straight_ref,
    cross_ref,
):
    tokens, states = b_ref.shape
    half = x_mine_ref.shape[1]
    heads = steps_ref.shape[0] // 4
    member = where_ref[0]
    triangle = causal_mask(tokens).astype(f32).astype(bf16)
    step = steps_ref[: 2 * heads, :].T
    decay = steps_ref[2 * heads :, :].T
    cumul = exact_dot(triangle, decay)
    total = cumul[tokens - 1 : tokens, :]
    scale = jnp.exp(total - cumul) * step
    kept = jnp.exp(total)

    def pick(value, which):
        return jnp.where(which == 0, value[:, :heads], value[:, heads:])

    other_ref[:, :half] = x_other_ref[...]
    for out_ref, base, which in ((mine_ref, 0, member), (other_ref, half, 1 - member)):
        out_ref[:, base : base + states] = b_ref[...]
        out_ref[:, base + states : base + 2 * states] = c_ref[...]
        base += 2 * states
        out_ref[:, base:] = jnp.zeros((tokens, out_ref.shape[1] - base), bf16)
        terms = parts_of(pick(step, which), 3) + parts_of(pick(decay, which), 3)
        for index, term in enumerate(terms):
            out_ref[:, base + index * heads : base + (index + 1) * heads] = term
    expand = expansion(heads)
    for out_ref, x_ref, which in (
        (straight_ref, x_mine_ref, member),
        (cross_ref, x_other_ref, 1 - member),
    ):
        wide = spread(pick(scale, which), expand)
        weighted = (x_ref[...].astype(f32) * wide).astype(bf16)
        for index in range(half // LANES):
            out_ref[block_rows(index, tokens), :] = weighted[:, block_rows(index, LANES)]
        for index in range(states // LANES):
            out_ref[block_rows(half // LANES + index, tokens), :] = b_ref[
                :, block_rows(index, LANES)
            ]
        base = (half + states) // LANES * tokens
        rows = out_ref.shape[0] - base
        out_ref[base:, :] = jnp.zeros((rows, LANES), bf16)
        for index, term in enumerate(parts_of(pick(kept, which), 2)):
            out_ref[base:, block_rows(index, heads)] = jnp.broadcast_to(term, (rows, heads))


def expansion(heads):
    shape = (heads, heads * P_SIZE)
    row = lax.broadcasted_iota(jnp.int32, shape, 0)
    col = lax.broadcasted_iota(jnp.int32, shape, 1)
    return ((col >= row * P_SIZE) & (col < (row + 1) * P_SIZE)).astype(f32).astype(bf16)


def pair_kernel(
    where_ref,
    x_ref,
    meta_ref,
    msg_ref,
    skip_ref,
    own_ref,
    far_ref,
    c_pair_ref,
    x_both,
    b_both,
    step_both,
    decay_both,
):
    tokens, half = x_ref.shape
    states = c_pair_ref.shape[1]
    heads = half // P_SIZE
    member = where_ref[0]
    for which, x, meta in (
        (member, x_ref, meta_ref),
        (1 - member, msg_ref.at[:, :half], msg_ref.at[:, half:]),
    ):
        rows = half_at(which, tokens)
        x_both[rows, :] = x[...]
        b_both[rows, :] = meta[:, :states]
        c_pair_ref[rows, :] = meta[:, states : 2 * states]
        for index, both in enumerate((step_both, decay_both)):
            base = 2 * states + 3 * index * heads
            terms = [
                meta[:, base + term * heads : base + (term + 1) * heads].astype(f32)
                for term in range(3)
            ]
            both[rows, :] = (terms[2] + terms[1]) + terms[0]

    span = 2 * tokens
    causal = causal_mask(span)
    inner = jnp.where(causal, dot_nt(c_pair_ref[...], b_both[...]), 0.0)
    cumul = exact_dot(causal.astype(f32).astype(bf16), decay_both[...])
    cumul_t = cumul.T
    step_t = step_both[...].T
    skip = skip_ref[:, half_at(member, half)]
    expand = expansion(heads)
    reach = parts_of(jnp.exp(cumul), 2)
    first = lax.broadcasted_iota(jnp.int32, (tokens, 2 * P_SIZE), 1) < P_SIZE
    for pair in range(heads // 2):
        at = slice(pair * 2 * P_SIZE, (pair + 1) * 2 * P_SIZE)
        spans = []
        for block in range(2):
            x_block = x_both[block * tokens : (block + 1) * tokens, at]
            zero = jnp.zeros_like(x_block)
            spans.append((jnp.where(first, x_block, zero), jnp.where(first, zero, x_block)))
        for block in range(2):
            rows = slice(block * tokens, (block + 1) * tokens)
            mixings, values = [], []
            for place, head in enumerate((2 * pair, 2 * pair + 1)):
                for earlier in range(block + 1):
                    cols = slice(earlier * tokens, (earlier + 1) * tokens)
                    differ = cumul[rows, head : head + 1] - cumul_t[head : head + 1, cols]
                    if earlier == block:
                        differ = jnp.where(causal[:tokens, :tokens], differ, 0.0)
                    ratio = jnp.exp(differ)
                    mixings.append(
                        (ratio * (inner[rows, cols] * step_t[head : head + 1, cols])).astype(bf16)
                    )
                    values.append(spans[earlier][place])
            own = dot(jnp.concatenate(mixings, axis=1), jnp.concatenate(values, axis=0))
            own_ref[rows, at] = own + x_both[rows, at].astype(f32) * skip[:, at]
            far_ref[rows, at] = sum(dot(term[rows, :], expand[:, at]) for term in reach)


def gate_mix_kernel(count, pieces, *refs):
    sent = refs[: 2 * count]
    where_ref, gate_ref, gate_pair_ref, c_ref, own_ref, far_ref, gain_ref, table_ref = refs[
        2 * count : -3
    ]
    out_refs, gate_both = refs[-3:-1], refs[-1]
    span, half = own_ref.shape
    tokens = span // 2
    states = c_ref.shape[1]
    heads = half // P_SIZE
    member = where_ref[0]
    c_pair = c_ref[...]
    expand = expansion(heads)

    for which, gate in ((member, gate_ref), (1 - member, gate_pair_ref)):
        gate_both[half_at(which, tokens), :] = gate[...]

    def columns(ref, start, size):
        blocks = range(start // LANES, (start + size) // LANES)
        return jnp.concatenate([ref[block_rows(index, tokens), :] for index in blocks], axis=1)

    def kept(ref):
        base = (half + states) // LANES * tokens
        high, low = (ref[base:, block_rows(index, heads)] for index in range(2))
        return (dot(high, expand) + dot(low, expand))[:1, :]

    inners = [dot_nt(c_pair, columns(ref, half, states)).astype(bf16) for ref in sent]
    factors, pair_kept = [], []
    for k in range(count):
        one, two = kept(sent[2 * k]), kept(sent[2 * k + 1])
        pair_kept.append(one * two)
        factors += [jnp.where(member == 0, two, 1.0), jnp.where(member == 0, 1.0, one)]
    gain = gain_ref[:, half_at(member, half)]
    table = table_ref[...]
    parts = []
    norm_width = NORM_HEADS * P_SIZE
    for start in range(0, half, norm_width):
        pres = []
        square = jnp.zeros((span, 1), f32)
        for begin in range(start, start + norm_width, H_BLOCK):
            at = slice(begin, begin + H_BLOCK)
            pre = own_ref[:, at]
            carried = None
            for k in reversed(range(count)):
                term = 0.0
                for j in (2 * k, 2 * k + 1):
                    term = term + factors[j][:, at] * dot(
                        inners[j], columns(sent[j], begin, H_BLOCK)
                    )
                carried = term if carried is None else term + pair_kept[k][:, at] * carried
            if carried is not None:
                pre = pre + far_ref[:, at] * carried
            gate = gate_both[:, at].astype(f32)
            pre = pre * (gate / (1.0 + jnp.exp(-gate)))
            square = square + jnp.sum(pre * pre, axis=1, keepdims=True)
            pres.append(pre)
        inverse = lax.rsqrt(square * (1.0 / norm_width) + norm_eps)
        for index, pre in enumerate(pres):
            at = slice(start + index * H_BLOCK, start + (index + 1) * H_BLOCK)
            parts.append(dot((pre * inverse * gain[:, at]).astype(bf16), table))
    butterflies(parts)
    size = span // pieces
    for index, part in enumerate(parts):
        at = slice(index * H_BLOCK, (index + 1) * H_BLOCK)
        part = part.astype(bf16)
        for piece in range(pieces):
            to = slice(piece // 2 * size, (piece // 2 + 1) * size)
            out_refs[piece % 2][to, at] = part[piece * size : (piece + 1) * size, :]


def butterflies(parts):
    span = 1
    while span < len(parts):
        for low in range(len(parts)):
            if low & span == 0:
                a, b = parts[low], parts[low + span]
                parts[low], parts[low + span] = a + b, a - b
        span *= 2


def add_kernel(sign_ref, mixed_ref, received_ref, out_ref):
    sign = sign_ref[0].astype(f32)
    out_ref[...] = (mixed_ref[...].astype(f32) * sign + received_ref[...].astype(f32)).astype(bf16)


def project_kernel(pairs, where_ref, weight_ref, *refs):
    pieces = refs[: 2 * pairs]
    up_ref, down_ref, out_ref, weight_own, sums, sems = refs[2 * pairs :]
    rows, half = pieces[0].shape
    sign = (1 - 2 * where_ref[0]).astype(f32)
    sub_count, chan_count, _, blocks, size, features = out_ref.shape
    tile = half // 2
    copies = start_all(
        [
            pltpu.make_async_copy(
                weight_ref.at[start : start + tile, :],
                weight_own.at[start : start + tile, :],
                sems.at[start // tile],
            )
            for start in range(0, 2 * half, tile)
        ]
    )
    for step, copy in enumerate(copies):
        at = slice(step * tile, (step + 1) * tile)
        inner = slice(step * tile % half, step * tile % half + tile)
        scaled = []
        for pair in range(pairs):
            one = pieces[2 * pair][:, inner].astype(f32)
            two = pieces[2 * pair + 1][:, inner].astype(f32)
            mixed = (one - two) * sign if step * tile >= half else one + two
            quant = jnp.clip(mixed * up_ref[:, at], -clip_level, clip_level).astype(bf16)
            scaled.append((quant.astype(f32) * down_ref[:, at]).astype(bf16))
        copy.wait()
        term = dot(jnp.concatenate(scaled, axis=0), weight_own[at, :])
        if step == 0:
            sums[...] = term
        elif step < len(copies) - 1:
            sums[...] += term
        else:
            total = (sums[...] + term).astype(bf16)
    row = 0
    for pair in range(pairs):
        for block in range(blocks):
            for chan in range(chan_count):
                for sub in range(sub_count):
                    out_ref[sub, chan, pair, block] = total[row : row + size, :]
                    row += size


def place_kernel(where_ref, *refs):
    out_ref = refs[-1]
    features = refs[0].shape[1]
    for distance, ref in enumerate(refs[:-1]):
        out_ref[:, half_at(where_ref[0] ^ distance, features)] = ref[...]


def sylvester(order):
    table = np.ones((1, 1), np.float32)
    while table.shape[0] < order:
        table = np.block([[table, table], [table, -table]])
    return table


def shift_up(value, axis, distance):
    count = lax.axis_size(axis)
    return lax.ppermute(value, axis, [(k, k + distance) for k in range(count - distance)])


def turn(value, axis, distance):
    count = lax.axis_size(axis)
    return lax.ppermute(value, axis, [(k, (k + distance) % count) for k in range(count)])


def swap(value, axis, bit):
    count = lax.axis_size(axis)
    return lax.ppermute(value, axis, [(k, k ^ (1 << bit)) for k in range(count)])


def bits_of(axis):
    return range(lax.axis_size(axis).bit_length() - 1)


def halve(value, axis):
    here = lax.axis_index(axis)
    for bit in reversed(bits_of(axis)):
        pair = value.reshape((2, value.shape[0] // 2) + value.shape[1:])
        mine = here // 2**bit % 2
        keep = lax.dynamic_index_in_dim(pair, mine, 0, keepdims=False)
        give = lax.dynamic_index_in_dim(pair, 1 - mine, 0, keepdims=False)
        value = (keep.astype(f32) + swap(give, axis, bit).astype(f32)).astype(bf16)
    return value[0]


def call(kernel, out_shape, name, args, scalars=0, anywhere=0, scratch=(), params=PARAMS, cost=COST):
    specs = [pl.BlockSpec(memory_space=pltpu.SMEM)] * scalars
    specs += [pl.BlockSpec(memory_space=pltpu.HBM)] * anywhere
    specs += [pl.BlockSpec(memory_space=pltpu.VMEM)] * (len(args) - scalars - anywhere)
    return pl.pallas_call(
        kernel,
        out_shape=out_shape,
        in_specs=specs,
        scratch_shapes=scratch,
        compiler_params=params,
        cost_estimate=cost,
        name=name,
    )(*args)


def swap_seq(value, distance):
    count = lax.axis_size("seq")
    return lax.ppermute(value, "seq", [(k, k ^ distance) for k in range(count)])


def paired_body(
    x_in,
    b_in,
    c_in,
    step_size,
    log_decay,
    skip,
    gate_in,
    norm_gain,
    walsh_sign,
    channel_shift_power,
    out_weight,
):
    tokens, width = x_in.shape
    heads = step_size.shape[1]
    states = b_in.shape[2]
    half, half_heads = width // 2, heads // 2
    seq_count, chan_count, sub_count = (lax.axis_size(a) for a in ("seq", "chan", "sub"))
    pairs = seq_count // 2
    here = lax.axis_index("seq")
    member = here % 2
    group_local = lax.axis_index("sub") * heads // (LOCAL_HEADS // G)
    where = jnp.full((1,), member, jnp.int32)
    b_group = lax.dynamic_index_in_dim(b_in, group_local, 1, keepdims=False)
    c_group = lax.dynamic_index_in_dim(c_in, group_local, 1, keepdims=False)
    table = jnp.asarray(sylvester(H_BLOCK), bf16)

    def shape(rows, columns, kind):
        return jax.ShapeDtypeStruct((rows, columns), kind)

    def padded(columns):
        return pl.cdiv(columns, LANES) * LANES

    def half_of(value, which):
        return lax.dynamic_slice_in_dim(value, which * half, half, 1)

    x_mine, x_other = half_of(x_in, member), half_of(x_in, 1 - member)
    gate_mine, gate_other = half_of(gate_in, member), half_of(gate_in, 1 - member)
    steps = jnp.concatenate([step_size.T, log_decay.T], axis=0)
    with_pair = shape(tokens, 2 * states + padded(6 * half_heads), bf16)
    with_later = shape((half + states) // LANES * tokens + 16, LANES, bf16)
    meta_mine, to_pair, straight, cross = call(
        pack_kernel,
        (with_pair, shape(tokens, half + with_pair.shape[1], bf16), with_later, with_later),
        "pack",
        (where, x_mine, x_other, b_group, c_group, steps),
        1,
    )
    sent = []
    for ahead in range(1, pairs):
        firsts = range(seq_count - 2 * ahead)
        sent.append(lax.ppermute(straight, "seq", [(k, k + 2 * ahead) for k in firsts]))
        sent.append(lax.ppermute(cross, "seq", [(k, (k ^ 1) + 2 * ahead) for k in firsts]))
    from_pair, gate_pair = swap_seq(to_pair, 1), swap_seq(gate_other, 1)

    span = 2 * tokens
    own, far, c_pair = call(
        pair_kernel,
        (
            shape(span, half, f32),
            shape(span, half, f32),
            shape(span, states, bf16),
        ),
        "pair",
        (
            where,
            x_mine,
            meta_mine,
            from_pair,
            jnp.repeat(skip, P_SIZE)[None, :],
        ),
        1,
        0,
        (
            pltpu.VMEM((span, half), bf16),
            pltpu.VMEM((span, states), bf16),
            pltpu.VMEM((span, half_heads), f32),
            pltpu.VMEM((span, half_heads), f32),
        ),
        cost=SMALL,
    )
    signed_gain = (jnp.where(walsh_sign == 1, 1.0, -1.0) * norm_gain)[None, :]
    owners = chan_count * sub_count
    size = tokens // (2 * owners)
    count = len(sent) // 2
    chunks = pl.pallas_call(
        functools.partial(gate_mix_kernel, count, span // size),
        out_shape=(shape(tokens, half, bf16),) * 2,
        in_specs=[pl.BlockSpec(memory_space=pltpu.VMEM)] * (2 * count)
        + [pl.BlockSpec(memory_space=pltpu.SMEM)]
        + [pl.BlockSpec(memory_space=pltpu.VMEM)] * 7,
        scratch_shapes=[pltpu.VMEM((span, half), bf16)],
        compiler_params=PARAMS,
        cost_estimate=COST,
        name="mix",
    )(*sent, where, gate_mine, gate_pair, c_pair, own, far, signed_gain, table)

    def add_across(mixed, axis, bit, received):
        place = lax.axis_index(axis)
        sign = 1.0 - 2.0 * (place // 2**bit % 2).astype(f32)
        return (mixed.astype(f32) * sign + received.astype(f32)).astype(bf16)

    def across(mixed, axis):
        for bit in bits_of(axis):
            mixed = add_across(mixed, axis, bit, swap(mixed, axis, bit))
        return mixed

    first, second = (across(chunk, "sub") for chunk in chunks)
    ahead = range(1, pairs)
    near_second = swap_seq(second, 1)
    far_early = [swap_seq(second[: tokens // 2], 2 * k) for k in ahead]
    first = across(first, "chan")
    first, second, near_second, far_early = lax.optimization_barrier(
        (first, second, near_second, far_early)
    )
    bits = bits_of("chan")
    moving = [second[: tokens // 2], second[tokens // 2 :], *far_early]
    for bit in bits[:-1]:
        moving = [add_across(value, "chan", bit, swap(value, "chan", bit)) for value in moving]
    received = [swap(value, "chan", bits[-1]) for value in moving if bits]
    far_first = [swap_seq(first, 2 * k) for k in ahead]
    near_first = swap_seq(first, 1)
    first, near_second, moving, received, far_first, near_first = lax.optimization_barrier(
        (first, near_second, moving, received, far_first, near_first)
    )
    if bits:
        sign = jnp.full((1,), 1 - 2 * (lax.axis_index("chan") // 2 ** bits[-1] % 2), jnp.int32)
        moving = [
            call(add_kernel, shape(*mixed.shape, bf16), "add", (sign, mixed, other), 1)
            for mixed, other in zip(moving, received)
        ]
    early, late, *far_early = moving
    passed_first = [swap_seq(value, 1) for value in far_first]
    all_first = [first, near_first]
    for far, passed in zip(far_first, passed_first):
        all_first += [far, passed]
    all_first, far_early = lax.optimization_barrier((all_first, far_early))
    passed_early = [swap_seq(value, 1) for value in far_early]
    far_late = [swap_seq(late, 2 * k) for k in ahead]
    cross_late = [swap_seq(late, 2 * k + 1) for k in ahead]
    near_second = across(near_second, "chan")

    up = (power_two(channel_shift_power, 1) * (1.0 / math.sqrt(LOCAL_HEADS * P_SIZE)))[None, :]
    down = power_two(channel_shift_power, -1)[None, :]
    features = out_weight.shape[1]

    def project(pieces):
        return call(
            functools.partial(project_kernel, pairs),
            jax.ShapeDtypeStruct((sub_count, chan_count, pairs, 2, size, features), bf16),
            "project",
            (where, out_weight, *pieces, up, down),
            1,
            1,
            (
                pltpu.VMEM(out_weight.shape, bf16),
                pltpu.VMEM((pairs * tokens, features), f32),
                pltpu.SemaphoreType.DMA((4,)),
            ),
            WIDE_PARAMS,
        )

    go = lax.optimization_barrier(jnp.bool_(True))

    def stage(pieces):
        return lax.cond(
            go,
            lambda *pieces: halve(project(pieces), "sub"),
            lambda *_: jnp.zeros((chan_count, pairs, 2, size, features), bf16),
            *pieces,
        )

    done_first = stage(all_first)
    done_first, near_second, far_late, cross_late, passed_early = lax.optimization_barrier(
        (done_first, near_second, far_late, cross_late, passed_early)
    )
    all_second = [jnp.concatenate([early, late], axis=0), near_second]
    for parts in zip(far_early, far_late, passed_early, cross_late):
        all_second += [jnp.concatenate(parts[:2], axis=0), jnp.concatenate(parts[2:], axis=0)]
    done_first, done_second = lax.optimization_barrier(
        (halve(done_first, "chan"), stage(all_second))
    )
    done_second = halve(done_second, "chan")
    summed = jnp.stack([done_first, done_second], axis=2)
    returned = []
    for distance in range(seq_count):
        block = (member + distance) % 2
        value = lax.dynamic_index_in_dim(summed[distance // 2], block, 0, keepdims=False)
        value = value.reshape(2 * size, features)
        returned.append(swap_seq(value, distance) if distance else value)
    return call(
        place_kernel,
        shape(2 * size, seq_count * features, bf16),
        "place",
        (jnp.full((1,), here, jnp.int32), *returned),
        1,
    )


def body(x_in, b_in, c_in, step_size, *rest):
    tokens, heads = step_size.shape
    seq_count = lax.axis_size("seq")
    pieces = 2 * lax.axis_size("chan") * lax.axis_size("sub")
    if (
        heads % (2 * NORM_HEADS) == 0
        and seq_count % 2 == 0
        and seq_count & (seq_count - 1) == 0
        and tokens % (16 * pieces) == 0
    ):
        return paired_body(x_in, b_in, c_in, step_size, *rest)
    return plain_body(x_in, b_in, c_in, step_size, *rest)


def plain_body(
    x_in,
    b_in,
    c_in,
    step_size,
    log_decay,
    skip,
    gate_in,
    norm_gain,
    walsh_sign,
    channel_shift_power,
    out_weight,
):
    tokens, width = x_in.shape
    heads = step_size.shape[1]
    states = b_in.shape[2]
    seq_count = lax.axis_size("seq")
    sub_index = lax.axis_index("sub")
    group_local = sub_index * heads // (LOCAL_HEADS // G)
    b_group = lax.dynamic_slice_in_dim(b_in, group_local, 1, 1)[:, 0, :]
    c_group = lax.dynamic_slice_in_dim(c_in, group_local, 1, 1)[:, 0, :]
    expand = jnp.asarray(np.kron(np.eye(heads), np.ones((1, P_SIZE))), bf16)
    table = jnp.asarray(sylvester(H_BLOCK), bf16)

    tail = pl.cdiv(2 * heads, LANES) * LANES
    message, cumul = pl.pallas_call(
        message_kernel,
        out_shape=(
            jax.ShapeDtypeStruct((tokens, width + states + tail), bf16),
            jax.ShapeDtypeStruct((tokens, heads), f32),
        ),
        compiler_params=PARAMS,
        name="message",
    )(x_in, b_group, step_size, log_decay, expand)
    arrived = [shift_up(message, "seq", k) for k in range(1, seq_count)]

    wide_skip = jnp.repeat(skip, P_SIZE)[None, :]
    own, far = pl.pallas_call(
        local_kernel,
        out_shape=(
            jax.ShapeDtypeStruct((tokens, width), f32),
            jax.ShapeDtypeStruct((tokens, width), f32),
        ),
        compiler_params=PARAMS,
        name="local",
    )(x_in, b_group, c_group, step_size, cumul, gate_in, wide_skip, expand)

    signed_gain = (jnp.where(walsh_sign == 1, 1.0, -1.0) * norm_gain)[None, :]
    mixed = pl.pallas_call(
        functools.partial(mix_kernel, len(arrived)),
        out_shape=jax.ShapeDtypeStruct((tokens, width), bf16),
        compiler_params=PARAMS,
        name="mix",
    )(*arrived, c_group, own, far, signed_gain, table, expand)

    for axis in ("sub", "chan"):
        here = lax.axis_index(axis)
        for bit in bits_of(axis):
            other = swap(mixed.astype(bf16), axis, bit).astype(f32)
            sign = 1.0 - 2.0 * (here // 2**bit % 2).astype(f32)
            mixed = mixed.astype(f32) * sign + other
    rotated = mixed * (1.0 / math.sqrt(LOCAL_HEADS * P_SIZE))
    quant = jnp.clip(
        rotated * power_two(channel_shift_power, 1)[None, :], -clip_level, clip_level
    ).astype(bf16)
    scaled = (quant.astype(f32) * power_two(channel_shift_power, -1)[None, :]).astype(bf16)

    chan_count, sub_count = lax.axis_size("chan"), lax.axis_size("sub")
    rows = tokens // (chan_count * sub_count)
    order = sorted(range(1, seq_count), key=lambda k: -min(k, seq_count - k))
    blocks = {0: scaled}
    for k in order:
        blocks[k] = turn(scaled, "seq", k)
    sums = []
    for k in [0] + order:
        partial = dot(blocks[k], out_weight).astype(bf16)
        partial = partial.reshape(chan_count, sub_count, rows, -1)
        partial = halve(jnp.swapaxes(partial, 0, 1), "sub")
        done = halve(partial, "chan")
        sums.append((k, turn(done, "seq", -k % seq_count) if k else done))
    pieces = [value for _, value in sorted(sums, key=lambda item: item[0])]
    stacked = jnp.stack(pieces + pieces, axis=0)
    here = lax.axis_index("seq")
    placed = lax.dynamic_slice_in_dim(
        stacked, (seq_count - here) % seq_count, seq_count, 0
    )
    return jnp.swapaxes(placed, 0, 1).reshape(rows, -1)


def solution(mesh):
    return jax.shard_map(
        body,
        mesh=mesh,
        in_specs=(
            P(("groups", "seq"), ("chan", "sub")),
            P(("groups", "seq"), "chan", None),
            P(("groups", "seq"), "chan", None),
            P(("groups", "seq"), ("chan", "sub")),
            P(("groups", "seq"), ("chan", "sub")),
            P(("chan", "sub")),
            P(("groups", "seq"), ("chan", "sub")),
            P(("chan", "sub")),
            P(("chan", "sub")),
            P(("chan", "sub")),
            P(("chan", "sub"), "seq"),
        ),
        out_specs=P(("groups", "seq", "chan", "sub"), None),
        check_vma=False,
    )
```

```python
import functools
import math

import jax
import jax.numpy as jnp
import numpy as np
from jax import lax
from jax.experimental import pallas as pl
from jax.experimental.pallas import tpu as pltpu
from jax.sharding import PartitionSpec as P

LOCAL_HEADS = 128
P_SIZE = 64
G = 4
NORM_HEADS = 16


norm_eps = 1e-05
clip_level = 4.0
expo_levels = (-1, 0, 1, 2, 3)
LANES = 128
H_BLOCK = 256
COST = pl.CostEstimate(flops=1, transcendentals=0, bytes_accessed=30_000_000)
SMALL = pl.CostEstimate(flops=1, transcendentals=0, bytes_accessed=1)
f32 = jnp.float32
bf16 = jnp.bfloat16
PARAMS = pltpu.CompilerParams(vmem_limit_bytes=16 * 2**20)
WIDE_PARAMS = pltpu.CompilerParams(vmem_limit_bytes=16 * 2**20)


def power_two(expo, sign_flip):
    result = jnp.zeros(expo.shape, jnp.float32)
    for level in expo_levels:
        result = result + jnp.where(
            expo == level, jnp.float32(2.0 ** (sign_flip * level)), jnp.float32(0.0)
        )
    return result


def dot(a, b):
    return jnp.dot(a, b, preferred_element_type=f32)


def dot_nt(a, b):
    return lax.dot_general(a, b, (((1,), (1,)), ((), ())), preferred_element_type=f32)


def parts_of(value, count):
    terms = []
    for _ in range(count):
        term = value.astype(bf16)
        terms.append(term)
        value = value - term.astype(f32)
    return terms


def exact_dot(exact, value, count=3):
    return sum(dot(exact, term) for term in parts_of(value, count))


def spread(value, expand, count=2):
    return sum(dot(term, expand) for term in parts_of(value, count))


def causal_mask(size):
    row = lax.broadcasted_iota(jnp.int32, (size, size), 0)
    col = lax.broadcasted_iota(jnp.int32, (size, size), 1)
    return row >= col


def message_kernel(x_ref, b_ref, step_ref, decay_ref, expand_ref, msg_ref, cumul_ref):
    tokens, width = x_ref.shape
    heads = step_ref.shape[1]
    states = b_ref.shape[1]
    expand = expand_ref[...]
    triangle = causal_mask(tokens).astype(f32).astype(bf16)
    cumul = exact_dot(triangle, decay_ref[...])
    cumul_ref[...] = cumul
    total = cumul[tokens - 1 : tokens, :]
    scale = spread(jnp.exp(total - cumul) * step_ref[...], expand)
    msg_ref[:, :width] = (x_ref[...].astype(f32) * scale).astype(bf16)
    msg_ref[:, width : width + states] = b_ref[...]
    high, low = parts_of(jnp.exp(total), 2)
    base = width + states
    msg_ref[:, base:] = jnp.zeros((tokens, msg_ref.shape[1] - base), bf16)
    msg_ref[:, base : base + heads] = jnp.broadcast_to(high, (tokens, heads))
    msg_ref[:, base + heads : base + 2 * heads] = jnp.broadcast_to(low, (tokens, heads))


def local_kernel(
    x_ref, b_ref, c_ref, step_ref, cumul_ref, gate_ref, skip_ref, expand_ref, own_ref, far_ref
):
    tokens, width = x_ref.shape
    heads = step_ref.shape[1]
    causal = causal_mask(tokens)
    inner = dot_nt(c_ref[...], b_ref[...])
    cumul = cumul_ref[...]
    cumul_t = cumul.T
    step_t = step_ref[...].T
    first = lax.broadcasted_iota(jnp.int32, (tokens, 2 * P_SIZE), 1) < P_SIZE
    for pair in range(heads // 2):
        mixings = []
        for head in (2 * pair, 2 * pair + 1):
            differ = cumul[:, head : head + 1] - cumul_t[head : head + 1, :]
            ratio = jnp.exp(jnp.where(causal, differ, -jnp.inf))
            mixings.append((ratio * (inner * step_t[head : head + 1, :])).astype(bf16))
        at = slice(pair * 2 * P_SIZE, (pair + 1) * 2 * P_SIZE)
        x_pair = x_ref[:, at]
        zero = jnp.zeros_like(x_pair)
        blocks = jnp.concatenate(
            [jnp.where(first, x_pair, zero), jnp.where(first, zero, x_pair)], axis=0
        )
        own = dot(jnp.concatenate(mixings, axis=1), blocks)
        own = own + x_pair.astype(f32) * skip_ref[:, at]
        gate = gate_ref[:, at].astype(f32)
        own_ref[:, at] = own * (gate / (1.0 + jnp.exp(-gate)))
    reach = jnp.exp(cumul)
    tile = min(width, 512)
    for start in range(0, width, tile):
        at = slice(start, start + tile)
        gate = gate_ref[:, at].astype(f32)
        far_ref[:, at] = spread(reach, expand_ref[:, at]) * (gate / (1.0 + jnp.exp(-gate)))


def mix_kernel(count, *refs):
    messages = refs[:count]
    c_ref, own_ref, far_ref, gain_ref, table_ref, expand_ref, out_ref = refs[count:]
    tokens, width = own_ref.shape
    states = c_ref.shape[1]
    heads = expand_ref.shape[0]
    base = width + states
    c_group = c_ref[...]
    inners = []
    decays = []
    for msg_ref in messages:
        inners.append(dot_nt(c_group, msg_ref[:, width:base]).astype(bf16))
        decay = dot(msg_ref[:16, base : base + heads], expand_ref[...]) + dot(
            msg_ref[:16, base + heads : base + 2 * heads], expand_ref[...]
        )
        decays.append(decay[:1, :])
    norm_width = NORM_HEADS * P_SIZE
    table = table_ref[...]
    parts = []
    for start in range(0, width, norm_width):
        pres = []
        square = jnp.zeros((tokens, 1), f32)
        for begin in range(start, start + norm_width, H_BLOCK):
            at = slice(begin, begin + H_BLOCK)
            carried = None
            for k in reversed(range(count)):
                term = dot(inners[k], messages[k][:, at])
                carried = term if carried is None else term + decays[k][:, at] * carried
            pre = own_ref[:, at]
            if carried is not None:
                pre = pre + far_ref[:, at] * carried
            square = square + jnp.sum(pre * pre, axis=1, keepdims=True)
            pres.append(pre)
        inverse = lax.rsqrt(square * (1.0 / norm_width) + norm_eps)
        for index, pre in enumerate(pres):
            at = slice(start + index * H_BLOCK, start + (index + 1) * H_BLOCK)
            signed = (pre * inverse * gain_ref[:, at]).astype(bf16)
            parts.append(dot(signed, table))
    butterflies(parts)
    for index, part in enumerate(parts):
        out_ref[:, index * H_BLOCK : (index + 1) * H_BLOCK] = part.astype(bf16)


def half_at(which, size):
    return pl.ds(pl.multiple_of(which * size, size), size)


def start_all(copies):
    for copy in copies:
        copy.start()
    return copies


def wait_all(copies):
    for copy in copies:
        copy.wait()


def block_rows(index, size):
    return slice(index * size, (index + 1) * size)


def pack_kernel(
    where_ref,
    x_mine_ref,
    x_other_ref,
    b_ref,
    c_ref,
    steps_ref,
    mine_ref,
    other_ref,
    straight_ref,
    cross_ref,
):
    tokens, states = b_ref.shape
    half = x_mine_ref.shape[1]
    heads = steps_ref.shape[0] // 4
    member = where_ref[0]
    triangle = causal_mask(tokens).astype(f32).astype(bf16)
    step = steps_ref[: 2 * heads, :].T
    decay = steps_ref[2 * heads :, :].T
    cumul = exact_dot(triangle, decay)
    total = cumul[tokens - 1 : tokens, :]
    scale = jnp.exp(total - cumul) * step
    kept = jnp.exp(total)

    def pick(value, which):
        return jnp.where(which == 0, value[:, :heads], value[:, heads:])

    other_ref[:, :half] = x_other_ref[...]
    for out_ref, base, which in ((mine_ref, 0, member), (other_ref, half, 1 - member)):
        out_ref[:, base : base + states] = b_ref[...]
        out_ref[:, base + states : base + 2 * states] = c_ref[...]
        base += 2 * states
        out_ref[:, base:] = jnp.zeros((tokens, out_ref.shape[1] - base), bf16)
        terms = parts_of(pick(step, which), 3) + parts_of(pick(decay, which), 3)
        for index, term in enumerate(terms):
            out_ref[:, base + index * heads : base + (index + 1) * heads] = term
    expand = expansion(heads)
    for out_ref, x_ref, which in (
        (straight_ref, x_mine_ref, member),
        (cross_ref, x_other_ref, 1 - member),
    ):
        wide = spread(pick(scale, which), expand)
        weighted = (x_ref[...].astype(f32) * wide).astype(bf16)
        for index in range(half // LANES):
            out_ref[block_rows(index, tokens), :] = weighted[:, block_rows(index, LANES)]
        for index in range(states // LANES):
            out_ref[block_rows(half // LANES + index, tokens), :] = b_ref[
                :, block_rows(index, LANES)
            ]
        base = (half + states) // LANES * tokens
        rows = out_ref.shape[0] - base
        out_ref[base:, :] = jnp.zeros((rows, LANES), bf16)
        for index, term in enumerate(parts_of(pick(kept, which), 2)):
            out_ref[base:, block_rows(index, heads)] = jnp.broadcast_to(term, (rows, heads))


def expansion(heads):
    shape = (heads, heads * P_SIZE)
    row = lax.broadcasted_iota(jnp.int32, shape, 0)
    col = lax.broadcasted_iota(jnp.int32, shape, 1)
    return ((col >= row * P_SIZE) & (col < (row + 1) * P_SIZE)).astype(f32).astype(bf16)


def pair_kernel(
    where_ref,
    x_ref,
    meta_ref,
    msg_ref,
    skip_ref,
    own_ref,
    far_ref,
    c_pair_ref,
    x_both,
    b_both,
    step_both,
    decay_both,
):
    tokens, half = x_ref.shape
    states = c_pair_ref.shape[1]
    heads = half // P_SIZE
    member = where_ref[0]
    for which, x, meta in (
        (member, x_ref, meta_ref),
        (1 - member, msg_ref.at[:, :half], msg_ref.at[:, half:]),
    ):
        rows = half_at(which, tokens)
        x_both[rows, :] = x[...]
        b_both[rows, :] = meta[:, :states]
        c_pair_ref[rows, :] = meta[:, states : 2 * states]
        for index, both in enumerate((step_both, decay_both)):
            base = 2 * states + 3 * index * heads
            terms = [
                meta[:, base + term * heads : base + (term + 1) * heads].astype(f32)
                for term in range(3)
            ]
            both[rows, :] = (terms[2] + terms[1]) + terms[0]

    span = 2 * tokens
    causal = causal_mask(span)
    inner = jnp.where(causal, dot_nt(c_pair_ref[...], b_both[...]), 0.0)
    cumul = exact_dot(causal.astype(f32).astype(bf16), decay_both[...])
    cumul_t = cumul.T
    step_t = step_both[...].T
    skip = skip_ref[:, half_at(member, half)]
    expand = expansion(heads)
    reach = parts_of(jnp.exp(cumul), 2)
    first = lax.broadcasted_iota(jnp.int32, (tokens, 2 * P_SIZE), 1) < P_SIZE
    for pair in range(heads // 2):
        at = slice(pair * 2 * P_SIZE, (pair + 1) * 2 * P_SIZE)
        spans = []
        for block in range(2):
            x_block = x_both[block * tokens : (block + 1) * tokens, at]
            zero = jnp.zeros_like(x_block)
            spans.append((jnp.where(first, x_block, zero), jnp.where(first, zero, x_block)))
        for block in range(2):
            rows = slice(block * tokens, (block + 1) * tokens)
            mixings, values = [], []
            for place, head in enumerate((2 * pair, 2 * pair + 1)):
                for earlier in range(block + 1):
                    cols = slice(earlier * tokens, (earlier + 1) * tokens)
                    differ = cumul[rows, head : head + 1] - cumul_t[head : head + 1, cols]
                    if earlier == block:
                        differ = jnp.where(causal[:tokens, :tokens], differ, 0.0)
                    ratio = jnp.exp(differ)
                    mixings.append(
                        (ratio * (inner[rows, cols] * step_t[head : head + 1, cols])).astype(bf16)
                    )
                    values.append(spans[earlier][place])
            own = dot(jnp.concatenate(mixings, axis=1), jnp.concatenate(values, axis=0))
            own_ref[rows, at] = own + x_both[rows, at].astype(f32) * skip[:, at]
            far_ref[rows, at] = sum(dot(term[rows, :], expand[:, at]) for term in reach)


def gate_mix_kernel(count, pieces, *refs):
    sent = refs[: 2 * count]
    where_ref, gate_ref, gate_pair_ref, c_ref, own_ref, far_ref, gain_ref, table_ref = refs[
        2 * count : -3
    ]
    out_refs, gate_both = refs[-3:-1], refs[-1]
    span, half = own_ref.shape
    tokens = span // 2
    states = c_ref.shape[1]
    heads = half // P_SIZE
    member = where_ref[0]
    c_pair = c_ref[...]
    expand = expansion(heads)

    for which, gate in ((member, gate_ref), (1 - member, gate_pair_ref)):
        gate_both[half_at(which, tokens), :] = gate[...]

    def columns(ref, start, size):
        blocks = range(start // LANES, (start + size) // LANES)
        return jnp.concatenate([ref[block_rows(index, tokens), :] for index in blocks], axis=1)

    def kept(ref):
        base = (half + states) // LANES * tokens
        high, low = (ref[base:, block_rows(index, heads)] for index in range(2))
        return (dot(high, expand) + dot(low, expand))[:1, :]

    inners = [dot_nt(c_pair, columns(ref, half, states)).astype(bf16) for ref in sent]
    factors, pair_kept = [], []
    for k in range(count):
        one, two = kept(sent[2 * k]), kept(sent[2 * k + 1])
        pair_kept.append(one * two)
        factors += [jnp.where(member == 0, two, 1.0), jnp.where(member == 0, 1.0, one)]
    gain = gain_ref[:, half_at(member, half)]
    table = table_ref[...]
    parts = []
    norm_width = NORM_HEADS * P_SIZE
    for start in range(0, half, norm_width):
        pres = []
        square = jnp.zeros((span, 1), f32)
        for begin in range(start, start + norm_width, H_BLOCK):
            at = slice(begin, begin + H_BLOCK)
            pre = own_ref[:, at]
            carried = None
            for k in reversed(range(count)):
                term = 0.0
                for j in (2 * k, 2 * k + 1):
                    term = term + factors[j][:, at] * dot(
                        inners[j], columns(sent[j], begin, H_BLOCK)
                    )
                carried = term if carried is None else term + pair_kept[k][:, at] * carried
            if carried is not None:
                pre = pre + far_ref[:, at] * carried
            gate = gate_both[:, at].astype(f32)
            pre = pre * (gate / (1.0 + jnp.exp(-gate)))
            square = square + jnp.sum(pre * pre, axis=1, keepdims=True)
            pres.append(pre)
        inverse = lax.rsqrt(square * (1.0 / norm_width) + norm_eps)
        for index, pre in enumerate(pres):
            at = slice(start + index * H_BLOCK, start + (index + 1) * H_BLOCK)
            parts.append(dot((pre * inverse * gain[:, at]).astype(bf16), table))
    butterflies(parts)
    size = span // pieces
    for index, part in enumerate(parts):
        at = slice(index * H_BLOCK, (index + 1) * H_BLOCK)
        part = part.astype(bf16)
        for piece in range(pieces):
            to = slice(piece // 2 * size, (piece // 2 + 1) * size)
            out_refs[piece % 2][to, at] = part[piece * size : (piece + 1) * size, :]


def butterflies(parts):
    span = 1
    while span < len(parts):
        for low in range(len(parts)):
            if low & span == 0:
                a, b = parts[low], parts[low + span]
                parts[low], parts[low + span] = a + b, a - b
        span *= 2


def add_kernel(sign_ref, mixed_ref, received_ref, out_ref):
    sign = sign_ref[0].astype(f32)
    out_ref[...] = (mixed_ref[...].astype(f32) * sign + received_ref[...].astype(f32)).astype(bf16)


def project_kernel(pairs, where_ref, weight_ref, *refs):
    pieces = refs[: 2 * pairs]
    up_ref, down_ref, out_ref, weight_own, sums, sems = refs[2 * pairs :]
    rows, half = pieces[0].shape
    sign = (1 - 2 * where_ref[0]).astype(f32)
    sub_count, chan_count, _, blocks, size, features = out_ref.shape
    tile = half // 2
    copies = start_all(
        [
            pltpu.make_async_copy(
                weight_ref.at[start : start + tile, :],
                weight_own.at[start : start + tile, :],
                sems.at[start // tile],
            )
            for start in range(0, 2 * half, tile)
        ]
    )
    for step, copy in enumerate(copies):
        at = slice(step * tile, (step + 1) * tile)
        inner = slice(step * tile % half, step * tile % half + tile)
        scaled = []
        for pair in range(pairs):
            one = pieces[2 * pair][:, inner].astype(f32)
            two = pieces[2 * pair + 1][:, inner].astype(f32)
            mixed = (one - two) * sign if step * tile >= half else one + two
            quant = jnp.clip(mixed * up_ref[:, at], -clip_level, clip_level).astype(bf16)
            scaled.append((quant.astype(f32) * down_ref[:, at]).astype(bf16))
        copy.wait()
        term = dot(jnp.concatenate(scaled, axis=0), weight_own[at, :])
        if step == 0:
            sums[...] = term
        elif step < len(copies) - 1:
            sums[...] += term
        else:
            total = (sums[...] + term).astype(bf16)
    row = 0
    for pair in range(pairs):
        for block in range(blocks):
            for chan in range(chan_count):
                for sub in range(sub_count):
                    out_ref[sub, chan, pair, block] = total[row : row + size, :]
                    row += size


def place_kernel(where_ref, *refs):
    out_ref = refs[-1]
    features = refs[0].shape[1]
    for distance, ref in enumerate(refs[:-1]):
        out_ref[:, half_at(where_ref[0] ^ distance, features)] = ref[...]


def sylvester(order):
    table = np.ones((1, 1), np.float32)
    while table.shape[0] < order:
        table = np.block([[table, table], [table, -table]])
    return table


def shift_up(value, axis, distance):
    count = lax.axis_size(axis)
    return lax.ppermute(value, axis, [(k, k + distance) for k in range(count - distance)])


def turn(value, axis, distance):
    count = lax.axis_size(axis)
    return lax.ppermute(value, axis, [(k, (k + distance) % count) for k in range(count)])


def swap(value, axis, bit):
    count = lax.axis_size(axis)
    return lax.ppermute(value, axis, [(k, k ^ (1 << bit)) for k in range(count)])


def bits_of(axis):
    return range(lax.axis_size(axis).bit_length() - 1)


def halve(value, axis):
    here = lax.axis_index(axis)
    for bit in reversed(bits_of(axis)):
        pair = value.reshape((2, value.shape[0] // 2) + value.shape[1:])
        mine = here // 2**bit % 2
        keep = lax.dynamic_index_in_dim(pair, mine, 0, keepdims=False)
        give = lax.dynamic_index_in_dim(pair, 1 - mine, 0, keepdims=False)
        value = (keep.astype(f32) + swap(give, axis, bit).astype(f32)).astype(bf16)
    return value[0]


def call(kernel, out_shape, name, args, scalars=0, anywhere=0, scratch=(), params=PARAMS, cost=COST):
    specs = [pl.BlockSpec(memory_space=pltpu.SMEM)] * scalars
    specs += [pl.BlockSpec(memory_space=pltpu.HBM)] * anywhere
    specs += [pl.BlockSpec(memory_space=pltpu.VMEM)] * (len(args) - scalars - anywhere)
    return pl.pallas_call(
        kernel,
        out_shape=out_shape,
        in_specs=specs,
        scratch_shapes=scratch,
        compiler_params=params,
        cost_estimate=cost,
        name=name,
    )(*args)


def swap_seq(value, distance):
    count = lax.axis_size("seq")
    return lax.ppermute(value, "seq", [(k, k ^ distance) for k in range(count)])


def paired_body(
    x_in,
    b_in,
    c_in,
    step_size,
    log_decay,
    skip,
    gate_in,
    norm_gain,
    walsh_sign,
    channel_shift_power,
    out_weight,
):
    tokens, width = x_in.shape
    heads = step_size.shape[1]
    states = b_in.shape[2]
    half, half_heads = width // 2, heads // 2
    seq_count, chan_count, sub_count = (lax.axis_size(a) for a in ("seq", "chan", "sub"))
    pairs = seq_count // 2
    here = lax.axis_index("seq")
    member = here % 2
    group_local = lax.axis_index("sub") * heads // (LOCAL_HEADS // G)
    where = jnp.full((1,), member, jnp.int32)
    b_group = lax.dynamic_index_in_dim(b_in, group_local, 1, keepdims=False)
    c_group = lax.dynamic_index_in_dim(c_in, group_local, 1, keepdims=False)
    table = jnp.asarray(sylvester(H_BLOCK), bf16)

    def shape(rows, columns, kind):
        return jax.ShapeDtypeStruct((rows, columns), kind)

    def padded(columns):
        return pl.cdiv(columns, LANES) * LANES

    def half_of(value, which):
        return lax.dynamic_slice_in_dim(value, which * half, half, 1)

    x_mine, x_other = half_of(x_in, member), half_of(x_in, 1 - member)
    gate_mine, gate_other = half_of(gate_in, member), half_of(gate_in, 1 - member)
    steps = jnp.concatenate([step_size.T, log_decay.T], axis=0)
    with_pair = shape(tokens, 2 * states + padded(6 * half_heads), bf16)
    with_later = shape((half + states) // LANES * tokens + 16, LANES, bf16)
    meta_mine, to_pair, straight, cross = call(
        pack_kernel,
        (with_pair, shape(tokens, half + with_pair.shape[1], bf16), with_later, with_later),
        "pack",
        (where, x_mine, x_other, b_group, c_group, steps),
        1,
    )
    sent = []
    for ahead in range(1, pairs):
        firsts = range(seq_count - 2 * ahead)
        sent.append(lax.ppermute(straight, "seq", [(k, k + 2 * ahead) for k in firsts]))
        sent.append(lax.ppermute(cross, "seq", [(k, (k ^ 1) + 2 * ahead) for k in firsts]))
    from_pair, gate_pair = swap_seq(to_pair, 1), swap_seq(gate_other, 1)

    span = 2 * tokens
    own, far, c_pair = call(
        pair_kernel,
        (
            shape(span, half, f32),
            shape(span, half, f32),
            shape(span, states, bf16),
        ),
        "pair",
        (
            where,
            x_mine,
            meta_mine,
            from_pair,
            jnp.repeat(skip, P_SIZE)[None, :],
        ),
        1,
        0,
        (
            pltpu.VMEM((span, half), bf16),
            pltpu.VMEM((span, states), bf16),
            pltpu.VMEM((span, half_heads), f32),
            pltpu.VMEM((span, half_heads), f32),
        ),
        cost=SMALL,
    )
    signed_gain = (jnp.where(walsh_sign == 1, 1.0, -1.0) * norm_gain)[None, :]
    owners = chan_count * sub_count
    size = tokens // (2 * owners)
    count = len(sent) // 2
    chunks = pl.pallas_call(
        functools.partial(gate_mix_kernel, count, span // size),
        out_shape=(shape(tokens, half, bf16),) * 2,
        in_specs=[pl.BlockSpec(memory_space=pltpu.VMEM)] * (2 * count)
        + [pl.BlockSpec(memory_space=pltpu.SMEM)]
        + [pl.BlockSpec(memory_space=pltpu.VMEM)] * 7,
        scratch_shapes=[pltpu.VMEM((span, half), bf16)],
        compiler_params=PARAMS,
        cost_estimate=COST,
        name="mix",
    )(*sent, where, gate_mine, gate_pair, c_pair, own, far, signed_gain, table)

    def add_across(mixed, axis, bit, received):
        place = lax.axis_index(axis)
        sign = 1.0 - 2.0 * (place // 2**bit % 2).astype(f32)
        return (mixed.astype(f32) * sign + received.astype(f32)).astype(bf16)

    def across(mixed, axis):
        for bit in bits_of(axis):
            mixed = add_across(mixed, axis, bit, swap(mixed, axis, bit))
        return mixed

    first, second = (across(chunk, "sub") for chunk in chunks)
    ahead = range(1, pairs)
    cut = tokens * 3 // 4
    near_second = swap_seq(second, 1)
    far_early = [swap_seq(second[:cut], 2 * k) for k in ahead]
    bits = bits_of("chan")
    halves = [first[: tokens // 2], first[tokens // 2 :]]
    for bit in bits[:-1]:
        halves = [add_across(value, "chan", bit, swap(value, "chan", bit)) for value in halves]
    received = [swap(value, "chan", bits[-1]) for value in halves if bits]
    halves, received, second, near_second, far_early = lax.optimization_barrier(
        (halves, received, second, near_second, far_early)
    )
    if bits:
        halves = [add_across(*pair[:1], "chan", bits[-1], pair[1]) for pair in zip(halves, received)]
    first = jnp.concatenate(halves, axis=0)
    moving = [second[:cut], second[cut:], *far_early]
    for bit in bits[:-1]:
        moving = [add_across(value, "chan", bit, swap(value, "chan", bit)) for value in moving]
    received = [swap(value, "chan", bits[-1]) for value in moving if bits]
    far_first = [swap_seq(first, 2 * k) for k in ahead]
    near_first = swap_seq(first, 1)
    first, near_second, moving, received, far_first, near_first = lax.optimization_barrier(
        (first, near_second, moving, received, far_first, near_first)
    )
    if bits:
        sign = jnp.full((1,), 1 - 2 * (lax.axis_index("chan") // 2 ** bits[-1] % 2), jnp.int32)
        moving = [
            call(add_kernel, shape(*mixed.shape, bf16), "add", (sign, mixed, other), 1)
            for mixed, other in zip(moving, received)
        ]
    early, late, *far_early = moving
    passed_first = [swap_seq(value, 1) for value in far_first]
    all_first = [first, near_first]
    for far, passed in zip(far_first, passed_first):
        all_first += [far, passed]
    all_first, far_early = lax.optimization_barrier((all_first, far_early))
    passed_early = [swap_seq(value, 1) for value in far_early]
    far_late = [swap_seq(late, 2 * k) for k in ahead]
    cross_late = [swap_seq(late, 2 * k + 1) for k in ahead]
    near_second = across(near_second, "chan")

    up = (power_two(channel_shift_power, 1) * (1.0 / math.sqrt(LOCAL_HEADS * P_SIZE)))[None, :]
    down = power_two(channel_shift_power, -1)[None, :]
    features = out_weight.shape[1]

    def project(pieces):
        return call(
            functools.partial(project_kernel, pairs),
            jax.ShapeDtypeStruct((sub_count, chan_count, pairs, 2, size, features), bf16),
            "project",
            (where, out_weight, *pieces, up, down),
            1,
            1,
            (
                pltpu.VMEM(out_weight.shape, bf16),
                pltpu.VMEM((pairs * tokens, features), f32),
                pltpu.SemaphoreType.DMA((4,)),
            ),
            WIDE_PARAMS,
        )

    go = lax.optimization_barrier(jnp.bool_(True))

    def stage(pieces):
        return lax.cond(
            go,
            lambda *pieces: halve(project(pieces), "sub"),
            lambda *_: jnp.zeros((chan_count, pairs, 2, size, features), bf16),
            *pieces,
        )

    done_first = stage(all_first)
    done_first, near_second, far_late, cross_late, passed_early = lax.optimization_barrier(
        (done_first, near_second, far_late, cross_late, passed_early)
    )
    all_second = [jnp.concatenate([early, late], axis=0), near_second]
    for parts in zip(far_early, far_late, passed_early, cross_late):
        all_second += [jnp.concatenate(parts[:2], axis=0), jnp.concatenate(parts[2:], axis=0)]
    done_first, done_second = lax.optimization_barrier(
        (halve(done_first, "chan"), stage(all_second))
    )
    done_second = halve(done_second, "chan")
    summed = jnp.stack([done_first, done_second], axis=2)
    returned = []
    for distance in range(seq_count):
        block = (member + distance) % 2
        value = lax.dynamic_index_in_dim(summed[distance // 2], block, 0, keepdims=False)
        value = value.reshape(2 * size, features)
        returned.append(swap_seq(value, distance) if distance else value)
    return call(
        place_kernel,
        shape(2 * size, seq_count * features, bf16),
        "place",
        (jnp.full((1,), here, jnp.int32), *returned),
        1,
    )


def body(x_in, b_in, c_in, step_size, *rest):
    tokens, heads = step_size.shape
    seq_count = lax.axis_size("seq")
    pieces = 2 * lax.axis_size("chan") * lax.axis_size("sub")
    if (
        heads % (2 * NORM_HEADS) == 0
        and seq_count % 2 == 0
        and seq_count & (seq_count - 1) == 0
        and tokens % (16 * pieces) == 0
    ):
        return paired_body(x_in, b_in, c_in, step_size, *rest)
    return plain_body(x_in, b_in, c_in, step_size, *rest)


def plain_body(
    x_in,
    b_in,
    c_in,
    step_size,
    log_decay,
    skip,
    gate_in,
    norm_gain,
    walsh_sign,
    channel_shift_power,
    out_weight,
):
    tokens, width = x_in.shape
    heads = step_size.shape[1]
    states = b_in.shape[2]
    seq_count = lax.axis_size("seq")
    sub_index = lax.axis_index("sub")
    group_local = sub_index * heads // (LOCAL_HEADS // G)
    b_group = lax.dynamic_slice_in_dim(b_in, group_local, 1, 1)[:, 0, :]
    c_group = lax.dynamic_slice_in_dim(c_in, group_local, 1, 1)[:, 0, :]
    expand = jnp.asarray(np.kron(np.eye(heads), np.ones((1, P_SIZE))), bf16)
    table = jnp.asarray(sylvester(H_BLOCK), bf16)

    tail = pl.cdiv(2 * heads, LANES) * LANES
    message, cumul = pl.pallas_call(
        message_kernel,
        out_shape=(
            jax.ShapeDtypeStruct((tokens, width + states + tail), bf16),
            jax.ShapeDtypeStruct((tokens, heads), f32),
        ),
        compiler_params=PARAMS,
        name="message",
    )(x_in, b_group, step_size, log_decay, expand)
    arrived = [shift_up(message, "seq", k) for k in range(1, seq_count)]

    wide_skip = jnp.repeat(skip, P_SIZE)[None, :]
    own, far = pl.pallas_call(
        local_kernel,
        out_shape=(
            jax.ShapeDtypeStruct((tokens, width), f32),
            jax.ShapeDtypeStruct((tokens, width), f32),
        ),
        compiler_params=PARAMS,
        name="local",
    )(x_in, b_group, c_group, step_size, cumul, gate_in, wide_skip, expand)

    signed_gain = (jnp.where(walsh_sign == 1, 1.0, -1.0) * norm_gain)[None, :]
    mixed = pl.pallas_call(
        functools.partial(mix_kernel, len(arrived)),
        out_shape=jax.ShapeDtypeStruct((tokens, width), bf16),
        compiler_params=PARAMS,
        name="mix",
    )(*arrived, c_group, own, far, signed_gain, table, expand)

    for axis in ("sub", "chan"):
        here = lax.axis_index(axis)
        for bit in bits_of(axis):
            other = swap(mixed.astype(bf16), axis, bit).astype(f32)
            sign = 1.0 - 2.0 * (here // 2**bit % 2).astype(f32)
            mixed = mixed.astype(f32) * sign + other
    rotated = mixed * (1.0 / math.sqrt(LOCAL_HEADS * P_SIZE))
    quant = jnp.clip(
        rotated * power_two(channel_shift_power, 1)[None, :], -clip_level, clip_level
    ).astype(bf16)
    scaled = (quant.astype(f32) * power_two(channel_shift_power, -1)[None, :]).astype(bf16)

    chan_count, sub_count = lax.axis_size("chan"), lax.axis_size("sub")
    rows = tokens // (chan_count * sub_count)
    order = sorted(range(1, seq_count), key=lambda k: -min(k, seq_count - k))
    blocks = {0: scaled}
    for k in order:
        blocks[k] = turn(scaled, "seq", k)
    sums = []
    for k in [0] + order:
        partial = dot(blocks[k], out_weight).astype(bf16)
        partial = partial.reshape(chan_count, sub_count, rows, -1)
        partial = halve(jnp.swapaxes(partial, 0, 1), "sub")
        done = halve(partial, "chan")
        sums.append((k, turn(done, "seq", -k % seq_count) if k else done))
    pieces = [value for _, value in sorted(sums, key=lambda item: item[0])]
    stacked = jnp.stack(pieces + pieces, axis=0)
    here = lax.axis_index("seq")
    placed = lax.dynamic_slice_in_dim(
        stacked, (seq_count - here) % seq_count, seq_count, 0
    )
    return jnp.swapaxes(placed, 0, 1).reshape(rows, -1)


def solution(mesh):
    return jax.shard_map(
        body,
        mesh=mesh,
        in_specs=(
            P(("groups", "seq"), ("chan", "sub")),
            P(("groups", "seq"), "chan", None),
            P(("groups", "seq"), "chan", None),
            P(("groups", "seq"), ("chan", "sub")),
            P(("groups", "seq"), ("chan", "sub")),
            P(("chan", "sub")),
            P(("groups", "seq"), ("chan", "sub")),
            P(("chan", "sub")),
            P(("chan", "sub")),
            P(("chan", "sub")),
            P(("chan", "sub"), "seq"),
        ),
        out_specs=P(("groups", "seq", "chan", "sub"), None),
        check_vma=False,
    )
```

```python
import functools
import math

import jax
import jax.numpy as jnp
import numpy as np
from jax import lax
from jax.experimental import pallas as pl
from jax.experimental.pallas import tpu as pltpu
from jax.sharding import PartitionSpec as P

LOCAL_HEADS = 128
P_SIZE = 64
G = 4
NORM_HEADS = 16


norm_eps = 1e-05
clip_level = 4.0
expo_levels = (-1, 0, 1, 2, 3)
LANES = 128
H_BLOCK = 256
COST = pl.CostEstimate(flops=1, transcendentals=0, bytes_accessed=30_000_000)
SMALL = pl.CostEstimate(flops=1, transcendentals=0, bytes_accessed=1)
f32 = jnp.float32
bf16 = jnp.bfloat16
PARAMS = pltpu.CompilerParams(vmem_limit_bytes=16 * 2**20)
WIDE_PARAMS = pltpu.CompilerParams(vmem_limit_bytes=16 * 2**20)


def power_two(expo, sign_flip):
    result = jnp.zeros(expo.shape, jnp.float32)
    for level in expo_levels:
        result = result + jnp.where(
            expo == level, jnp.float32(2.0 ** (sign_flip * level)), jnp.float32(0.0)
        )
    return result


def dot(a, b):
    return jnp.dot(a, b, preferred_element_type=f32)


def dot_nt(a, b):
    return lax.dot_general(a, b, (((1,), (1,)), ((), ())), preferred_element_type=f32)


def parts_of(value, count):
    terms = []
    for _ in range(count):
        term = value.astype(bf16)
        terms.append(term)
        value = value - term.astype(f32)
    return terms


def exact_dot(exact, value, count=3):
    return sum(dot(exact, term) for term in parts_of(value, count))


def spread(value, expand, count=2):
    return sum(dot(term, expand) for term in parts_of(value, count))


def causal_mask(size):
    row = lax.broadcasted_iota(jnp.int32, (size, size), 0)
    col = lax.broadcasted_iota(jnp.int32, (size, size), 1)
    return row >= col


def message_kernel(x_ref, b_ref, step_ref, decay_ref, expand_ref, msg_ref, cumul_ref):
    tokens, width = x_ref.shape
    heads = step_ref.shape[1]
    states = b_ref.shape[1]
    expand = expand_ref[...]
    triangle = causal_mask(tokens).astype(f32).astype(bf16)
    cumul = exact_dot(triangle, decay_ref[...])
    cumul_ref[...] = cumul
    total = cumul[tokens - 1 : tokens, :]
    scale = spread(jnp.exp(total - cumul) * step_ref[...], expand)
    msg_ref[:, :width] = (x_ref[...].astype(f32) * scale).astype(bf16)
    msg_ref[:, width : width + states] = b_ref[...]
    high, low = parts_of(jnp.exp(total), 2)
    base = width + states
    msg_ref[:, base:] = jnp.zeros((tokens, msg_ref.shape[1] - base), bf16)
    msg_ref[:, base : base + heads] = jnp.broadcast_to(high, (tokens, heads))
    msg_ref[:, base + heads : base + 2 * heads] = jnp.broadcast_to(low, (tokens, heads))


def local_kernel(
    x_ref, b_ref, c_ref, step_ref, cumul_ref, gate_ref, skip_ref, expand_ref, own_ref, far_ref
):
    tokens, width = x_ref.shape
    heads = step_ref.shape[1]
    causal = causal_mask(tokens)
    inner = dot_nt(c_ref[...], b_ref[...])
    cumul = cumul_ref[...]
    cumul_t = cumul.T
    step_t = step_ref[...].T
    first = lax.broadcasted_iota(jnp.int32, (tokens, 2 * P_SIZE), 1) < P_SIZE
    for pair in range(heads // 2):
        mixings = []
        for head in (2 * pair, 2 * pair + 1):
            differ = cumul[:, head : head + 1] - cumul_t[head : head + 1, :]
            ratio = jnp.exp(jnp.where(causal, differ, -jnp.inf))
            mixings.append((ratio * (inner * step_t[head : head + 1, :])).astype(bf16))
        at = slice(pair * 2 * P_SIZE, (pair + 1) * 2 * P_SIZE)
        x_pair = x_ref[:, at]
        zero = jnp.zeros_like(x_pair)
        blocks = jnp.concatenate(
            [jnp.where(first, x_pair, zero), jnp.where(first, zero, x_pair)], axis=0
        )
        own = dot(jnp.concatenate(mixings, axis=1), blocks)
        own = own + x_pair.astype(f32) * skip_ref[:, at]
        gate = gate_ref[:, at].astype(f32)
        own_ref[:, at] = own * (gate / (1.0 + jnp.exp(-gate)))
    reach = jnp.exp(cumul)
    tile = min(width, 512)
    for start in range(0, width, tile):
        at = slice(start, start + tile)
        gate = gate_ref[:, at].astype(f32)
        far_ref[:, at] = spread(reach, expand_ref[:, at]) * (gate / (1.0 + jnp.exp(-gate)))


def mix_kernel(count, *refs):
    messages = refs[:count]
    c_ref, own_ref, far_ref, gain_ref, table_ref, expand_ref, out_ref = refs[count:]
    tokens, width = own_ref.shape
    states = c_ref.shape[1]
    heads = expand_ref.shape[0]
    base = width + states
    c_group = c_ref[...]
    inners = []
    decays = []
    for msg_ref in messages:
        inners.append(dot_nt(c_group, msg_ref[:, width:base]).astype(bf16))
        decay = dot(msg_ref[:16, base : base + heads], expand_ref[...]) + dot(
            msg_ref[:16, base + heads : base + 2 * heads], expand_ref[...]
        )
        decays.append(decay[:1, :])
    norm_width = NORM_HEADS * P_SIZE
    table = table_ref[...]
    parts = []
    for start in range(0, width, norm_width):
        pres = []
        square = jnp.zeros((tokens, 1), f32)
        for begin in range(start, start + norm_width, H_BLOCK):
            at = slice(begin, begin + H_BLOCK)
            carried = None
            for k in reversed(range(count)):
                term = dot(inners[k], messages[k][:, at])
                carried = term if carried is None else term + decays[k][:, at] * carried
            pre = own_ref[:, at]
            if carried is not None:
                pre = pre + far_ref[:, at] * carried
            square = square + jnp.sum(pre * pre, axis=1, keepdims=True)
            pres.append(pre)
        inverse = lax.rsqrt(square * (1.0 / norm_width) + norm_eps)
        for index, pre in enumerate(pres):
            at = slice(start + index * H_BLOCK, start + (index + 1) * H_BLOCK)
            signed = (pre * inverse * gain_ref[:, at]).astype(bf16)
            parts.append(dot(signed, table))
    butterflies(parts)
    for index, part in enumerate(parts):
        out_ref[:, index * H_BLOCK : (index + 1) * H_BLOCK] = part.astype(bf16)


def half_at(which, size):
    return pl.ds(pl.multiple_of(which * size, size), size)


def start_all(copies):
    for copy in copies:
        copy.start()
    return copies


def wait_all(copies):
    for copy in copies:
        copy.wait()


def block_rows(index, size):
    return slice(index * size, (index + 1) * size)


def pack_kernel(
    where_ref,
    x_mine_ref,
    x_other_ref,
    b_ref,
    c_ref,
    steps_ref,
    mine_ref,
    other_ref,
    straight_ref,
    cross_ref,
):
    tokens, states = b_ref.shape
    half = x_mine_ref.shape[1]
    heads = steps_ref.shape[0] // 4
    member = where_ref[0]
    triangle = causal_mask(tokens).astype(f32).astype(bf16)
    step = steps_ref[: 2 * heads, :].T
    decay = steps_ref[2 * heads :, :].T
    cumul = exact_dot(triangle, decay)
    total = cumul[tokens - 1 : tokens, :]
    scale = jnp.exp(total - cumul) * step
    kept = jnp.exp(total)

    def pick(value, which):
        return jnp.where(which == 0, value[:, :heads], value[:, heads:])

    other_ref[:, :half] = x_other_ref[...]
    for out_ref, base, which in ((mine_ref, 0, member), (other_ref, half, 1 - member)):
        out_ref[:, base : base + states] = b_ref[...]
        out_ref[:, base + states : base + 2 * states] = c_ref[...]
        base += 2 * states
        out_ref[:, base:] = jnp.zeros((tokens, out_ref.shape[1] - base), bf16)
        terms = parts_of(pick(step, which), 3) + parts_of(pick(decay, which), 3)
        for index, term in enumerate(terms):
            out_ref[:, base + index * heads : base + (index + 1) * heads] = term
    expand = expansion(heads)
    for out_ref, x_ref, which in (
        (straight_ref, x_mine_ref, member),
        (cross_ref, x_other_ref, 1 - member),
    ):
        wide = spread(pick(scale, which), expand)
        weighted = (x_ref[...].astype(f32) * wide).astype(bf16)
        for index in range(half // LANES):
            out_ref[block_rows(index, tokens), :] = weighted[:, block_rows(index, LANES)]
        for index in range(states // LANES):
            out_ref[block_rows(half // LANES + index, tokens), :] = b_ref[
                :, block_rows(index, LANES)
            ]
        base = (half + states) // LANES * tokens
        rows = out_ref.shape[0] - base
        out_ref[base:, :] = jnp.zeros((rows, LANES), bf16)
        for index, term in enumerate(parts_of(pick(kept, which), 2)):
            out_ref[base:, block_rows(index, heads)] = jnp.broadcast_to(term, (rows, heads))


def expansion(heads):
    shape = (heads, heads * P_SIZE)
    row = lax.broadcasted_iota(jnp.int32, shape, 0)
    col = lax.broadcasted_iota(jnp.int32, shape, 1)
    return ((col >= row * P_SIZE) & (col < (row + 1) * P_SIZE)).astype(f32).astype(bf16)


def pair_kernel(
    where_ref,
    x_ref,
    meta_ref,
    msg_ref,
    skip_ref,
    own_ref,
    far_ref,
    c_pair_ref,
    x_both,
    b_both,
    step_both,
    decay_both,
):
    tokens, half = x_ref.shape
    states = c_pair_ref.shape[1]
    heads = half // P_SIZE
    member = where_ref[0]
    for which, x, meta in (
        (member, x_ref, meta_ref),
        (1 - member, msg_ref.at[:, :half], msg_ref.at[:, half:]),
    ):
        rows = half_at(which, tokens)
        x_both[rows, :] = x[...]
        b_both[rows, :] = meta[:, :states]
        c_pair_ref[rows, :] = meta[:, states : 2 * states]
        for index, both in enumerate((step_both, decay_both)):
            base = 2 * states + 3 * index * heads
            terms = [
                meta[:, base + term * heads : base + (term + 1) * heads].astype(f32)
                for term in range(3)
            ]
            both[rows, :] = (terms[2] + terms[1]) + terms[0]

    span = 2 * tokens
    causal = causal_mask(span)
    inner = jnp.where(causal, dot_nt(c_pair_ref[...], b_both[...]), 0.0)
    cumul = exact_dot(causal.astype(f32).astype(bf16), decay_both[...])
    cumul_t = cumul.T
    step_t = step_both[...].T
    skip = skip_ref[:, half_at(member, half)]
    expand = expansion(heads)
    reach = parts_of(jnp.exp(cumul), 2)
    first = lax.broadcasted_iota(jnp.int32, (tokens, 2 * P_SIZE), 1) < P_SIZE
    for pair in range(heads // 2):
        at = slice(pair * 2 * P_SIZE, (pair + 1) * 2 * P_SIZE)
        spans = []
        for block in range(2):
            x_block = x_both[block * tokens : (block + 1) * tokens, at]
            zero = jnp.zeros_like(x_block)
            spans.append((jnp.where(first, x_block, zero), jnp.where(first, zero, x_block)))
        for block in range(2):
            rows = slice(block * tokens, (block + 1) * tokens)
            mixings, values = [], []
            for place, head in enumerate((2 * pair, 2 * pair + 1)):
                for earlier in range(block + 1):
                    cols = slice(earlier * tokens, (earlier + 1) * tokens)
                    differ = cumul[rows, head : head + 1] - cumul_t[head : head + 1, cols]
                    if earlier == block:
                        differ = jnp.where(causal[:tokens, :tokens], differ, 0.0)
                    ratio = jnp.exp(differ)
                    mixings.append(
                        (ratio * (inner[rows, cols] * step_t[head : head + 1, cols])).astype(bf16)
                    )
                    values.append(spans[earlier][place])
            own = dot(jnp.concatenate(mixings, axis=1), jnp.concatenate(values, axis=0))
            own_ref[rows, at] = own + x_both[rows, at].astype(f32) * skip[:, at]
            far_ref[rows, at] = sum(dot(term[rows, :], expand[:, at]) for term in reach)


def gate_mix_kernel(count, pieces, *refs):
    sent = refs[: 2 * count]
    where_ref, gate_ref, gate_pair_ref, c_ref, own_ref, far_ref, gain_ref, table_ref = refs[
        2 * count : -3
    ]
    out_refs, gate_both = refs[-3:-1], refs[-1]
    span, half = own_ref.shape
    tokens = span // 2
    states = c_ref.shape[1]
    heads = half // P_SIZE
    member = where_ref[0]
    c_pair = c_ref[...]
    expand = expansion(heads)

    for which, gate in ((member, gate_ref), (1 - member, gate_pair_ref)):
        gate_both[half_at(which, tokens), :] = gate[...]

    def columns(ref, start, size):
        blocks = range(start // LANES, (start + size) // LANES)
        return jnp.concatenate([ref[block_rows(index, tokens), :] for index in blocks], axis=1)

    def kept(ref):
        base = (half + states) // LANES * tokens
        high, low = (ref[base:, block_rows(index, heads)] for index in range(2))
        return (dot(high, expand) + dot(low, expand))[:1, :]

    inners = [dot_nt(c_pair, columns(ref, half, states)).astype(bf16) for ref in sent]
    factors, pair_kept = [], []
    for k in range(count):
        one, two = kept(sent[2 * k]), kept(sent[2 * k + 1])
        pair_kept.append(one * two)
        factors += [jnp.where(member == 0, two, 1.0), jnp.where(member == 0, 1.0, one)]
    gain = gain_ref[:, half_at(member, half)]
    table = table_ref[...]
    parts = []
    norm_width = NORM_HEADS * P_SIZE
    for start in range(0, half, norm_width):
        pres = []
        square = jnp.zeros((span, 1), f32)
        for begin in range(start, start + norm_width, H_BLOCK):
            at = slice(begin, begin + H_BLOCK)
            pre = own_ref[:, at]
            carried = None
            for k in reversed(range(count)):
                term = 0.0
                for j in (2 * k, 2 * k + 1):
                    term = term + factors[j][:, at] * dot(
                        inners[j], columns(sent[j], begin, H_BLOCK)
                    )
                carried = term if carried is None else term + pair_kept[k][:, at] * carried
            if carried is not None:
                pre = pre + far_ref[:, at] * carried
            gate = gate_both[:, at].astype(f32)
            pre = pre * (gate / (1.0 + jnp.exp(-gate)))
            square = square + jnp.sum(pre * pre, axis=1, keepdims=True)
            pres.append(pre)
        inverse = lax.rsqrt(square * (1.0 / norm_width) + norm_eps)
        for index, pre in enumerate(pres):
            at = slice(start + index * H_BLOCK, start + (index + 1) * H_BLOCK)
            parts.append(dot((pre * inverse * gain[:, at]).astype(bf16), table))
    butterflies(parts)
    size = span // pieces
    for index, part in enumerate(parts):
        at = slice(index * H_BLOCK, (index + 1) * H_BLOCK)
        part = part.astype(bf16)
        for piece in range(pieces):
            to = slice(piece // 2 * size, (piece // 2 + 1) * size)
            out_refs[piece % 2][to, at] = part[piece * size : (piece + 1) * size, :]


def butterflies(parts):
    span = 1
    while span < len(parts):
        for low in range(len(parts)):
            if low & span == 0:
                a, b = parts[low], parts[low + span]
                parts[low], parts[low + span] = a + b, a - b
        span *= 2


def add_kernel(sign_ref, mixed_ref, received_ref, out_ref):
    sign = sign_ref[0].astype(f32)
    out_ref[...] = (mixed_ref[...].astype(f32) * sign + received_ref[...].astype(f32)).astype(bf16)


def project_kernel(pairs, where_ref, weight_ref, *refs):
    pieces = refs[: 2 * pairs]
    up_ref, down_ref, out_ref, weight_own, scaled, sums, sems = refs[2 * pairs :]
    rows, half = pieces[0].shape
    sign = (1 - 2 * where_ref[0]).astype(f32)
    sub_count, chan_count, _, blocks, size, features = out_ref.shape
    bounds = [half * eighth // 4 for eighth in (0, 2, 4, 6, 7, 8)]
    spans = [slice(*ends) for ends in zip(bounds, bounds[1:])]
    copies = start_all(
        [
            pltpu.make_async_copy(weight_ref.at[at, :], weight_own.at[at, :], sems.at[index])
            for index, at in enumerate(spans)
        ]
    )
    for start in range(0, half, H_BLOCK):
        inner = slice(start, start + H_BLOCK)
        for pair in range(pairs):
            one = pieces[2 * pair][:, inner].astype(f32)
            two = pieces[2 * pair + 1][:, inner].astype(f32)
            for side, mixed in enumerate((one + two, (one - two) * sign)):
                at = slice(side * half + start, side * half + start + H_BLOCK)
                quant = jnp.clip(mixed * up_ref[:, at], -clip_level, clip_level).astype(bf16)
                scaled[pair * rows : (pair + 1) * rows, at] = (
                    quant.astype(f32) * down_ref[:, at]
                ).astype(bf16)
    for index, (copy, at) in enumerate(zip(copies, spans)):
        copy.wait()
        term = dot(scaled[:, at], weight_own[at, :])
        if index == 0:
            sums[...] = term
        elif index < len(spans) - 1:
            sums[...] += term
        else:
            total = (sums[...] + term).astype(bf16)
    row = 0
    for pair in range(pairs):
        for block in range(blocks):
            for chan in range(chan_count):
                for sub in range(sub_count):
                    out_ref[sub, chan, pair, block] = total[row : row + size, :]
                    row += size


def place_kernel(where_ref, *refs):
    out_ref = refs[-1]
    features = refs[0].shape[1]
    for distance, ref in enumerate(refs[:-1]):
        out_ref[:, half_at(where_ref[0] ^ distance, features)] = ref[...]


def sylvester(order):
    table = np.ones((1, 1), np.float32)
    while table.shape[0] < order:
        table = np.block([[table, table], [table, -table]])
    return table


def shift_up(value, axis, distance):
    count = lax.axis_size(axis)
    return lax.ppermute(value, axis, [(k, k + distance) for k in range(count - distance)])


def turn(value, axis, distance):
    count = lax.axis_size(axis)
    return lax.ppermute(value, axis, [(k, (k + distance) % count) for k in range(count)])


def swap(value, axis, bit):
    count = lax.axis_size(axis)
    return lax.ppermute(value, axis, [(k, k ^ (1 << bit)) for k in range(count)])


def bits_of(axis):
    return range(lax.axis_size(axis).bit_length() - 1)


def halve(value, axis):
    here = lax.axis_index(axis)
    for bit in reversed(bits_of(axis)):
        pair = value.reshape((2, value.shape[0] // 2) + value.shape[1:])
        mine = here // 2**bit % 2
        keep = lax.dynamic_index_in_dim(pair, mine, 0, keepdims=False)
        give = lax.dynamic_index_in_dim(pair, 1 - mine, 0, keepdims=False)
        value = (keep.astype(f32) + swap(give, axis, bit).astype(f32)).astype(bf16)
    return value[0]


def call(kernel, out_shape, name, args, scalars=0, anywhere=0, scratch=(), params=PARAMS, cost=COST):
    specs = [pl.BlockSpec(memory_space=pltpu.SMEM)] * scalars
    specs += [pl.BlockSpec(memory_space=pltpu.HBM)] * anywhere
    specs += [pl.BlockSpec(memory_space=pltpu.VMEM)] * (len(args) - scalars - anywhere)
    return pl.pallas_call(
        kernel,
        out_shape=out_shape,
        in_specs=specs,
        scratch_shapes=scratch,
        compiler_params=params,
        cost_estimate=cost,
        name=name,
    )(*args)


def swap_seq(value, distance):
    count = lax.axis_size("seq")
    return lax.ppermute(value, "seq", [(k, k ^ distance) for k in range(count)])


def paired_body(
    x_in,
    b_in,
    c_in,
    step_size,
    log_decay,
    skip,
    gate_in,
    norm_gain,
    walsh_sign,
    channel_shift_power,
    out_weight,
):
    tokens, width = x_in.shape
    heads = step_size.shape[1]
    states = b_in.shape[2]
    half, half_heads = width // 2, heads // 2
    seq_count, chan_count, sub_count = (lax.axis_size(a) for a in ("seq", "chan", "sub"))
    pairs = seq_count // 2
    here = lax.axis_index("seq")
    member = here % 2
    group_local = lax.axis_index("sub") * heads // (LOCAL_HEADS // G)
    where = jnp.full((1,), member, jnp.int32)
    b_group = lax.dynamic_index_in_dim(b_in, group_local, 1, keepdims=False)
    c_group = lax.dynamic_index_in_dim(c_in, group_local, 1, keepdims=False)
    table = jnp.asarray(sylvester(H_BLOCK), bf16)

    def shape(rows, columns, kind):
        return jax.ShapeDtypeStruct((rows, columns), kind)

    def padded(columns):
        return pl.cdiv(columns, LANES) * LANES

    def half_of(value, which):
        return lax.dynamic_slice_in_dim(value, which * half, half, 1)

    x_mine, x_other = half_of(x_in, member), half_of(x_in, 1 - member)
    gate_mine, gate_other = half_of(gate_in, member), half_of(gate_in, 1 - member)
    steps = jnp.concatenate([step_size.T, log_decay.T], axis=0)
    with_pair = shape(tokens, 2 * states + padded(6 * half_heads), bf16)
    with_later = shape((half + states) // LANES * tokens + 16, LANES, bf16)
    meta_mine, to_pair, straight, cross = call(
        pack_kernel,
        (with_pair, shape(tokens, half + with_pair.shape[1], bf16), with_later, with_later),
        "pack",
        (where, x_mine, x_other, b_group, c_group, steps),
        1,
    )
    sent = []
    for ahead in range(1, pairs):
        firsts = range(seq_count - 2 * ahead)
        sent.append(lax.ppermute(straight, "seq", [(k, k + 2 * ahead) for k in firsts]))
        sent.append(lax.ppermute(cross, "seq", [(k, (k ^ 1) + 2 * ahead) for k in firsts]))
    from_pair, gate_pair = swap_seq(to_pair, 1), swap_seq(gate_other, 1)

    span = 2 * tokens
    own, far, c_pair = call(
        pair_kernel,
        (
            shape(span, half, f32),
            shape(span, half, f32),
            shape(span, states, bf16),
        ),
        "pair",
        (
            where,
            x_mine,
            meta_mine,
            from_pair,
            jnp.repeat(skip, P_SIZE)[None, :],
        ),
        1,
        0,
        (
            pltpu.VMEM((span, half), bf16),
            pltpu.VMEM((span, states), bf16),
            pltpu.VMEM((span, half_heads), f32),
            pltpu.VMEM((span, half_heads), f32),
        ),
        cost=SMALL,
    )
    signed_gain = (jnp.where(walsh_sign == 1, 1.0, -1.0) * norm_gain)[None, :]
    owners = chan_count * sub_count
    size = tokens // (2 * owners)
    count = len(sent) // 2
    chunks = pl.pallas_call(
        functools.partial(gate_mix_kernel, count, span // size),
        out_shape=(shape(tokens, half, bf16),) * 2,
        in_specs=[pl.BlockSpec(memory_space=pltpu.VMEM)] * (2 * count)
        + [pl.BlockSpec(memory_space=pltpu.SMEM)]
        + [pl.BlockSpec(memory_space=pltpu.VMEM)] * 7,
        scratch_shapes=[pltpu.VMEM((span, half), bf16)],
        compiler_params=PARAMS,
        cost_estimate=COST,
        name="mix",
    )(*sent, where, gate_mine, gate_pair, c_pair, own, far, signed_gain, table)

    def add_across(mixed, axis, bit, received):
        place = lax.axis_index(axis)
        sign = 1.0 - 2.0 * (place // 2**bit % 2).astype(f32)
        return (mixed.astype(f32) * sign + received.astype(f32)).astype(bf16)

    def across(mixed, axis):
        for bit in bits_of(axis):
            mixed = add_across(mixed, axis, bit, swap(mixed, axis, bit))
        return mixed

    first, second = (across(chunk, "sub") for chunk in chunks)
    ahead = range(1, pairs)
    cut = tokens * 3 // 4
    near_second = swap_seq(second, 1)
    far_early = [swap_seq(second[:cut], 2 * k) for k in ahead]
    bits = bits_of("chan")
    halves = [first[: tokens // 2], first[tokens // 2 :]]
    for bit in bits[:-1]:
        halves = [add_across(value, "chan", bit, swap(value, "chan", bit)) for value in halves]
    received = [swap(value, "chan", bits[-1]) for value in halves if bits]
    halves, received, second, near_second, far_early = lax.optimization_barrier(
        (halves, received, second, near_second, far_early)
    )
    if bits:
        halves = [add_across(*pair[:1], "chan", bits[-1], pair[1]) for pair in zip(halves, received)]
    first = jnp.concatenate(halves, axis=0)
    moving = [second[:cut], second[cut:], *far_early]
    for bit in bits[:-1]:
        moving = [add_across(value, "chan", bit, swap(value, "chan", bit)) for value in moving]
    received = [swap(value, "chan", bits[-1]) for value in moving if bits]
    far_first = [swap_seq(first, 2 * k) for k in ahead]
    near_first = swap_seq(first, 1)
    first, near_second, moving, received, far_first, near_first = lax.optimization_barrier(
        (first, near_second, moving, received, far_first, near_first)
    )
    if bits:
        sign = jnp.full((1,), 1 - 2 * (lax.axis_index("chan") // 2 ** bits[-1] % 2), jnp.int32)
        moving = [
            call(add_kernel, shape(*mixed.shape, bf16), "add", (sign, mixed, other), 1)
            for mixed, other in zip(moving, received)
        ]
    early, late, *far_early = moving
    passed_first = [swap_seq(value, 1) for value in far_first]
    all_first = [first, near_first]
    for far, passed in zip(far_first, passed_first):
        all_first += [far, passed]
    all_first, far_early = lax.optimization_barrier((all_first, far_early))
    passed_early = [swap_seq(value, 1) for value in far_early]
    far_late = [swap_seq(late, 2 * k) for k in ahead]
    cross_late = [swap_seq(late, 2 * k + 1) for k in ahead]
    near_second = across(near_second, "chan")

    up = (power_two(channel_shift_power, 1) * (1.0 / math.sqrt(LOCAL_HEADS * P_SIZE)))[None, :]
    down = power_two(channel_shift_power, -1)[None, :]
    features = out_weight.shape[1]

    def project(pieces):
        return call(
            functools.partial(project_kernel, pairs),
            jax.ShapeDtypeStruct((sub_count, chan_count, pairs, 2, size, features), bf16),
            "project",
            (where, out_weight, *pieces, up, down),
            1,
            1,
            (
                pltpu.VMEM(out_weight.shape, bf16),
                pltpu.VMEM((pairs * tokens, width), bf16),
                pltpu.VMEM((pairs * tokens, features), f32),
                pltpu.SemaphoreType.DMA((5,)),
            ),
            WIDE_PARAMS,
        )

    go = lax.optimization_barrier(jnp.bool_(True))

    def stage(pieces):
        return lax.cond(
            go,
            lambda *pieces: halve(project(pieces), "sub"),
            lambda *_: jnp.zeros((chan_count, pairs, 2, size, features), bf16),
            *pieces,
        )

    done_first = stage(all_first)
    done_first, near_second, far_late, cross_late, passed_early = lax.optimization_barrier(
        (done_first, near_second, far_late, cross_late, passed_early)
    )
    all_second = [jnp.concatenate([early, late], axis=0), near_second]
    for parts in zip(far_early, far_late, passed_early, cross_late):
        all_second += [jnp.concatenate(parts[:2], axis=0), jnp.concatenate(parts[2:], axis=0)]
    done_first, done_second = lax.optimization_barrier(
        (halve(done_first, "chan"), stage(all_second))
    )
    done_second = halve(done_second, "chan")
    summed = jnp.stack([done_first, done_second], axis=2)
    returned = []
    for distance in range(seq_count):
        block = (member + distance) % 2
        value = lax.dynamic_index_in_dim(summed[distance // 2], block, 0, keepdims=False)
        value = value.reshape(2 * size, features)
        returned.append(swap_seq(value, distance) if distance else value)
    return call(
        place_kernel,
        shape(2 * size, seq_count * features, bf16),
        "place",
        (jnp.full((1,), here, jnp.int32), *returned),
        1,
    )


def body(x_in, b_in, c_in, step_size, *rest):
    tokens, heads = step_size.shape
    seq_count = lax.axis_size("seq")
    pieces = 2 * lax.axis_size("chan") * lax.axis_size("sub")
    if (
        heads % (2 * NORM_HEADS) == 0
        and seq_count % 2 == 0
        and seq_count & (seq_count - 1) == 0
        and tokens % (16 * pieces) == 0
    ):
        return paired_body(x_in, b_in, c_in, step_size, *rest)
    return plain_body(x_in, b_in, c_in, step_size, *rest)


def plain_body(
    x_in,
    b_in,
    c_in,
    step_size,
    log_decay,
    skip,
    gate_in,
    norm_gain,
    walsh_sign,
    channel_shift_power,
    out_weight,
):
    tokens, width = x_in.shape
    heads = step_size.shape[1]
    states = b_in.shape[2]
    seq_count = lax.axis_size("seq")
    sub_index = lax.axis_index("sub")
    group_local = sub_index * heads // (LOCAL_HEADS // G)
    b_group = lax.dynamic_slice_in_dim(b_in, group_local, 1, 1)[:, 0, :]
    c_group = lax.dynamic_slice_in_dim(c_in, group_local, 1, 1)[:, 0, :]
    expand = jnp.asarray(np.kron(np.eye(heads), np.ones((1, P_SIZE))), bf16)
    table = jnp.asarray(sylvester(H_BLOCK), bf16)

    tail = pl.cdiv(2 * heads, LANES) * LANES
    message, cumul = pl.pallas_call(
        message_kernel,
        out_shape=(
            jax.ShapeDtypeStruct((tokens, width + states + tail), bf16),
            jax.ShapeDtypeStruct((tokens, heads), f32),
        ),
        compiler_params=PARAMS,
        name="message",
    )(x_in, b_group, step_size, log_decay, expand)
    arrived = [shift_up(message, "seq", k) for k in range(1, seq_count)]

    wide_skip = jnp.repeat(skip, P_SIZE)[None, :]
    own, far = pl.pallas_call(
        local_kernel,
        out_shape=(
            jax.ShapeDtypeStruct((tokens, width), f32),
            jax.ShapeDtypeStruct((tokens, width), f32),
        ),
        compiler_params=PARAMS,
        name="local",
    )(x_in, b_group, c_group, step_size, cumul, gate_in, wide_skip, expand)

    signed_gain = (jnp.where(walsh_sign == 1, 1.0, -1.0) * norm_gain)[None, :]
    mixed = pl.pallas_call(
        functools.partial(mix_kernel, len(arrived)),
        out_shape=jax.ShapeDtypeStruct((tokens, width), bf16),
        compiler_params=PARAMS,
        name="mix",
    )(*arrived, c_group, own, far, signed_gain, table, expand)

    for axis in ("sub", "chan"):
        here = lax.axis_index(axis)
        for bit in bits_of(axis):
            other = swap(mixed.astype(bf16), axis, bit).astype(f32)
            sign = 1.0 - 2.0 * (here // 2**bit % 2).astype(f32)
            mixed = mixed.astype(f32) * sign + other
    rotated = mixed * (1.0 / math.sqrt(LOCAL_HEADS * P_SIZE))
    quant = jnp.clip(
        rotated * power_two(channel_shift_power, 1)[None, :], -clip_level, clip_level
    ).astype(bf16)
    scaled = (quant.astype(f32) * power_two(channel_shift_power, -1)[None, :]).astype(bf16)

    chan_count, sub_count = lax.axis_size("chan"), lax.axis_size("sub")
    rows = tokens // (chan_count * sub_count)
    order = sorted(range(1, seq_count), key=lambda k: -min(k, seq_count - k))
    blocks = {0: scaled}
    for k in order:
        blocks[k] = turn(scaled, "seq", k)
    sums = []
    for k in [0] + order:
        partial = dot(blocks[k], out_weight).astype(bf16)
        partial = partial.reshape(chan_count, sub_count, rows, -1)
        partial = halve(jnp.swapaxes(partial, 0, 1), "sub")
        done = halve(partial, "chan")
        sums.append((k, turn(done, "seq", -k % seq_count) if k else done))
    pieces = [value for _, value in sorted(sums, key=lambda item: item[0])]
    stacked = jnp.stack(pieces + pieces, axis=0)
    here = lax.axis_index("seq")
    placed = lax.dynamic_slice_in_dim(
        stacked, (seq_count - here) % seq_count, seq_count, 0
    )
    return jnp.swapaxes(placed, 0, 1).reshape(rows, -1)


def solution(mesh):
    return jax.shard_map(
        body,
        mesh=mesh,
        in_specs=(
            P(("groups", "seq"), ("chan", "sub")),
            P(("groups", "seq"), "chan", None),
            P(("groups", "seq"), "chan", None),
            P(("groups", "seq"), ("chan", "sub")),
            P(("groups", "seq"), ("chan", "sub")),
            P(("chan", "sub")),
            P(("groups", "seq"), ("chan", "sub")),
            P(("chan", "sub")),
            P(("chan", "sub")),
            P(("chan", "sub")),
            P(("chan", "sub"), "seq"),
        ),
        out_specs=P(("groups", "seq", "chan", "sub"), None),
        check_vma=False,
    )
```

```python
import functools
import math

import jax
import jax.numpy as jnp
import numpy as np
from jax import lax
from jax.experimental import pallas as pl
from jax.experimental.pallas import tpu as pltpu
from jax.sharding import PartitionSpec as P

LOCAL_HEADS = 128
P_SIZE = 64
G = 4
NORM_HEADS = 16


norm_eps = 1e-05
clip_level = 4.0
expo_levels = (-1, 0, 1, 2, 3)
LANES = 128
H_BLOCK = 256
COST = pl.CostEstimate(flops=1, transcendentals=0, bytes_accessed=30_000_000)
SMALL = pl.CostEstimate(flops=1, transcendentals=0, bytes_accessed=1)
f32 = jnp.float32
bf16 = jnp.bfloat16
PARAMS = pltpu.CompilerParams(vmem_limit_bytes=16 * 2**20)
WIDE_PARAMS = pltpu.CompilerParams(vmem_limit_bytes=16 * 2**20)


def power_two(expo, sign_flip):
    result = jnp.zeros(expo.shape, jnp.float32)
    for level in expo_levels:
        result = result + jnp.where(
            expo == level, jnp.float32(2.0 ** (sign_flip * level)), jnp.float32(0.0)
        )
    return result


def dot(a, b):
    return jnp.dot(a, b, preferred_element_type=f32)


def dot_nt(a, b):
    return lax.dot_general(a, b, (((1,), (1,)), ((), ())), preferred_element_type=f32)


def parts_of(value, count):
    terms = []
    for _ in range(count):
        term = value.astype(bf16)
        terms.append(term)
        value = value - term.astype(f32)
    return terms


def exact_dot(exact, value, count=3):
    return sum(dot(exact, term) for term in parts_of(value, count))


def spread(value, expand, count=2):
    return sum(dot(term, expand) for term in parts_of(value, count))


def causal_mask(size):
    row = lax.broadcasted_iota(jnp.int32, (size, size), 0)
    col = lax.broadcasted_iota(jnp.int32, (size, size), 1)
    return row >= col


def message_kernel(x_ref, b_ref, step_ref, decay_ref, expand_ref, msg_ref, cumul_ref):
    tokens, width = x_ref.shape
    heads = step_ref.shape[1]
    states = b_ref.shape[1]
    expand = expand_ref[...]
    triangle = causal_mask(tokens).astype(f32).astype(bf16)
    cumul = exact_dot(triangle, decay_ref[...])
    cumul_ref[...] = cumul
    total = cumul[tokens - 1 : tokens, :]
    scale = spread(jnp.exp(total - cumul) * step_ref[...], expand)
    msg_ref[:, :width] = (x_ref[...].astype(f32) * scale).astype(bf16)
    msg_ref[:, width : width + states] = b_ref[...]
    high, low = parts_of(jnp.exp(total), 2)
    base = width + states
    msg_ref[:, base:] = jnp.zeros((tokens, msg_ref.shape[1] - base), bf16)
    msg_ref[:, base : base + heads] = jnp.broadcast_to(high, (tokens, heads))
    msg_ref[:, base + heads : base + 2 * heads] = jnp.broadcast_to(low, (tokens, heads))


def local_kernel(
    x_ref, b_ref, c_ref, step_ref, cumul_ref, gate_ref, skip_ref, expand_ref, own_ref, far_ref
):
    tokens, width = x_ref.shape
    heads = step_ref.shape[1]
    causal = causal_mask(tokens)
    inner = dot_nt(c_ref[...], b_ref[...])
    cumul = cumul_ref[...]
    cumul_t = cumul.T
    step_t = step_ref[...].T
    first = lax.broadcasted_iota(jnp.int32, (tokens, 2 * P_SIZE), 1) < P_SIZE
    for pair in range(heads // 2):
        mixings = []
        for head in (2 * pair, 2 * pair + 1):
            differ = cumul[:, head : head + 1] - cumul_t[head : head + 1, :]
            ratio = jnp.exp(jnp.where(causal, differ, -jnp.inf))
            mixings.append((ratio * (inner * step_t[head : head + 1, :])).astype(bf16))
        at = slice(pair * 2 * P_SIZE, (pair + 1) * 2 * P_SIZE)
        x_pair = x_ref[:, at]
        zero = jnp.zeros_like(x_pair)
        blocks = jnp.concatenate(
            [jnp.where(first, x_pair, zero), jnp.where(first, zero, x_pair)], axis=0
        )
        own = dot(jnp.concatenate(mixings, axis=1), blocks)
        own = own + x_pair.astype(f32) * skip_ref[:, at]
        gate = gate_ref[:, at].astype(f32)
        own_ref[:, at] = own * (gate / (1.0 + jnp.exp(-gate)))
    reach = jnp.exp(cumul)
    tile = min(width, 512)
    for start in range(0, width, tile):
        at = slice(start, start + tile)
        gate = gate_ref[:, at].astype(f32)
        far_ref[:, at] = spread(reach, expand_ref[:, at]) * (gate / (1.0 + jnp.exp(-gate)))


def mix_kernel(count, *refs):
    messages = refs[:count]
    c_ref, own_ref, far_ref, gain_ref, table_ref, expand_ref, out_ref = refs[count:]
    tokens, width = own_ref.shape
    states = c_ref.shape[1]
    heads = expand_ref.shape[0]
    base = width + states
    c_group = c_ref[...]
    inners = []
    decays = []
    for msg_ref in messages:
        inners.append(dot_nt(c_group, msg_ref[:, width:base]).astype(bf16))
        decay = dot(msg_ref[:16, base : base + heads], expand_ref[...]) + dot(
            msg_ref[:16, base + heads : base + 2 * heads], expand_ref[...]
        )
        decays.append(decay[:1, :])
    norm_width = NORM_HEADS * P_SIZE
    table = table_ref[...]
    parts = []
    for start in range(0, width, norm_width):
        pres = []
        square = jnp.zeros((tokens, 1), f32)
        for begin in range(start, start + norm_width, H_BLOCK):
            at = slice(begin, begin + H_BLOCK)
            carried = None
            for k in reversed(range(count)):
                term = dot(inners[k], messages[k][:, at])
                carried = term if carried is None else term + decays[k][:, at] * carried
            pre = own_ref[:, at]
            if carried is not None:
                pre = pre + far_ref[:, at] * carried
            square = square + jnp.sum(pre * pre, axis=1, keepdims=True)
            pres.append(pre)
        inverse = lax.rsqrt(square * (1.0 / norm_width) + norm_eps)
        for index, pre in enumerate(pres):
            at = slice(start + index * H_BLOCK, start + (index + 1) * H_BLOCK)
            signed = (pre * inverse * gain_ref[:, at]).astype(bf16)
            parts.append(dot(signed, table))
    butterflies(parts)
    for index, part in enumerate(parts):
        out_ref[:, index * H_BLOCK : (index + 1) * H_BLOCK] = part.astype(bf16)


def half_at(which, size):
    return pl.ds(pl.multiple_of(which * size, size), size)


def start_all(copies):
    for copy in copies:
        copy.start()
    return copies


def wait_all(copies):
    for copy in copies:
        copy.wait()


def block_rows(index, size):
    return slice(index * size, (index + 1) * size)


def pack_kernel(
    where_ref,
    x_mine_ref,
    x_other_ref,
    b_ref,
    c_ref,
    steps_ref,
    mine_ref,
    other_ref,
    straight_ref,
    cross_ref,
):
    tokens, states = b_ref.shape
    half = x_mine_ref.shape[1]
    heads = steps_ref.shape[0] // 4
    member = where_ref[0]
    triangle = causal_mask(tokens).astype(f32).astype(bf16)
    step = steps_ref[: 2 * heads, :].T
    decay = steps_ref[2 * heads :, :].T
    cumul = exact_dot(triangle, decay)
    total = cumul[tokens - 1 : tokens, :]
    scale = jnp.exp(total - cumul) * step
    kept = jnp.exp(total)

    def pick(value, which):
        return jnp.where(which == 0, value[:, :heads], value[:, heads:])

    other_ref[:, :half] = x_other_ref[...]
    for out_ref, base, which in ((mine_ref, 0, member), (other_ref, half, 1 - member)):
        out_ref[:, base : base + states] = b_ref[...]
        out_ref[:, base + states : base + 2 * states] = c_ref[...]
        base += 2 * states
        out_ref[:, base:] = jnp.zeros((tokens, out_ref.shape[1] - base), bf16)
        terms = parts_of(pick(step, which), 3) + parts_of(pick(decay, which), 3)
        for index, term in enumerate(terms):
            out_ref[:, base + index * heads : base + (index + 1) * heads] = term
    expand = expansion(heads)
    for out_ref, x_ref, which in (
        (straight_ref, x_mine_ref, member),
        (cross_ref, x_other_ref, 1 - member),
    ):
        wide = spread(pick(scale, which), expand)
        weighted = (x_ref[...].astype(f32) * wide).astype(bf16)
        for index in range(half // LANES):
            out_ref[block_rows(index, tokens), :] = weighted[:, block_rows(index, LANES)]
        for index in range(states // LANES):
            out_ref[block_rows(half // LANES + index, tokens), :] = b_ref[
                :, block_rows(index, LANES)
            ]
        base = (half + states) // LANES * tokens
        rows = out_ref.shape[0] - base
        out_ref[base:, :] = jnp.zeros((rows, LANES), bf16)
        for index, term in enumerate(parts_of(pick(kept, which), 2)):
            out_ref[base:, block_rows(index, heads)] = jnp.broadcast_to(term, (rows, heads))


def expansion(heads):
    shape = (heads, heads * P_SIZE)
    row = lax.broadcasted_iota(jnp.int32, shape, 0)
    col = lax.broadcasted_iota(jnp.int32, shape, 1)
    return ((col >= row * P_SIZE) & (col < (row + 1) * P_SIZE)).astype(f32).astype(bf16)


def pair_kernel(
    where_ref,
    x_ref,
    meta_ref,
    msg_ref,
    skip_ref,
    own_ref,
    far_ref,
    c_pair_ref,
    x_both,
    b_both,
    step_both,
    decay_both,
):
    tokens, half = x_ref.shape
    states = c_pair_ref.shape[1]
    heads = half // P_SIZE
    member = where_ref[0]
    for which, x, meta in (
        (member, x_ref, meta_ref),
        (1 - member, msg_ref.at[:, :half], msg_ref.at[:, half:]),
    ):
        rows = half_at(which, tokens)
        x_both[rows, :] = x[...]
        b_both[rows, :] = meta[:, :states]
        c_pair_ref[rows, :] = meta[:, states : 2 * states]
        for index, both in enumerate((step_both, decay_both)):
            base = 2 * states + 3 * index * heads
            terms = [
                meta[:, base + term * heads : base + (term + 1) * heads].astype(f32)
                for term in range(3)
            ]
            both[rows, :] = (terms[2] + terms[1]) + terms[0]

    span = 2 * tokens
    causal = causal_mask(span)
    inner = jnp.where(causal, dot_nt(c_pair_ref[...], b_both[...]), 0.0)
    cumul = exact_dot(causal.astype(f32).astype(bf16), decay_both[...])
    cumul_t = cumul.T
    step_t = step_both[...].T
    skip = skip_ref[:, half_at(member, half)]
    expand = expansion(heads)
    reach = parts_of(jnp.exp(cumul), 2)
    first = lax.broadcasted_iota(jnp.int32, (tokens, 2 * P_SIZE), 1) < P_SIZE
    for pair in range(heads // 2):
        at = slice(pair * 2 * P_SIZE, (pair + 1) * 2 * P_SIZE)
        spans = []
        for block in range(2):
            x_block = x_both[block * tokens : (block + 1) * tokens, at]
            zero = jnp.zeros_like(x_block)
            spans.append((jnp.where(first, x_block, zero), jnp.where(first, zero, x_block)))
        for block in range(2):
            rows = slice(block * tokens, (block + 1) * tokens)
            mixings, values = [], []
            for place, head in enumerate((2 * pair, 2 * pair + 1)):
                for earlier in range(block + 1):
                    cols = slice(earlier * tokens, (earlier + 1) * tokens)
                    differ = cumul[rows, head : head + 1] - cumul_t[head : head + 1, cols]
                    if earlier == block:
                        differ = jnp.where(causal[:tokens, :tokens], differ, 0.0)
                    ratio = jnp.exp(differ)
                    mixings.append(
                        (ratio * (inner[rows, cols] * step_t[head : head + 1, cols])).astype(bf16)
                    )
                    values.append(spans[earlier][place])
            own = dot(jnp.concatenate(mixings, axis=1), jnp.concatenate(values, axis=0))
            own_ref[rows, at] = own + x_both[rows, at].astype(f32) * skip[:, at]
            far_ref[rows, at] = sum(dot(term[rows, :], expand[:, at]) for term in reach)


def gate_mix_kernel(count, pieces, *refs):
    sent = refs[: 2 * count]
    where_ref, gate_ref, gate_pair_ref, c_ref, own_ref, far_ref, gain_ref, table_ref = refs[
        2 * count : -3
    ]
    out_refs, gate_both = refs[-3:-1], refs[-1]
    span, half = own_ref.shape
    tokens = span // 2
    states = c_ref.shape[1]
    heads = half // P_SIZE
    member = where_ref[0]
    c_pair = c_ref[...]
    expand = expansion(heads)

    for which, gate in ((member, gate_ref), (1 - member, gate_pair_ref)):
        gate_both[half_at(which, tokens), :] = gate[...]

    def columns(ref, start, size):
        blocks = range(start // LANES, (start + size) // LANES)
        return jnp.concatenate([ref[block_rows(index, tokens), :] for index in blocks], axis=1)

    def kept(ref):
        base = (half + states) // LANES * tokens
        high, low = (ref[base:, block_rows(index, heads)] for index in range(2))
        return (dot(high, expand) + dot(low, expand))[:1, :]

    inners = [dot_nt(c_pair, columns(ref, half, states)).astype(bf16) for ref in sent]
    factors, pair_kept = [], []
    for k in range(count):
        one, two = kept(sent[2 * k]), kept(sent[2 * k + 1])
        pair_kept.append(one * two)
        factors += [jnp.where(member == 0, two, 1.0), jnp.where(member == 0, 1.0, one)]
    gain = gain_ref[:, half_at(member, half)]
    table = table_ref[...]
    parts = []
    norm_width = NORM_HEADS * P_SIZE
    for start in range(0, half, norm_width):
        pres = []
        square = jnp.zeros((span, 1), f32)
        for begin in range(start, start + norm_width, H_BLOCK):
            at = slice(begin, begin + H_BLOCK)
            pre = own_ref[:, at]
            carried = None
            for k in reversed(range(count)):
                term = 0.0
                for j in (2 * k, 2 * k + 1):
                    term = term + factors[j][:, at] * dot(
                        inners[j], columns(sent[j], begin, H_BLOCK)
                    )
                carried = term if carried is None else term + pair_kept[k][:, at] * carried
            if carried is not None:
                pre = pre + far_ref[:, at] * carried
            gate = gate_both[:, at].astype(f32)
            pre = pre * (gate / (1.0 + jnp.exp(-gate)))
            square = square + jnp.sum(pre * pre, axis=1, keepdims=True)
            pres.append(pre)
        inverse = lax.rsqrt(square * (1.0 / norm_width) + norm_eps)
        for index, pre in enumerate(pres):
            at = slice(start + index * H_BLOCK, start + (index + 1) * H_BLOCK)
            parts.append(dot((pre * inverse * gain[:, at]).astype(bf16), table))
    butterflies(parts)
    size = span // pieces
    for index, part in enumerate(parts):
        at = slice(index * H_BLOCK, (index + 1) * H_BLOCK)
        part = part.astype(bf16)
        for piece in range(pieces):
            to = slice(piece // 2 * size, (piece // 2 + 1) * size)
            out_refs[piece % 2][to, at] = part[piece * size : (piece + 1) * size, :]


def butterflies(parts):
    span = 1
    while span < len(parts):
        for low in range(len(parts)):
            if low & span == 0:
                a, b = parts[low], parts[low + span]
                parts[low], parts[low + span] = a + b, a - b
        span *= 2


def add_kernel(sign_ref, mixed_ref, received_ref, out_ref):
    sign = sign_ref[0].astype(f32)
    out_ref[...] = (mixed_ref[...].astype(f32) * sign + received_ref[...].astype(f32)).astype(bf16)


def project_kernel(pairs, where_ref, weight_ref, *refs):
    pieces = refs[: 2 * pairs]
    up_ref, down_ref, out_ref, weight_own, scaled, sums, sems = refs[2 * pairs :]
    rows, half = pieces[0].shape
    sign = (1 - 2 * where_ref[0]).astype(f32)
    sub_count, chan_count, _, blocks, size, features = out_ref.shape
    bounds = [half * eighth // 4 for eighth in (0, 2, 4, 6, 7, 8)]
    spans = [slice(*ends) for ends in zip(bounds, bounds[1:])]
    copies = start_all(
        [
            pltpu.make_async_copy(weight_ref.at[at, :], weight_own.at[at, :], sems.at[index])
            for index, at in enumerate(spans)
        ]
    )
    for start in range(0, half, H_BLOCK):
        inner = slice(start, start + H_BLOCK)
        for pair in range(pairs):
            one = pieces[2 * pair][:, inner].astype(f32)
            two = pieces[2 * pair + 1][:, inner].astype(f32)
            for side, mixed in enumerate((one + two, (one - two) * sign)):
                at = slice(side * half + start, side * half + start + H_BLOCK)
                quant = jnp.clip(mixed * up_ref[:, at], -clip_level, clip_level).astype(bf16)
                scaled[pair * rows : (pair + 1) * rows, at] = (
                    quant.astype(f32) * down_ref[:, at]
                ).astype(bf16)
    for index, (copy, at) in enumerate(zip(copies, spans)):
        copy.wait()
        term = dot(scaled[:, at], weight_own[at, :])
        if index == 0:
            sums[...] = term
        elif index < len(spans) - 1:
            sums[...] += term
        else:
            total = (sums[...] + term).astype(bf16)
    row = 0
    for pair in range(pairs):
        for block in range(blocks):
            for chan in range(chan_count):
                for sub in range(sub_count):
                    out_ref[sub, chan, pair, block] = total[row : row + size, :]
                    row += size


def place_kernel(where_ref, *refs):
    out_ref = refs[-1]
    features = refs[0].shape[1]
    for distance, ref in enumerate(refs[:-1]):
        out_ref[:, half_at(where_ref[0] ^ distance, features)] = ref[...]


def sylvester(order):
    table = np.ones((1, 1), np.float32)
    while table.shape[0] < order:
        table = np.block([[table, table], [table, -table]])
    return table


def shift_up(value, axis, distance):
    count = lax.axis_size(axis)
    return lax.ppermute(value, axis, [(k, k + distance) for k in range(count - distance)])


def turn(value, axis, distance):
    count = lax.axis_size(axis)
    return lax.ppermute(value, axis, [(k, (k + distance) % count) for k in range(count)])


def swap(value, axis, bit):
    count = lax.axis_size(axis)
    return lax.ppermute(value, axis, [(k, k ^ (1 << bit)) for k in range(count)])


def bits_of(axis):
    return range(lax.axis_size(axis).bit_length() - 1)


def halve(value, axis):
    here = lax.axis_index(axis)
    for bit in reversed(bits_of(axis)):
        pair = value.reshape((2, value.shape[0] // 2) + value.shape[1:])
        mine = here // 2**bit % 2
        keep = lax.dynamic_index_in_dim(pair, mine, 0, keepdims=False)
        give = lax.dynamic_index_in_dim(pair, 1 - mine, 0, keepdims=False)
        value = (keep.astype(f32) + swap(give, axis, bit).astype(f32)).astype(bf16)
    return value[0]


def call(kernel, out_shape, name, args, scalars=0, anywhere=0, scratch=(), params=PARAMS, cost=COST):
    specs = [pl.BlockSpec(memory_space=pltpu.SMEM)] * scalars
    specs += [pl.BlockSpec(memory_space=pltpu.HBM)] * anywhere
    specs += [pl.BlockSpec(memory_space=pltpu.VMEM)] * (len(args) - scalars - anywhere)
    return pl.pallas_call(
        kernel,
        out_shape=out_shape,
        in_specs=specs,
        scratch_shapes=scratch,
        compiler_params=params,
        cost_estimate=cost,
        name=name,
    )(*args)


def swap_seq(value, distance):
    count = lax.axis_size("seq")
    return lax.ppermute(value, "seq", [(k, k ^ distance) for k in range(count)])


def paired_body(
    x_in,
    b_in,
    c_in,
    step_size,
    log_decay,
    skip,
    gate_in,
    norm_gain,
    walsh_sign,
    channel_shift_power,
    out_weight,
):
    tokens, width = x_in.shape
    heads = step_size.shape[1]
    states = b_in.shape[2]
    half, half_heads = width // 2, heads // 2
    seq_count, chan_count, sub_count = (lax.axis_size(a) for a in ("seq", "chan", "sub"))
    pairs = seq_count // 2
    here = lax.axis_index("seq")
    member = here % 2
    group_local = lax.axis_index("sub") * heads // (LOCAL_HEADS // G)
    where = jnp.full((1,), member, jnp.int32)
    b_group = lax.dynamic_index_in_dim(b_in, group_local, 1, keepdims=False)
    c_group = lax.dynamic_index_in_dim(c_in, group_local, 1, keepdims=False)
    table = jnp.asarray(sylvester(H_BLOCK), bf16)

    def shape(rows, columns, kind):
        return jax.ShapeDtypeStruct((rows, columns), kind)

    def padded(columns):
        return pl.cdiv(columns, LANES) * LANES

    def half_of(value, which):
        return lax.dynamic_slice_in_dim(value, which * half, half, 1)

    x_mine, x_other = half_of(x_in, member), half_of(x_in, 1 - member)
    gate_mine, gate_other = half_of(gate_in, member), half_of(gate_in, 1 - member)
    steps = jnp.concatenate([step_size.T, log_decay.T], axis=0)
    with_pair = shape(tokens, 2 * states + padded(6 * half_heads), bf16)
    with_later = shape((half + states) // LANES * tokens + 16, LANES, bf16)
    meta_mine, to_pair, straight, cross = call(
        pack_kernel,
        (with_pair, shape(tokens, half + with_pair.shape[1], bf16), with_later, with_later),
        "pack",
        (where, x_mine, x_other, b_group, c_group, steps),
        1,
    )
    sent = []
    for ahead in range(1, pairs):
        firsts = range(seq_count - 2 * ahead)
        sent.append(lax.ppermute(straight, "seq", [(k, k + 2 * ahead) for k in firsts]))
        sent.append(lax.ppermute(cross, "seq", [(k, (k ^ 1) + 2 * ahead) for k in firsts]))
    from_pair, gate_pair = swap_seq(to_pair, 1), swap_seq(gate_other, 1)

    span = 2 * tokens
    own, far, c_pair = call(
        pair_kernel,
        (
            shape(span, half, f32),
            shape(span, half, f32),
            shape(span, states, bf16),
        ),
        "pair",
        (
            where,
            x_mine,
            meta_mine,
            from_pair,
            jnp.repeat(skip, P_SIZE)[None, :],
        ),
        1,
        0,
        (
            pltpu.VMEM((span, half), bf16),
            pltpu.VMEM((span, states), bf16),
            pltpu.VMEM((span, half_heads), f32),
            pltpu.VMEM((span, half_heads), f32),
        ),
        cost=SMALL,
    )
    signed_gain = (jnp.where(walsh_sign == 1, 1.0, -1.0) * norm_gain)[None, :]
    owners = chan_count * sub_count
    size = tokens // (2 * owners)
    count = len(sent) // 2
    chunks = pl.pallas_call(
        functools.partial(gate_mix_kernel, count, span // size),
        out_shape=(shape(tokens, half, bf16),) * 2,
        in_specs=[pl.BlockSpec(memory_space=pltpu.VMEM)] * (2 * count)
        + [pl.BlockSpec(memory_space=pltpu.SMEM)]
        + [pl.BlockSpec(memory_space=pltpu.VMEM)] * 7,
        scratch_shapes=[pltpu.VMEM((span, half), bf16)],
        compiler_params=PARAMS,
        cost_estimate=COST,
        name="mix",
    )(*sent, where, gate_mine, gate_pair, c_pair, own, far, signed_gain, table)

    def add_across(mixed, axis, bit, received):
        place = lax.axis_index(axis)
        sign = 1.0 - 2.0 * (place // 2**bit % 2).astype(f32)
        return (mixed.astype(f32) * sign + received.astype(f32)).astype(bf16)

    def across(mixed, axis):
        for bit in bits_of(axis):
            mixed = add_across(mixed, axis, bit, swap(mixed, axis, bit))
        return mixed

    first, second = (across(chunk, "sub") for chunk in chunks)
    ahead = range(1, pairs)
    cut = tokens * 5 // 8
    near_second = swap_seq(second[:cut], 1)
    far_early = [swap_seq(second[:cut], 2 * k) for k in ahead]
    bits = bits_of("chan")
    halves = [first[: tokens // 2], first[tokens // 2 :]]
    for bit in bits[:-1]:
        halves = [add_across(value, "chan", bit, swap(value, "chan", bit)) for value in halves]
    received = [swap(value, "chan", bits[-1]) for value in halves if bits]
    halves, received, second, near_second, far_early = lax.optimization_barrier(
        (halves, received, second, near_second, far_early)
    )
    if bits:
        halves = [add_across(*pair[:1], "chan", bits[-1], pair[1]) for pair in zip(halves, received)]
    first = jnp.concatenate(halves, axis=0)
    moving = [second[:cut], second[cut:], *far_early]
    for bit in bits[:-1]:
        moving = [add_across(value, "chan", bit, swap(value, "chan", bit)) for value in moving]
    received = [swap(value, "chan", bits[-1]) for value in moving if bits]
    far_first = [swap_seq(first, 2 * k) for k in ahead]
    near_first = swap_seq(first, 1)
    first, near_second, moving, received, far_first, near_first = lax.optimization_barrier(
        (first, near_second, moving, received, far_first, near_first)
    )
    if bits:
        sign = jnp.full((1,), 1 - 2 * (lax.axis_index("chan") // 2 ** bits[-1] % 2), jnp.int32)
        moving = [
            call(add_kernel, shape(*mixed.shape, bf16), "add", (sign, mixed, other), 1, cost=SMALL)
            for mixed, other in zip(moving, received)
        ]
    early, late, *far_early = moving
    passed_first = [swap_seq(value, 1) for value in far_first]
    all_first = [first, near_first]
    for far, passed in zip(far_first, passed_first):
        all_first += [far, passed]
    sending = [*far_early[:-1], jnp.concatenate([*far_early[-1:], late])]
    all_first, sending = lax.optimization_barrier((all_first, sending))
    passed_early = [swap_seq(value, 1) for value in sending]
    near_late = passed_early[-1][-late.shape[0] :]
    passed_early = [value[:cut] for value in passed_early][: len(far_early)]
    far_late = [swap_seq(late, 2 * k) for k in ahead]
    cross_late = [swap_seq(late, 2 * k + 1) for k in ahead]
    near_second = across(near_second, "chan")

    up = (power_two(channel_shift_power, 1) * (1.0 / math.sqrt(LOCAL_HEADS * P_SIZE)))[None, :]
    down = power_two(channel_shift_power, -1)[None, :]
    features = out_weight.shape[1]

    def project(pieces):
        return call(
            functools.partial(project_kernel, pairs),
            jax.ShapeDtypeStruct((sub_count, chan_count, pairs, 2, size, features), bf16),
            "project",
            (where, out_weight, *pieces, up, down),
            1,
            1,
            (
                pltpu.VMEM(out_weight.shape, bf16),
                pltpu.VMEM((pairs * tokens, width), bf16),
                pltpu.VMEM((pairs * tokens, features), f32),
                pltpu.SemaphoreType.DMA((5,)),
            ),
            WIDE_PARAMS,
        )

    go = lax.optimization_barrier(jnp.bool_(True))

    def stage(pieces):
        return lax.cond(
            go,
            lambda *pieces: halve(project(pieces), "sub"),
            lambda *_: jnp.zeros((chan_count, pairs, 2, size, features), bf16),
            *pieces,
        )

    done_first = stage(all_first)
    done_first, near_second, near_late, far_late, cross_late, passed_early = (
        lax.optimization_barrier(
            (done_first, near_second, near_late, far_late, cross_late, passed_early)
        )
    )
    all_second = [jnp.concatenate(parts) for parts in ([early, late], [near_second, near_late])]
    for parts in zip(far_early, far_late, passed_early, cross_late):
        all_second += [jnp.concatenate(parts[:2], axis=0), jnp.concatenate(parts[2:], axis=0)]
    done_first, done_second = lax.optimization_barrier(
        (halve(done_first, "chan"), stage(all_second))
    )
    done_second = halve(done_second, "chan")
    summed = jnp.stack([done_first, done_second], axis=2)
    returned = []
    for distance in range(seq_count):
        block = (member + distance) % 2
        value = lax.dynamic_index_in_dim(summed[distance // 2], block, 0, keepdims=False)
        value = value.reshape(2 * size, features)
        returned.append(swap_seq(value, distance) if distance else value)
    return call(
        place_kernel,
        shape(2 * size, seq_count * features, bf16),
        "place",
        (jnp.full((1,), here, jnp.int32), *returned),
        1,
    )


def body(x_in, b_in, c_in, step_size, *rest):
    tokens, heads = step_size.shape
    seq_count = lax.axis_size("seq")
    pieces = 2 * lax.axis_size("chan") * lax.axis_size("sub")
    if (
        heads % (2 * NORM_HEADS) == 0
        and seq_count % 2 == 0
        and seq_count & (seq_count - 1) == 0
        and tokens % (16 * pieces) == 0
    ):
        return paired_body(x_in, b_in, c_in, step_size, *rest)
    return plain_body(x_in, b_in, c_in, step_size, *rest)


def plain_body(
    x_in,
    b_in,
    c_in,
    step_size,
    log_decay,
    skip,
    gate_in,
    norm_gain,
    walsh_sign,
    channel_shift_power,
    out_weight,
):
    tokens, width = x_in.shape
    heads = step_size.shape[1]
    states = b_in.shape[2]
    seq_count = lax.axis_size("seq")
    sub_index = lax.axis_index("sub")
    group_local = sub_index * heads // (LOCAL_HEADS // G)
    b_group = lax.dynamic_slice_in_dim(b_in, group_local, 1, 1)[:, 0, :]
    c_group = lax.dynamic_slice_in_dim(c_in, group_local, 1, 1)[:, 0, :]
    expand = jnp.asarray(np.kron(np.eye(heads), np.ones((1, P_SIZE))), bf16)
    table = jnp.asarray(sylvester(H_BLOCK), bf16)

    tail = pl.cdiv(2 * heads, LANES) * LANES
    message, cumul = pl.pallas_call(
        message_kernel,
        out_shape=(
            jax.ShapeDtypeStruct((tokens, width + states + tail), bf16),
            jax.ShapeDtypeStruct((tokens, heads), f32),
        ),
        compiler_params=PARAMS,
        name="message",
    )(x_in, b_group, step_size, log_decay, expand)
    arrived = [shift_up(message, "seq", k) for k in range(1, seq_count)]

    wide_skip = jnp.repeat(skip, P_SIZE)[None, :]
    own, far = pl.pallas_call(
        local_kernel,
        out_shape=(
            jax.ShapeDtypeStruct((tokens, width), f32),
            jax.ShapeDtypeStruct((tokens, width), f32),
        ),
        compiler_params=PARAMS,
        name="local",
    )(x_in, b_group, c_group, step_size, cumul, gate_in, wide_skip, expand)

    signed_gain = (jnp.where(walsh_sign == 1, 1.0, -1.0) * norm_gain)[None, :]
    mixed = pl.pallas_call(
        functools.partial(mix_kernel, len(arrived)),
        out_shape=jax.ShapeDtypeStruct((tokens, width), bf16),
        compiler_params=PARAMS,
        name="mix",
    )(*arrived, c_group, own, far, signed_gain, table, expand)

    for axis in ("sub", "chan"):
        here = lax.axis_index(axis)
        for bit in bits_of(axis):
            other = swap(mixed.astype(bf16), axis, bit).astype(f32)
            sign = 1.0 - 2.0 * (here // 2**bit % 2).astype(f32)
            mixed = mixed.astype(f32) * sign + other
    rotated = mixed * (1.0 / math.sqrt(LOCAL_HEADS * P_SIZE))
    quant = jnp.clip(
        rotated * power_two(channel_shift_power, 1)[None, :], -clip_level, clip_level
    ).astype(bf16)
    scaled = (quant.astype(f32) * power_two(channel_shift_power, -1)[None, :]).astype(bf16)

    chan_count, sub_count = lax.axis_size("chan"), lax.axis_size("sub")
    rows = tokens // (chan_count * sub_count)
    order = sorted(range(1, seq_count), key=lambda k: -min(k, seq_count - k))
    blocks = {0: scaled}
    for k in order:
        blocks[k] = turn(scaled, "seq", k)
    sums = []
    for k in [0] + order:
        partial = dot(blocks[k], out_weight).astype(bf16)
        partial = partial.reshape(chan_count, sub_count, rows, -1)
        partial = halve(jnp.swapaxes(partial, 0, 1), "sub")
        done = halve(partial, "chan")
        sums.append((k, turn(done, "seq", -k % seq_count) if k else done))
    pieces = [value for _, value in sorted(sums, key=lambda item: item[0])]
    stacked = jnp.stack(pieces + pieces, axis=0)
    here = lax.axis_index("seq")
    placed = lax.dynamic_slice_in_dim(
        stacked, (seq_count - here) % seq_count, seq_count, 0
    )
    return jnp.swapaxes(placed, 0, 1).reshape(rows, -1)


def solution(mesh):
    return jax.shard_map(
        body,
        mesh=mesh,
        in_specs=(
            P(("groups", "seq"), ("chan", "sub")),
            P(("groups", "seq"), "chan", None),
            P(("groups", "seq"), "chan", None),
            P(("groups", "seq"), ("chan", "sub")),
            P(("groups", "seq"), ("chan", "sub")),
            P(("chan", "sub")),
            P(("groups", "seq"), ("chan", "sub")),
            P(("chan", "sub")),
            P(("chan", "sub")),
            P(("chan", "sub")),
            P(("chan", "sub"), "seq"),
        ),
        out_specs=P(("groups", "seq", "chan", "sub"), None),
        check_vma=False,
    )
```

```python
import functools
import math

import jax
import jax.numpy as jnp
import numpy as np
from jax import lax
from jax.experimental import pallas as pl
from jax.experimental.pallas import tpu as pltpu
from jax.sharding import PartitionSpec as P

LOCAL_HEADS = 128
P_SIZE = 64
G = 4
NORM_HEADS = 16


norm_eps = 1e-05
clip_level = 4.0
expo_levels = (-1, 0, 1, 2, 3)
LANES = 128
H_BLOCK = 256
COST = pl.CostEstimate(flops=1, transcendentals=0, bytes_accessed=30_000_000)
SMALL = pl.CostEstimate(flops=1, transcendentals=0, bytes_accessed=1)
f32 = jnp.float32
bf16 = jnp.bfloat16
PARAMS = pltpu.CompilerParams(vmem_limit_bytes=16 * 2**20)
WIDE_PARAMS = pltpu.CompilerParams(vmem_limit_bytes=16 * 2**20)


def power_two(expo, sign_flip):
    result = jnp.zeros(expo.shape, jnp.float32)
    for level in expo_levels:
        result = result + jnp.where(
            expo == level, jnp.float32(2.0 ** (sign_flip * level)), jnp.float32(0.0)
        )
    return result


def dot(a, b):
    return jnp.dot(a, b, preferred_element_type=f32)


def dot_nt(a, b):
    return lax.dot_general(a, b, (((1,), (1,)), ((), ())), preferred_element_type=f32)


def parts_of(value, count):
    terms = []
    for _ in range(count):
        term = value.astype(bf16)
        terms.append(term)
        value = value - term.astype(f32)
    return terms


def exact_dot(exact, value, count=3):
    return sum(dot(exact, term) for term in parts_of(value, count))


def spread(value, expand, count=2):
    return sum(dot(term, expand) for term in parts_of(value, count))


def causal_mask(size):
    row = lax.broadcasted_iota(jnp.int32, (size, size), 0)
    col = lax.broadcasted_iota(jnp.int32, (size, size), 1)
    return row >= col


def message_kernel(x_ref, b_ref, step_ref, decay_ref, expand_ref, msg_ref, cumul_ref):
    tokens, width = x_ref.shape
    heads = step_ref.shape[1]
    states = b_ref.shape[1]
    expand = expand_ref[...]
    triangle = causal_mask(tokens).astype(f32).astype(bf16)
    cumul = exact_dot(triangle, decay_ref[...])
    cumul_ref[...] = cumul
    total = cumul[tokens - 1 : tokens, :]
    scale = spread(jnp.exp(total - cumul) * step_ref[...], expand)
    msg_ref[:, :width] = (x_ref[...].astype(f32) * scale).astype(bf16)
    msg_ref[:, width : width + states] = b_ref[...]
    high, low = parts_of(jnp.exp(total), 2)
    base = width + states
    msg_ref[:, base:] = jnp.zeros((tokens, msg_ref.shape[1] - base), bf16)
    msg_ref[:, base : base + heads] = jnp.broadcast_to(high, (tokens, heads))
    msg_ref[:, base + heads : base + 2 * heads] = jnp.broadcast_to(low, (tokens, heads))


def local_kernel(
    x_ref, b_ref, c_ref, step_ref, cumul_ref, gate_ref, skip_ref, expand_ref, own_ref, far_ref
):
    tokens, width = x_ref.shape
    heads = step_ref.shape[1]
    causal = causal_mask(tokens)
    inner = dot_nt(c_ref[...], b_ref[...])
    cumul = cumul_ref[...]
    cumul_t = cumul.T
    step_t = step_ref[...].T
    first = lax.broadcasted_iota(jnp.int32, (tokens, 2 * P_SIZE), 1) < P_SIZE
    for pair in range(heads // 2):
        mixings = []
        for head in (2 * pair, 2 * pair + 1):
            differ = cumul[:, head : head + 1] - cumul_t[head : head + 1, :]
            ratio = jnp.exp(jnp.where(causal, differ, -jnp.inf))
            mixings.append((ratio * (inner * step_t[head : head + 1, :])).astype(bf16))
        at = slice(pair * 2 * P_SIZE, (pair + 1) * 2 * P_SIZE)
        x_pair = x_ref[:, at]
        zero = jnp.zeros_like(x_pair)
        blocks = jnp.concatenate(
            [jnp.where(first, x_pair, zero), jnp.where(first, zero, x_pair)], axis=0
        )
        own = dot(jnp.concatenate(mixings, axis=1), blocks)
        own = own + x_pair.astype(f32) * skip_ref[:, at]
        gate = gate_ref[:, at].astype(f32)
        own_ref[:, at] = own * (gate / (1.0 + jnp.exp(-gate)))
    reach = jnp.exp(cumul)
    tile = min(width, 512)
    for start in range(0, width, tile):
        at = slice(start, start + tile)
        gate = gate_ref[:, at].astype(f32)
        far_ref[:, at] = spread(reach, expand_ref[:, at]) * (gate / (1.0 + jnp.exp(-gate)))


def mix_kernel(count, *refs):
    messages = refs[:count]
    c_ref, own_ref, far_ref, gain_ref, table_ref, expand_ref, out_ref = refs[count:]
    tokens, width = own_ref.shape
    states = c_ref.shape[1]
    heads = expand_ref.shape[0]
    base = width + states
    c_group = c_ref[...]
    inners = []
    decays = []
    for msg_ref in messages:
        inners.append(dot_nt(c_group, msg_ref[:, width:base]).astype(bf16))
        decay = dot(msg_ref[:16, base : base + heads], expand_ref[...]) + dot(
            msg_ref[:16, base + heads : base + 2 * heads], expand_ref[...]
        )
        decays.append(decay[:1, :])
    norm_width = NORM_HEADS * P_SIZE
    table = table_ref[...]
    parts = []
    for start in range(0, width, norm_width):
        pres = []
        square = jnp.zeros((tokens, 1), f32)
        for begin in range(start, start + norm_width, H_BLOCK):
            at = slice(begin, begin + H_BLOCK)
            carried = None
            for k in reversed(range(count)):
                term = dot(inners[k], messages[k][:, at])
                carried = term if carried is None else term + decays[k][:, at] * carried
            pre = own_ref[:, at]
            if carried is not None:
                pre = pre + far_ref[:, at] * carried
            square = square + jnp.sum(pre * pre, axis=1, keepdims=True)
            pres.append(pre)
        inverse = lax.rsqrt(square * (1.0 / norm_width) + norm_eps)
        for index, pre in enumerate(pres):
            at = slice(start + index * H_BLOCK, start + (index + 1) * H_BLOCK)
            signed = (pre * inverse * gain_ref[:, at]).astype(bf16)
            parts.append(dot(signed, table))
    butterflies(parts)
    for index, part in enumerate(parts):
        out_ref[:, index * H_BLOCK : (index + 1) * H_BLOCK] = part.astype(bf16)


def half_at(which, size):
    return pl.ds(pl.multiple_of(which * size, size), size)


def start_all(copies):
    for copy in copies:
        copy.start()
    return copies


def wait_all(copies):
    for copy in copies:
        copy.wait()


def block_rows(index, size):
    return slice(index * size, (index + 1) * size)


def pack_kernel(
    where_ref,
    x_mine_ref,
    x_other_ref,
    b_ref,
    c_ref,
    steps_ref,
    mine_ref,
    other_ref,
    straight_ref,
    cross_ref,
):
    tokens, states = b_ref.shape
    half = x_mine_ref.shape[1]
    heads = steps_ref.shape[0] // 4
    member = where_ref[0]
    triangle = causal_mask(tokens).astype(f32).astype(bf16)
    step = steps_ref[: 2 * heads, :].T
    decay = steps_ref[2 * heads :, :].T
    cumul = exact_dot(triangle, decay)
    total = cumul[tokens - 1 : tokens, :]
    scale = jnp.exp(total - cumul) * step
    kept = jnp.exp(total)

    def pick(value, which):
        return jnp.where(which == 0, value[:, :heads], value[:, heads:])

    other_ref[:, :half] = x_other_ref[...]
    for out_ref, base, which in ((mine_ref, 0, member), (other_ref, half, 1 - member)):
        out_ref[:, base : base + states] = b_ref[...]
        out_ref[:, base + states : base + 2 * states] = c_ref[...]
        base += 2 * states
        out_ref[:, base:] = jnp.zeros((tokens, out_ref.shape[1] - base), bf16)
        terms = parts_of(pick(step, which), 3) + parts_of(pick(decay, which), 3)
        for index, term in enumerate(terms):
            out_ref[:, base + index * heads : base + (index + 1) * heads] = term
    expand = expansion(heads)
    for out_ref, x_ref, which in (
        (straight_ref, x_mine_ref, member),
        (cross_ref, x_other_ref, 1 - member),
    ):
        wide = spread(pick(scale, which), expand)
        weighted = (x_ref[...].astype(f32) * wide).astype(bf16)
        for index in range(half // LANES):
            out_ref[block_rows(index, tokens), :] = weighted[:, block_rows(index, LANES)]
        for index in range(states // LANES):
            out_ref[block_rows(half // LANES + index, tokens), :] = b_ref[
                :, block_rows(index, LANES)
            ]
        base = (half + states) // LANES * tokens
        rows = out_ref.shape[0] - base
        out_ref[base:, :] = jnp.zeros((rows, LANES), bf16)
        for index, term in enumerate(parts_of(pick(kept, which), 2)):
            out_ref[base:, block_rows(index, heads)] = jnp.broadcast_to(term, (rows, heads))


def expansion(heads):
    shape = (heads, heads * P_SIZE)
    row = lax.broadcasted_iota(jnp.int32, shape, 0)
    col = lax.broadcasted_iota(jnp.int32, shape, 1)
    return ((col >= row * P_SIZE) & (col < (row + 1) * P_SIZE)).astype(f32).astype(bf16)


def pair_kernel(
    where_ref,
    x_ref,
    meta_ref,
    msg_ref,
    skip_ref,
    own_ref,
    far_ref,
    c_pair_ref,
    x_both,
    b_both,
    step_both,
    decay_both,
):
    tokens, half = x_ref.shape
    states = c_pair_ref.shape[1]
    heads = half // P_SIZE
    member = where_ref[0]
    for which, x, meta in (
        (member, x_ref, meta_ref),
        (1 - member, msg_ref.at[:, :half], msg_ref.at[:, half:]),
    ):
        rows = half_at(which, tokens)
        x_both[rows, :] = x[...]
        b_both[rows, :] = meta[:, :states]
        c_pair_ref[rows, :] = meta[:, states : 2 * states]
        for index, both in enumerate((step_both, decay_both)):
            base = 2 * states + 3 * index * heads
            terms = [
                meta[:, base + term * heads : base + (term + 1) * heads].astype(f32)
                for term in range(3)
            ]
            both[rows, :] = (terms[2] + terms[1]) + terms[0]

    span = 2 * tokens
    causal = causal_mask(span)
    inner = jnp.where(causal, dot_nt(c_pair_ref[...], b_both[...]), 0.0)
    cumul = exact_dot(causal.astype(f32).astype(bf16), decay_both[...])
    cumul_t = cumul.T
    step_t = step_both[...].T
    skip = skip_ref[:, half_at(member, half)]
    expand = expansion(heads)
    reach = parts_of(jnp.exp(cumul), 2)
    first = lax.broadcasted_iota(jnp.int32, (tokens, 2 * P_SIZE), 1) < P_SIZE
    for pair in range(heads // 2):
        at = slice(pair * 2 * P_SIZE, (pair + 1) * 2 * P_SIZE)
        spans = []
        for block in range(2):
            x_block = x_both[block * tokens : (block + 1) * tokens, at]
            zero = jnp.zeros_like(x_block)
            spans.append((jnp.where(first, x_block, zero), jnp.where(first, zero, x_block)))
        for block in range(2):
            rows = slice(block * tokens, (block + 1) * tokens)
            mixings, values = [], []
            for place, head in enumerate((2 * pair, 2 * pair + 1)):
                for earlier in range(block + 1):
                    cols = slice(earlier * tokens, (earlier + 1) * tokens)
                    differ = cumul[rows, head : head + 1] - cumul_t[head : head + 1, cols]
                    if earlier == block:
                        differ = jnp.where(causal[:tokens, :tokens], differ, 0.0)
                    ratio = jnp.exp(differ)
                    mixings.append(
                        (ratio * (inner[rows, cols] * step_t[head : head + 1, cols])).astype(bf16)
                    )
                    values.append(spans[earlier][place])
            own = dot(jnp.concatenate(mixings, axis=1), jnp.concatenate(values, axis=0))
            own_ref[rows, at] = own + x_both[rows, at].astype(f32) * skip[:, at]
            far_ref[rows, at] = sum(dot(term[rows, :], expand[:, at]) for term in reach)


def gate_mix_kernel(count, pieces, *refs):
    sent = refs[: 2 * count]
    where_ref, gate_ref, gate_pair_ref, c_ref, own_ref, far_ref, gain_ref, table_ref = refs[
        2 * count : -3
    ]
    out_refs, gate_both = refs[-3:-1], refs[-1]
    span, half = own_ref.shape
    tokens = span // 2
    states = c_ref.shape[1]
    heads = half // P_SIZE
    member = where_ref[0]
    c_pair = c_ref[...]
    expand = expansion(heads)

    for which, gate in ((member, gate_ref), (1 - member, gate_pair_ref)):
        gate_both[half_at(which, tokens), :] = gate[...]

    def columns(ref, start, size):
        blocks = range(start // LANES, (start + size) // LANES)
        return jnp.concatenate([ref[block_rows(index, tokens), :] for index in blocks], axis=1)

    def kept(ref):
        base = (half + states) // LANES * tokens
        high, low = (ref[base:, block_rows(index, heads)] for index in range(2))
        return (dot(high, expand) + dot(low, expand))[:1, :]

    inners = [dot_nt(c_pair, columns(ref, half, states)).astype(bf16) for ref in sent]
    factors, pair_kept = [], []
    for k in range(count):
        one, two = kept(sent[2 * k]), kept(sent[2 * k + 1])
        pair_kept.append(one * two)
        factors += [jnp.where(member == 0, two, 1.0), jnp.where(member == 0, 1.0, one)]
    gain = gain_ref[:, half_at(member, half)]
    table = table_ref[...]
    parts = []
    norm_width = NORM_HEADS * P_SIZE
    for start in range(0, half, norm_width):
        pres = []
        square = jnp.zeros((span, 1), f32)
        for begin in range(start, start + norm_width, H_BLOCK):
            at = slice(begin, begin + H_BLOCK)
            pre = own_ref[:, at]
            carried = None
            for k in reversed(range(count)):
                term = 0.0
                for j in (2 * k, 2 * k + 1):
                    term = term + factors[j][:, at] * dot(
                        inners[j], columns(sent[j], begin, H_BLOCK)
                    )
                carried = term if carried is None else term + pair_kept[k][:, at] * carried
            if carried is not None:
                pre = pre + far_ref[:, at] * carried
            gate = gate_both[:, at].astype(f32)
            pre = pre * (gate / (1.0 + jnp.exp(-gate)))
            square = square + jnp.sum(pre * pre, axis=1, keepdims=True)
            pres.append(pre)
        inverse = lax.rsqrt(square * (1.0 / norm_width) + norm_eps)
        for index, pre in enumerate(pres):
            at = slice(start + index * H_BLOCK, start + (index + 1) * H_BLOCK)
            parts.append(dot((pre * inverse * gain[:, at]).astype(bf16), table))
    butterflies(parts)
    size = span // pieces
    for index, part in enumerate(parts):
        at = slice(index * H_BLOCK, (index + 1) * H_BLOCK)
        part = part.astype(bf16)
        for piece in range(pieces):
            to = slice(piece // 2 * size, (piece // 2 + 1) * size)
            out_refs[piece % 2][to, at] = part[piece * size : (piece + 1) * size, :]


def butterflies(parts):
    span = 1
    while span < len(parts):
        for low in range(len(parts)):
            if low & span == 0:
                a, b = parts[low], parts[low + span]
                parts[low], parts[low + span] = a + b, a - b
        span *= 2


def add_kernel(sign_ref, mixed_ref, received_ref, out_ref):
    sign = sign_ref[0].astype(f32)
    out_ref[...] = (mixed_ref[...].astype(f32) * sign + received_ref[...].astype(f32)).astype(bf16)


def project_kernel(pairs, where_ref, weight_ref, *refs):
    pieces = refs[: 2 * pairs]
    up_ref, down_ref, out_ref, weight_own, scaled, sums, sems = refs[2 * pairs :]
    rows, half = pieces[0].shape
    sign = (1 - 2 * where_ref[0]).astype(f32)
    sub_count, chan_count, _, blocks, size, features = out_ref.shape
    bounds = [half * eighth // 4 for eighth in (0, 2, 4, 6, 7, 8)]
    spans = [slice(*ends) for ends in zip(bounds, bounds[1:])]
    copies = start_all(
        [
            pltpu.make_async_copy(weight_ref.at[at, :], weight_own.at[at, :], sems.at[index])
            for index, at in enumerate(spans)
        ]
    )
    for start in range(0, half, H_BLOCK):
        inner = slice(start, start + H_BLOCK)
        for pair in range(pairs):
            one = pieces[2 * pair][:, inner].astype(f32)
            two = pieces[2 * pair + 1][:, inner].astype(f32)
            for side, mixed in enumerate((one + two, (one - two) * sign)):
                at = slice(side * half + start, side * half + start + H_BLOCK)
                quant = jnp.clip(mixed * up_ref[:, at], -clip_level, clip_level).astype(bf16)
                scaled[pair * rows : (pair + 1) * rows, at] = (
                    quant.astype(f32) * down_ref[:, at]
                ).astype(bf16)
    for index, (copy, at) in enumerate(zip(copies, spans)):
        copy.wait()
        term = dot(scaled[:, at], weight_own[at, :])
        if index == 0:
            sums[...] = term
        elif index < len(spans) - 1:
            sums[...] += term
        else:
            total = (sums[...] + term).astype(bf16)
    row = 0
    for pair in range(pairs):
        for block in range(blocks):
            for chan in range(chan_count):
                for sub in range(sub_count):
                    out_ref[sub, chan, pair, block] = total[row : row + size, :]
                    row += size


def place_kernel(where_ref, *refs):
    out_ref = refs[-1]
    features = refs[0].shape[1]
    for distance, ref in enumerate(refs[:-1]):
        out_ref[:, half_at(where_ref[0] ^ distance, features)] = ref[...]


def sylvester(order):
    table = np.ones((1, 1), np.float32)
    while table.shape[0] < order:
        table = np.block([[table, table], [table, -table]])
    return table


def shift_up(value, axis, distance):
    count = lax.axis_size(axis)
    return lax.ppermute(value, axis, [(k, k + distance) for k in range(count - distance)])


def turn(value, axis, distance):
    count = lax.axis_size(axis)
    return lax.ppermute(value, axis, [(k, (k + distance) % count) for k in range(count)])


def swap(value, axis, bit):
    count = lax.axis_size(axis)
    return lax.ppermute(value, axis, [(k, k ^ (1 << bit)) for k in range(count)])


def bits_of(axis):
    return range(lax.axis_size(axis).bit_length() - 1)


def halve(value, axis):
    here = lax.axis_index(axis)
    for bit in reversed(bits_of(axis)):
        pair = value.reshape((2, value.shape[0] // 2) + value.shape[1:])
        mine = here // 2**bit % 2
        keep = lax.dynamic_index_in_dim(pair, mine, 0, keepdims=False)
        give = lax.dynamic_index_in_dim(pair, 1 - mine, 0, keepdims=False)
        value = (keep.astype(f32) + swap(give, axis, bit).astype(f32)).astype(bf16)
    return value[0]


def call(kernel, out_shape, name, args, scalars=0, anywhere=0, scratch=(), params=PARAMS, cost=COST):
    specs = [pl.BlockSpec(memory_space=pltpu.SMEM)] * scalars
    specs += [pl.BlockSpec(memory_space=pltpu.HBM)] * anywhere
    specs += [pl.BlockSpec(memory_space=pltpu.VMEM)] * (len(args) - scalars - anywhere)
    return pl.pallas_call(
        kernel,
        out_shape=out_shape,
        in_specs=specs,
        scratch_shapes=scratch,
        compiler_params=params,
        cost_estimate=cost,
        name=name,
    )(*args)


def swap_seq(value, distance):
    count = lax.axis_size("seq")
    return lax.ppermute(value, "seq", [(k, k ^ distance) for k in range(count)])


def paired_body(
    x_in,
    b_in,
    c_in,
    step_size,
    log_decay,
    skip,
    gate_in,
    norm_gain,
    walsh_sign,
    channel_shift_power,
    out_weight,
):
    tokens, width = x_in.shape
    heads = step_size.shape[1]
    states = b_in.shape[2]
    half, half_heads = width // 2, heads // 2
    seq_count, chan_count, sub_count = (lax.axis_size(a) for a in ("seq", "chan", "sub"))
    pairs = seq_count // 2
    here = lax.axis_index("seq")
    member = here % 2
    group_local = lax.axis_index("sub") * heads // (LOCAL_HEADS // G)
    where = jnp.full((1,), member, jnp.int32)
    b_group = lax.dynamic_index_in_dim(b_in, group_local, 1, keepdims=False)
    c_group = lax.dynamic_index_in_dim(c_in, group_local, 1, keepdims=False)
    table = jnp.asarray(sylvester(H_BLOCK), bf16)

    def shape(rows, columns, kind):
        return jax.ShapeDtypeStruct((rows, columns), kind)

    def padded(columns):
        return pl.cdiv(columns, LANES) * LANES

    def half_of(value, which):
        return lax.dynamic_slice_in_dim(value, which * half, half, 1)

    x_mine, x_other = half_of(x_in, member), half_of(x_in, 1 - member)
    gate_mine, gate_other = half_of(gate_in, member), half_of(gate_in, 1 - member)
    steps = jnp.concatenate([step_size.T, log_decay.T], axis=0)
    with_pair = shape(tokens, 2 * states + padded(6 * half_heads), bf16)
    with_later = shape((half + states) // LANES * tokens + 16, LANES, bf16)
    meta_mine, to_pair, straight, cross = call(
        pack_kernel,
        (with_pair, shape(tokens, half + with_pair.shape[1], bf16), with_later, with_later),
        "pack",
        (where, x_mine, x_other, b_group, c_group, steps),
        1,
    )
    sent = []
    for ahead in range(1, pairs):
        firsts = range(seq_count - 2 * ahead)
        sent.append(lax.ppermute(straight, "seq", [(k, k + 2 * ahead) for k in firsts]))
        sent.append(lax.ppermute(cross, "seq", [(k, (k ^ 1) + 2 * ahead) for k in firsts]))
    from_pair, gate_pair = swap_seq(to_pair, 1), swap_seq(gate_other, 1)

    span = 2 * tokens
    own, far, c_pair = call(
        pair_kernel,
        (
            shape(span, half, f32),
            shape(span, half, f32),
            shape(span, states, bf16),
        ),
        "pair",
        (
            where,
            x_mine,
            meta_mine,
            from_pair,
            jnp.repeat(skip, P_SIZE)[None, :],
        ),
        1,
        0,
        (
            pltpu.VMEM((span, half), bf16),
            pltpu.VMEM((span, states), bf16),
            pltpu.VMEM((span, half_heads), f32),
            pltpu.VMEM((span, half_heads), f32),
        ),
        cost=SMALL,
    )
    signed_gain = (jnp.where(walsh_sign == 1, 1.0, -1.0) * norm_gain)[None, :]
    owners = chan_count * sub_count
    size = tokens // (2 * owners)
    count = len(sent) // 2
    chunks = pl.pallas_call(
        functools.partial(gate_mix_kernel, count, span // size),
        out_shape=(shape(tokens, half, bf16),) * 2,
        in_specs=[pl.BlockSpec(memory_space=pltpu.VMEM)] * (2 * count)
        + [pl.BlockSpec(memory_space=pltpu.SMEM)]
        + [pl.BlockSpec(memory_space=pltpu.VMEM)] * 7,
        scratch_shapes=[pltpu.VMEM((span, half), bf16)],
        compiler_params=PARAMS,
        cost_estimate=COST,
        name="mix",
    )(*sent, where, gate_mine, gate_pair, c_pair, own, far, signed_gain, table)

    def add_across(mixed, axis, bit, received):
        place = lax.axis_index(axis)
        sign = 1.0 - 2.0 * (place // 2**bit % 2).astype(f32)
        return (mixed.astype(f32) * sign + received.astype(f32)).astype(bf16)

    def across(mixed, axis):
        for bit in bits_of(axis):
            mixed = add_across(mixed, axis, bit, swap(mixed, axis, bit))
        return mixed

    first, second = (across(chunk, "sub") for chunk in chunks)
    ahead = range(1, pairs)
    cut = tokens * 3 // 4
    near_second = swap_seq(second, 1)
    far_early = [swap_seq(second[:cut], 2 * k) for k in ahead]
    bits = bits_of("chan")
    halves = [first[: tokens // 2], first[tokens // 2 :]]
    for bit in bits[:-1]:
        halves = [add_across(value, "chan", bit, swap(value, "chan", bit)) for value in halves]
    received = [swap(value, "chan", bits[-1]) for value in halves if bits]
    halves, received, second, near_second, far_early = lax.optimization_barrier(
        (halves, received, second, near_second, far_early)
    )
    if bits:
        halves = [add_across(*pair[:1], "chan", bits[-1], pair[1]) for pair in zip(halves, received)]
    first = jnp.concatenate(halves, axis=0)
    moving = [second[:cut], second[cut:], *far_early]
    for bit in bits[:-1]:
        moving = [add_across(value, "chan", bit, swap(value, "chan", bit)) for value in moving]
    received = [swap(value, "chan", bits[-1]) for value in moving if bits]
    far_first = [swap_seq(first, 2 * k) for k in ahead]
    near_first = swap_seq(first, 1)
    first, near_second, moving, received, far_first, near_first = lax.optimization_barrier(
        (first, near_second, moving, received, far_first, near_first)
    )
    if bits:
        sign = jnp.full((1,), 1 - 2 * (lax.axis_index("chan") // 2 ** bits[-1] % 2), jnp.int32)
        moving = [
            call(add_kernel, shape(*mixed.shape, bf16), "add", (sign, mixed, other), 1, cost=SMALL)
            for mixed, other in zip(moving, received)
        ]
    early, late, *far_early = moving
    passed_first = [swap_seq(value, 1) for value in far_first]
    all_first = [first, near_first]
    for far, passed in zip(far_first, passed_first):
        all_first += [far, passed]
    all_first, far_early = lax.optimization_barrier((all_first, far_early))
    passed_early = [swap_seq(value, 1) for value in far_early]
    far_late = [swap_seq(late, 2 * k) for k in ahead]
    cross_late = [swap_seq(late, 2 * k + 1) for k in ahead]
    near_second = across(near_second, "chan")

    up = (power_two(channel_shift_power, 1) * (1.0 / math.sqrt(LOCAL_HEADS * P_SIZE)))[None, :]
    down = power_two(channel_shift_power, -1)[None, :]
    features = out_weight.shape[1]

    def project(pieces):
        return call(
            functools.partial(project_kernel, pairs),
            jax.ShapeDtypeStruct((sub_count, chan_count, pairs, 2, size, features), bf16),
            "project",
            (where, out_weight, *pieces, up, down),
            1,
            1,
            (
                pltpu.VMEM(out_weight.shape, bf16),
                pltpu.VMEM((pairs * tokens, width), bf16),
                pltpu.VMEM((pairs * tokens, features), f32),
                pltpu.SemaphoreType.DMA((5,)),
            ),
            WIDE_PARAMS,
        )

    go = lax.optimization_barrier(jnp.bool_(True))

    def stage(pieces):
        return lax.cond(
            go,
            lambda *pieces: halve(project(pieces), "sub"),
            lambda *_: jnp.zeros((chan_count, pairs, 2, size, features), bf16),
            *pieces,
        )

    done_first = stage(all_first)
    done_first, near_second, far_late, cross_late, passed_early = lax.optimization_barrier(
        (done_first, near_second, far_late, cross_late, passed_early)
    )
    all_second = [jnp.concatenate([early, late], axis=0), near_second]
    for parts in zip(far_early, far_late, passed_early, cross_late):
        all_second += [jnp.concatenate(parts[:2], axis=0), jnp.concatenate(parts[2:], axis=0)]
    done_first, done_second = lax.optimization_barrier(
        (halve(done_first, "chan"), stage(all_second))
    )
    done_second = halve(done_second, "chan")
    summed = jnp.stack([done_first, done_second], axis=2)
    returned = []
    for distance in range(seq_count):
        block = (member + distance) % 2
        value = lax.dynamic_index_in_dim(summed[distance // 2], block, 0, keepdims=False)
        value = value.reshape(2 * size, features)
        returned.append(swap_seq(value, distance) if distance else value)
    return call(
        place_kernel,
        shape(2 * size, seq_count * features, bf16),
        "place",
        (jnp.full((1,), here, jnp.int32), *returned),
        1,
    )


def body(x_in, b_in, c_in, step_size, *rest):
    tokens, heads = step_size.shape
    seq_count = lax.axis_size("seq")
    pieces = 2 * lax.axis_size("chan") * lax.axis_size("sub")
    if (
        heads % (2 * NORM_HEADS) == 0
        and seq_count % 2 == 0
        and seq_count & (seq_count - 1) == 0
        and tokens % (16 * pieces) == 0
    ):
        return paired_body(x_in, b_in, c_in, step_size, *rest)
    return plain_body(x_in, b_in, c_in, step_size, *rest)


def plain_body(
    x_in,
    b_in,
    c_in,
    step_size,
    log_decay,
    skip,
    gate_in,
    norm_gain,
    walsh_sign,
    channel_shift_power,
    out_weight,
):
    tokens, width = x_in.shape
    heads = step_size.shape[1]
    states = b_in.shape[2]
    seq_count = lax.axis_size("seq")
    sub_index = lax.axis_index("sub")
    group_local = sub_index * heads // (LOCAL_HEADS // G)
    b_group = lax.dynamic_slice_in_dim(b_in, group_local, 1, 1)[:, 0, :]
    c_group = lax.dynamic_slice_in_dim(c_in, group_local, 1, 1)[:, 0, :]
    expand = jnp.asarray(np.kron(np.eye(heads), np.ones((1, P_SIZE))), bf16)
    table = jnp.asarray(sylvester(H_BLOCK), bf16)

    tail = pl.cdiv(2 * heads, LANES) * LANES
    message, cumul = pl.pallas_call(
        message_kernel,
        out_shape=(
            jax.ShapeDtypeStruct((tokens, width + states + tail), bf16),
            jax.ShapeDtypeStruct((tokens, heads), f32),
        ),
        compiler_params=PARAMS,
        name="message",
    )(x_in, b_group, step_size, log_decay, expand)
    arrived = [shift_up(message, "seq", k) for k in range(1, seq_count)]

    wide_skip = jnp.repeat(skip, P_SIZE)[None, :]
    own, far = pl.pallas_call(
        local_kernel,
        out_shape=(
            jax.ShapeDtypeStruct((tokens, width), f32),
            jax.ShapeDtypeStruct((tokens, width), f32),
        ),
        compiler_params=PARAMS,
        name="local",
    )(x_in, b_group, c_group, step_size, cumul, gate_in, wide_skip, expand)

    signed_gain = (jnp.where(walsh_sign == 1, 1.0, -1.0) * norm_gain)[None, :]
    mixed = pl.pallas_call(
        functools.partial(mix_kernel, len(arrived)),
        out_shape=jax.ShapeDtypeStruct((tokens, width), bf16),
        compiler_params=PARAMS,
        name="mix",
    )(*arrived, c_group, own, far, signed_gain, table, expand)

    for axis in ("sub", "chan"):
        here = lax.axis_index(axis)
        for bit in bits_of(axis):
            other = swap(mixed.astype(bf16), axis, bit).astype(f32)
            sign = 1.0 - 2.0 * (here // 2**bit % 2).astype(f32)
            mixed = mixed.astype(f32) * sign + other
    rotated = mixed * (1.0 / math.sqrt(LOCAL_HEADS * P_SIZE))
    quant = jnp.clip(
        rotated * power_two(channel_shift_power, 1)[None, :], -clip_level, clip_level
    ).astype(bf16)
    scaled = (quant.astype(f32) * power_two(channel_shift_power, -1)[None, :]).astype(bf16)

    chan_count, sub_count = lax.axis_size("chan"), lax.axis_size("sub")
    rows = tokens // (chan_count * sub_count)
    order = sorted(range(1, seq_count), key=lambda k: -min(k, seq_count - k))
    blocks = {0: scaled}
    for k in order:
        blocks[k] = turn(scaled, "seq", k)
    sums = []
    for k in [0] + order:
        partial = dot(blocks[k], out_weight).astype(bf16)
        partial = partial.reshape(chan_count, sub_count, rows, -1)
        partial = halve(jnp.swapaxes(partial, 0, 1), "sub")
        done = halve(partial, "chan")
        sums.append((k, turn(done, "seq", -k % seq_count) if k else done))
    pieces = [value for _, value in sorted(sums, key=lambda item: item[0])]
    stacked = jnp.stack(pieces + pieces, axis=0)
    here = lax.axis_index("seq")
    placed = lax.dynamic_slice_in_dim(
        stacked, (seq_count - here) % seq_count, seq_count, 0
    )
    return jnp.swapaxes(placed, 0, 1).reshape(rows, -1)


def solution(mesh):
    return jax.shard_map(
        body,
        mesh=mesh,
        in_specs=(
            P(("groups", "seq"), ("chan", "sub")),
            P(("groups", "seq"), "chan", None),
            P(("groups", "seq"), "chan", None),
            P(("groups", "seq"), ("chan", "sub")),
            P(("groups", "seq"), ("chan", "sub")),
            P(("chan", "sub")),
            P(("groups", "seq"), ("chan", "sub")),
            P(("chan", "sub")),
            P(("chan", "sub")),
            P(("chan", "sub")),
            P(("chan", "sub"), "seq"),
        ),
        out_specs=P(("groups", "seq", "chan", "sub"), None),
        check_vma=False,
    )
```
